32 devices in a mesh: group: 2 (over y), expert: 2 (over core), tile: 8 (over z, x).
Axes of the slice: x: 2, y: 2, z: 4, core: 2. Of those that a mesh axis runs over, the one named last changes fastest.
Arguments:
- tokens: bfloat16 [64, 6144], P(('group', 'tile'), 'expert'), parts along dimension 0, may hold values from -6 to 6
- routes: int32 [64, 2], P(('group', 'tile')), parts along dimension 0, may hold values from 0 to 7, as said below
- gates: float32 [64, 2], P(('group', 'tile')), parts along dimension 0, may hold values from 0.2 to 1
- w_gate: bfloat16 [2, 6144, 16384], P('expert', None, 'tile'), may hold values from -0.078125 to 0.078125
- w_up: bfloat16 [2, 6144, 16384], P('expert', None, 'tile'), may hold values from -0.078125 to 0.078125
- w_down: bfloat16 [2, 6144, 16384], P('expert', 'tile'), may hold values from -0.046875 to 0.046875
Outputs:
- mixed_out: bfloat16 [64, 6144], P(('group', 'tile'), 'expert'), parts along dimension 0
The draws below stay inside these ranges and needn't reach their ends.
There are 2 independent parts, one for each index of `group`. The reference program is written for one: setup_inputs(seed, part) draws one part's arguments, and reference() takes and returns one part's arrays. A program takes and returns all parts, laid end to end along the dimension named above; an argument that names none is the same for every part. Nothing has to cross between parts.
Inputs may be any that keep to these rules, and one draw needn't show every extreme that they name: `routes`: each row names two different experts. Over the 4 rows of one index of tile, each expert below 2 is named by at most 2 rows, and in every draw some expert below 2 is named by exactly 2 rows of every such block.
All inputs are finite; a program needn't handle non-finite values.
Results may differ from the reference program's by a relative error of at most 0.0095.
Values may be sent and summed in bfloat16 or wider, within the bound.
No kernel may reach another device: no remote copies, remote signals or barrier semaphores. Data moves between devices by JAX's collectives and lax.ppermute only.
A program may use at most 192 MiB of HBM per device.

```python
import jax
import jax.numpy as jnp
from jax import lax

D = 6144
FF = 16384
ALL_EXPERTS = 8
TOK_DEV = 4
CAP = 2
EXPERTS = 2
TOKENS = 32
N_TILE = 8


def draw_routes(key, part):
    key = jax.random.fold_in(key, 7)
    subkeys = jax.random.split(key, 4)
    blocks = TOKENS // TOK_DEV
    full_expert = jax.random.randint(subkeys[0], (), 0, EXPERTS)
    window = jnp.arange(EXPERTS, dtype=jnp.int32)
    counts = jax.random.randint(subkeys[1], (blocks, EXPERTS), 0, CAP + 1)
    counts = jnp.where(window[None, :] == full_expert, CAP, counts)
    rows_in = jnp.arange(TOK_DEV, dtype=jnp.int32)
    order_score = jax.random.randint(subkeys[2], (blocks, EXPERTS, TOK_DEV), 0, 1000) * TOK_DEV + rows_in[None, None, :]
    ranking = jnp.sum((order_score[:, :, None, :] < order_score[:, :, :, None]).astype(jnp.int32), axis=3)
    assigned = ranking < counts[:, :, None]
    assigned = jnp.transpose(assigned, (0, 2, 1))
    inside = jnp.where(assigned, 1000000 + window[None, None, :], -1 - window[None, None, :])
    outside_ids = jnp.arange(EXPERTS, ALL_EXPERTS, dtype=jnp.int32)
    random_part = jax.random.randint(subkeys[3], (blocks, TOK_DEV, ALL_EXPERTS - EXPERTS), 0, 1000)
    outer_score = random_part * ALL_EXPERTS + outside_ids[None, None, :]
    scores = jnp.concatenate([inside, outer_score], axis=2).reshape(TOKENS, ALL_EXPERTS)
    ranked = lax.top_k(scores, 2)[1]
    return ranked.astype(jnp.int32)


def level_of(rng, dims, cuts, low, top_value):
    loudness, own = 1.0, jax.random.fold_in(rng, 6)
    for dim, parts in cuts:
        draws = jnp.exp(jax.random.uniform(jax.random.fold_in(own, dim), (parts,), jnp.float32, low / len(cuts), top_value / len(cuts)))
        loudness = loudness * jnp.repeat(draws, dims[dim] // parts).reshape([-1 if axis == dim else 1 for axis in range(len(dims))])
    return loudness


def gaussian(key, extent, deviation, reach, cuts=(), kind=jnp.bfloat16):
    loudness = level_of(key, extent, cuts, -0.22, 0.18) if cuts else 1.0
    entries = jax.random.normal(key, extent, jnp.float32) * deviation * loudness
    return jnp.minimum(jnp.maximum(entries, -reach), reach).astype(kind)


def setup_inputs(seed: int = 0, part: int = 0) -> dict:
    streams_of = jax.random.split(jax.random.key(seed), 7)
    own_keys = jax.random.split(jax.random.fold_in(streams_of[6], part), 7)
    tokens = gaussian(own_keys[0], (TOKENS, D), 1.0, 6.0, ((0, 8), (1, 2)))
    routes = draw_routes(jax.random.fold_in(jax.random.fold_in(streams_of[6], part), 71), part)
    gates = jnp.clip(0.2 + 0.8 * jax.random.uniform(own_keys[2], (TOKENS, 2), jnp.float32) ** level_of(own_keys[2], (TOKENS, 2), ((0, 8),), -0.2, 0.2), 0.2, 1.0)
    w_gate = gaussian(streams_of[3], (EXPERTS, D, FF), D ** -0.5, 0.078125, ((0, 2), (2, 8)))
    w_up = gaussian(streams_of[4], (EXPERTS, D, FF), D ** -0.5, 0.078125, ((0, 2), (2, 8)))
    w_down = gaussian(streams_of[5], (EXPERTS, D, FF), FF ** -0.5, 0.046875, ((0, 2), (1, 8)))
    return dict(tokens=tokens, routes=routes, gates=gates, w_gate=w_gate, w_up=w_up, w_down=w_down)


def reference(tokens, routes, gates, w_gate, w_up, w_down):
    model_width = tokens.shape[1]
    blocks = tokens.reshape(N_TILE, TOK_DEV, model_width).astype(jnp.float32)
    slot_ids = jnp.arange(CAP, dtype=jnp.int32)
    running = jnp.zeros((N_TILE, TOK_DEV, model_width), jnp.float32)
    for expert_id in range(w_gate.shape[0]):
        is_named = routes == expert_id
        chosen = jnp.any(is_named, axis=1).reshape(N_TILE, TOK_DEV)
        weight = jnp.sum(jnp.where(is_named, gates, jnp.float32(0.0)), axis=1).reshape(N_TILE, TOK_DEV)
        position = (jnp.cumsum(chosen.astype(jnp.int32), axis=1) - 1).astype(jnp.int32)
        dispatch = jnp.logical_and(chosen[:, None, :], position[:, None, :] == slot_ids[None, :, None]).astype(jnp.float32)
        picked = jnp.einsum("bct,btd->bcd", dispatch, blocks).astype(jnp.bfloat16).reshape(N_TILE * CAP, model_width)
        gate_proj = jnp.dot(picked, w_gate[expert_id], preferred_element_type=jnp.float32)
        up_proj = jnp.dot(picked, w_up[expert_id], preferred_element_type=jnp.float32)
        hidden = (jax.nn.silu(gate_proj) * up_proj).astype(jnp.bfloat16)
        result = jnp.dot(hidden, w_down[expert_id].T, preferred_element_type=jnp.float32)
        slot_weight = jnp.einsum("bct,bt->bc", dispatch, weight).reshape(N_TILE * CAP)
        contribution = (slot_weight[:, None] * result).astype(jnp.bfloat16).astype(jnp.float32)
        contribution = contribution.reshape(N_TILE, CAP, model_width)
        running = running + jnp.einsum("bct,bcd->btd", dispatch, contribution)
    return running.reshape(N_TILE * TOK_DEV, model_width).astype(jnp.bfloat16)
```

```python
import functools

import jax
import jax.numpy as jnp
from jax import lax
from jax.experimental import pallas as pl
from jax.experimental.pallas import tpu as pltpu
from jax.sharding import PartitionSpec as P

MIB = 1 << 20
SLOTS = 2
VMEM = pl.BlockSpec(memory_space=pltpu.VMEM)
SMEM = pl.BlockSpec(memory_space=pltpu.SMEM)
ANY = pl.BlockSpec(memory_space=pl.ANY)


def in_hbm(x):
    return pltpu.with_memory_space_constraint(x, pltpu.HBM)


def dispatch_kernel(tokens_ref, routes_ref, sends_ref, *, experts):
    tokens = tokens_ref[...].astype(jnp.float32)
    tiles = sends_ref.shape[0] // experts
    rows = tokens.shape[0]
    for e in range(experts):
        taken = jnp.int32(0)
        slots = [jnp.zeros((1, tokens.shape[1]), jnp.float32) for _ in range(SLOTS)]
        for r in range(rows):
            named = jnp.logical_or(routes_ref[r, 0] == e, routes_ref[r, 1] == e)
            for c in range(SLOTS):
                here = jnp.logical_and(named, taken == c).astype(jnp.float32)
                slots[c] = slots[c] + here * tokens[r:r + 1, :]
            taken = taken + named.astype(jnp.int32)
        block = jnp.concatenate(slots, axis=0).astype(jnp.bfloat16)
        for t in range(tiles):
            sends_ref[e * tiles + t] = block


def load_kernel(after_ref, hbm_ref, vmem_ref, sems):
    parts = sems.shape[0]
    rows = hbm_ref.shape[1] // parts
    copies = []
    for i in range(parts):
        part = pl.ds(i * rows, rows)
        copies.append(pltpu.make_async_copy(hbm_ref.at[0, part], vmem_ref.at[part], sems.at[i]))
        copies[-1].start()
    for copy in copies:
        copy.wait()


def load(w, after, name):
    parts = 6
    return pl.pallas_call(
        load_kernel,
        out_shape=pltpu.VMEM(w.shape[1:], w.dtype),
        in_specs=[ANY, ANY],
        out_specs=VMEM,
        scratch_shapes=[pltpu.SemaphoreType.DMA((parts,))],
        compiler_params=pltpu.CompilerParams(vmem_limit_bytes=MIB),
        cost_estimate=pl.CostEstimate(flops=0, bytes_accessed=2 * w.size * 2, transcendentals=0),
        name=name,
    )(after, in_hbm(w))


def hidden_kernel(rows_ref, w_gate_ref, w_up_hbm, hidden_ref, x_ref, ring, gate_ref, up_ref, sems):
    slots = hidden_ref.shape[0]
    half = rows_ref.shape[2]
    depth, chunk = ring.shape[0], ring.shape[1]
    steps = w_gate_ref.shape[0] // chunk

    def copy(i):
        return pltpu.make_async_copy(w_up_hbm.at[0, pl.ds(i * chunk, chunk)], ring.at[i % depth], sems.at[i % depth])

    for i in range(depth):
        copy(i).start()
    x_ref[...] = rows_ref[...].reshape(x_ref.shape)
    for i in range(steps):
        h, k = divmod(i * chunk, half)
        x = x_ref[h * slots:(h + 1) * slots, k:k + chunk]
        gate = jnp.dot(x, w_gate_ref[i * chunk:(i + 1) * chunk, :], preferred_element_type=jnp.float32)
        copy(i).wait()
        up = jnp.dot(x, ring[i % depth], preferred_element_type=jnp.float32)
        if i + depth < steps:
            copy(i + depth).start()
        gate_ref[...] = gate if i == 0 else gate_ref[...] + gate
        up_ref[...] = up if i == 0 else up_ref[...] + up
    gate = gate_ref[...]
    hidden_ref[...] = (gate / (1.0 + jnp.exp(-gate)) * up_ref[...]).astype(jnp.bfloat16)


def down_kernel(n, *refs):
    blocks, w_ref, sends_ref = refs[:n], refs[n], refs[n + 1]
    me = lax.axis_index("tile")
    tiles = blocks[0].shape[0] // SLOTS
    width = blocks[0].shape[1]
    total = jnp.zeros((blocks[0].shape[0], w_ref.shape[0]), jnp.float32)
    for k in range(n):
        columns = pl.ds(pl.multiple_of((me ^ k) * width, width), width)
        total += lax.dot_general(
            blocks[k][...], w_ref[:, columns], (((1,), (1,)), ((), ())),
            preferred_element_type=jnp.float32,
        )
    for t in range(tiles):
        for e in range(sends_ref.shape[0] // tiles):
            sends_ref[e * tiles + t] = total[t * SLOTS:(t + 1) * SLOTS, :]


def spread(x, experts):
    x = x.reshape(1, x.shape[0] // SLOTS, SLOTS, x.shape[1])
    return jnp.broadcast_to(x, (experts,) + x.shape[1:]).reshape(-1, SLOTS, x.shape[3])


def local(tokens, routes, gates, w_gate, w_up, w_down):
    experts = lax.axis_size("expert")
    tiles = lax.axis_size("tile")
    own = lax.axis_index("expert")
    half_width = tokens.shape[1]
    width = w_gate.shape[2]
    features = w_down.shape[1]
    slots = tiles * SLOTS
    direct = tiles <= 8

    sends = pl.pallas_call(
        functools.partial(dispatch_kernel, experts=experts),
        out_shape=jax.ShapeDtypeStruct((experts * tiles, SLOTS, half_width), jnp.bfloat16),
        in_specs=[VMEM, SMEM],
        out_specs=VMEM,
        compiler_params=pltpu.CompilerParams(vmem_limit_bytes=16 * MIB),
        name="dispatch",
    )(tokens, routes)
    gate_held = load(w_gate, sends, "load_gate")
    rows = lax.all_to_all(sends, ("expert", "tile"), split_axis=0, concat_axis=0, tiled=True)

    chunk = half_width // 4
    depth = 4
    hidden = pl.pallas_call(
        hidden_kernel,
        out_shape=jax.ShapeDtypeStruct((slots, width), jnp.bfloat16),
        in_specs=[VMEM, VMEM, ANY],
        out_specs=VMEM,
        scratch_shapes=[
            pltpu.VMEM((experts * slots, half_width), jnp.bfloat16),
            pltpu.VMEM((depth, chunk, width), jnp.bfloat16),
            pltpu.VMEM((slots, width), jnp.float32),
            pltpu.VMEM((slots, width), jnp.float32),
            pltpu.SemaphoreType.DMA((depth,)),
        ],
        compiler_params=pltpu.CompilerParams(vmem_limit_bytes=24 * MIB),
        name="hidden",
    )(rows, gate_held, in_hbm(w_up))

    if direct:
        down_held = load(w_down, hidden, "load_down")
        blocks = [hidden]
        for k in range(1, tiles):
            blocks.append(lax.ppermute(hidden, "tile", [(t, t ^ k) for t in range(tiles)]))
        sends = pl.pallas_call(
            functools.partial(down_kernel, tiles),
            out_shape=jax.ShapeDtypeStruct((experts * tiles, SLOTS, features), jnp.float32),
            in_specs=[VMEM] * (tiles + 1),
            out_specs=VMEM,
            compiler_params=pltpu.CompilerParams(vmem_limit_bytes=8 * MIB),
            name="down",
        )(*blocks, down_held)
    else:
        gathered = lax.all_gather(hidden, "tile", axis=1, tiled=True)
        sends = spread(lax.dot_general(
            gathered, w_down[0], (((1,), (1,)), ((), ())), preferred_element_type=jnp.float32
        ), experts)

    back = lax.all_to_all(sends, ("expert", "tile"), split_axis=0, concat_axis=0, tiled=True)
    back, routes, gates = lax.optimization_barrier((back, routes, gates))
    back = back.reshape(experts, tiles, SLOTS, features)
    back = lax.dynamic_slice_in_dim(back, own * (tiles // experts), tiles // experts, 1)
    back = jnp.transpose(back, (0, 2, 1, 3)).reshape(experts, SLOTS, half_width)

    window_ids = lax.broadcasted_iota(jnp.int32, (1, 1, experts), 2)
    is_named = routes[:, :, None] == window_ids
    chosen = jnp.any(is_named, axis=1)
    weight = jnp.sum(jnp.where(is_named, gates[:, :, None], jnp.float32(0.0)), axis=1)
    position = jnp.cumsum(chosen.astype(jnp.int32), axis=0) - 1
    mixed = jnp.zeros((tokens.shape[0], half_width), jnp.float32)
    for e in range(experts):
        for c in range(SLOTS):
            mask = jnp.logical_and(chosen[:, e:e + 1], position[:, e:e + 1] == c)
            contribution = (weight[:, e:e + 1] * back[e, c][None]).astype(jnp.bfloat16)
            mixed += jnp.where(mask, contribution, 0).astype(jnp.float32)
    return mixed.astype(jnp.bfloat16)


def solution(mesh):
    in_specs = (
        P(("group", "tile"), "expert"),
        P(("group", "tile"), None),
        P(("group", "tile"), None),
        P("expert", None, "tile"),
        P("expert", None, "tile"),
        P("expert", "tile", None),
    )
    out_specs = P(("group", "tile"), "expert")
    return jax.shard_map(local, mesh=mesh, in_specs=in_specs, out_specs=out_specs, check_vma=False)
```

```python
import functools

import jax
import jax.numpy as jnp
from jax import lax
from jax.experimental import pallas as pl
from jax.experimental.pallas import tpu as pltpu
from jax.sharding import PartitionSpec as P

MIB = 1 << 20
SLOTS = 2
VMEM = pl.BlockSpec(memory_space=pltpu.VMEM)
SMEM = pl.BlockSpec(memory_space=pltpu.SMEM)


def load_kernel(after_ref, hbm_ref, vmem_ref, sems):
    parts = sems.shape[0]
    rows = hbm_ref.shape[1] // parts
    copies = []
    for i in range(parts):
        part = pl.ds(i * rows, rows)
        copies.append(pltpu.make_async_copy(hbm_ref.at[:, part], vmem_ref.at[:, part], sems.at[i]))
        copies[-1].start()
    for copy in copies:
        copy.wait()


def load(w, after, name):
    parts = 6
    return pl.pallas_call(
        load_kernel,
        out_shape=pltpu.VMEM(w.shape, w.dtype),
        in_specs=[pl.BlockSpec(memory_space=pl.ANY)] * 2,
        out_specs=VMEM,
        scratch_shapes=[pltpu.SemaphoreType.DMA((parts,))],
        compiler_params=pltpu.CompilerParams(vmem_limit_bytes=MIB),
        cost_estimate=pl.CostEstimate(flops=0, bytes_accessed=2 * w.size * 2, transcendentals=0),
        name=name,
    )(after, pltpu.with_memory_space_constraint(w, pltpu.HBM))


def call(kernel, name, out, in_specs, limit, seconds=0.0, scratch=()):
    return pl.pallas_call(
        kernel,
        out_shape=out,
        in_specs=in_specs,
        out_specs=jax.tree.map(lambda _: VMEM, out),
        scratch_shapes=scratch,
        compiler_params=pltpu.CompilerParams(vmem_limit_bytes=limit),
        cost_estimate=pl.CostEstimate(flops=int(seconds*1e15), bytes_accessed=0, transcendentals=0),
        name=name,
    )


def slot_rows(routes_ref, e, rows):
    taken = jnp.int32(0)
    found = []
    for r in range(rows):
        named = jnp.logical_or(routes_ref[0, r] == e, routes_ref[1, r] == e)
        found.append((named, taken))
        taken = taken + named.astype(jnp.int32)
    return found


def dispatch_kernel(tokens_ref, routes_ref, sends_ref):
    tokens = tokens_ref[...].astype(jnp.float32)
    rows = tokens.shape[0]
    blocks = []
    for e in range(sends_ref.shape[0] // SLOTS):
        found = slot_rows(routes_ref, e, rows)
        for c in range(SLOTS):
            row = jnp.zeros((1, tokens.shape[1]), jnp.float32)
            for r, (named, slot) in enumerate(found):
                here = jnp.logical_and(named, slot == c).astype(jnp.float32)
                row = row + here * tokens[r:r + 1, :]
            blocks.append(row)
    sends_ref[...] = jnp.concatenate(blocks, axis=0).astype(jnp.bfloat16)


def merge_kernel(*refs):
    *blocks, own_ref, other_ref, own_f32, other_f32 = refs
    me, mine = lax.axis_index("tile"), lax.axis_index("expert")
    for k, block in enumerate(blocks):
        rows = block[...].astype(jnp.float32)
        first, second = rows[:SLOTS], rows[SLOTS:]
        own_f32[me ^ k] = jnp.where(mine == 0, first, second)
        other_f32[me ^ k] = jnp.where(mine == 0, second, first)
    own_ref[...] = own_f32[...].reshape(own_ref.shape).astype(jnp.bfloat16)
    other_ref[...] = other_f32[...].reshape(other_ref.shape).astype(jnp.bfloat16)


def project_kernel(own_ref, other_ref, w_gate_ref, w_up_hbm, gate_ref, up_ref, ring, sems):
    mine = lax.axis_index("expert")
    half = own_ref.shape[1]
    depth, chunk = ring.shape[0], ring.shape[1]
    steps = 2 * half // chunk

    def first_row(i):
        part, k = divmod(i * chunk, half)
        return pl.multiple_of((mine if part == 0 else 1 - mine) * half + k, chunk)

    def copy(i):
        return pltpu.make_async_copy(
            w_up_hbm.at[0, pl.ds(first_row(i), chunk)], ring.at[i % depth], sems.at[i % depth])

    for i in range(depth):
        copy(i).start()
    for i in range(steps):
        part, k = divmod(i * chunk, half)
        x = (own_ref if part == 0 else other_ref)[:, k:k + chunk]
        gate = jnp.dot(x, w_gate_ref[0, pl.ds(first_row(i), chunk), :], preferred_element_type=jnp.float32)
        copy(i).wait()
        up = jnp.dot(x, ring[i % depth], preferred_element_type=jnp.float32)
        if i + depth < steps:
            copy(i + depth).start()
        gate_ref[...] = gate if i == 0 else gate_ref[...] + gate
        up_ref[...] = up if i == 0 else up_ref[...] + up


def activate_kernel(gate_ref, up_ref, hidden_ref):
    gate = gate_ref[...]
    hidden_ref[...] = (gate / (1.0 + jnp.exp(-gate)) * up_ref[...]).astype(jnp.bfloat16)


def down_kernel(n, *refs):
    blocks, w_ref, sends_ref = refs[:n], refs[n], refs[n + 1]
    me = lax.axis_index("tile")
    width = blocks[0].shape[1]
    total = jnp.zeros((w_ref.shape[1], blocks[0].shape[0]), jnp.float32)
    for k in range(n):
        columns = pl.ds(pl.multiple_of((me ^ k) * width, width), width)
        total += lax.dot_general(
            w_ref[0, :, columns], blocks[k][...], (((1,), (1,)), ((), ())),
            preferred_element_type=jnp.float32,
        )
    total = total.T
    for t in range(sends_ref.shape[0]):
        sends_ref[t] = total[t * SLOTS:(t + 1) * SLOTS, :]


def combine_kernel(own_ref, other_ref, routes_ref, gates_ref, out_ref):
    mine = lax.axis_index("expert")
    tiles, _, features = own_ref.shape
    halves = tiles // 2
    rows = out_ref.shape[0]
    found = [slot_rows(routes_ref, e, rows) for e in range(2)]
    weight = [[
        jnp.where(routes_ref[0, r] == e, gates_ref[0, r], 0.0)
        + jnp.where(routes_ref[1, r] == e, gates_ref[1, r], 0.0)
        for r in range(rows)
    ] for e in range(2)]
    for i in range(halves):
        own, other = own_ref[mine * halves + i], other_ref[mine * halves + i]
        lines = []
        for r in range(rows):
            line = jnp.zeros((1, features), jnp.float32)
            for e in range(2):
                named, slot = found[e][r]
                both = jnp.where(mine == e, own, other)
                value = jnp.where(slot == 0, both[0:1], both[1:2])
                value = (weight[e][r] * value).astype(jnp.bfloat16).astype(jnp.float32)
                line = line + jnp.where(named, value, 0.0)
            lines.append(line)
        out_ref[:, i * features:(i + 1) * features] = jnp.concatenate(lines, axis=0).astype(jnp.bfloat16)


def local_direct(tokens, routes, gates, w_gate, w_up, w_down):
    tiles = lax.axis_size("tile")
    rows, half_width = tokens.shape
    width, features = w_gate.shape[2], w_down.shape[1]
    slots = tiles * SLOTS
    routes, gates = routes.T, gates.T

    def to_tiles(x):
        return [x] + [lax.ppermute(x, "tile", [(t, t ^ k) for t in range(tiles)]) for k in range(1, tiles)]

    def to_core(x):
        return lax.ppermute(x, "expert", [(0, 1), (1, 0)])

    f32 = lambda *shape: jax.ShapeDtypeStruct(shape, jnp.float32)
    bf16 = lambda *shape: jax.ShapeDtypeStruct(shape, jnp.bfloat16)
    sends = call(dispatch_kernel, "dispatch", bf16(2 * SLOTS, half_width), [VMEM, SMEM], 16 * MIB, 0)(tokens, routes)
    own, other = call(
        merge_kernel, "merge", (bf16(slots, half_width),) * 2, [VMEM] * tiles, 16 * MIB, 0e-6,
        [pltpu.VMEM((tiles, SLOTS, half_width), jnp.float32)] * 2,
    )(*to_tiles(sends))
    other = to_core(other)
    chunk, depth = half_width // 4, 3
    gate, up = call(
        project_kernel, "project", (f32(slots, width),) * 2, [VMEM, VMEM, VMEM, pl.BlockSpec(memory_space=pl.ANY)], 20 * MIB, 0,
        [pltpu.VMEM((depth, chunk, width), jnp.bfloat16), pltpu.SemaphoreType.DMA((depth,))],
    )(own, other, load(w_gate, sends, "load_gate"), pltpu.with_memory_space_constraint(w_up, pltpu.HBM))
    hidden = call(activate_kernel, "activate", bf16(slots, width), [VMEM, VMEM], 16 * MIB, 0)(gate, up)
    result = call(functools.partial(down_kernel, tiles), "down", f32(tiles, SLOTS, features), [VMEM] * (tiles + 1), 16 * MIB, 0e-6)(
        *to_tiles(hidden), load(w_down, hidden, "load_down"))
    back = lax.all_to_all(result, "tile", split_axis=0, concat_axis=0, tiled=True)
    return call(combine_kernel, "combine", bf16(rows, half_width), [VMEM, VMEM, SMEM, SMEM], 16 * MIB)(
        back, to_core(back), routes, gates)


def local_gathered(tokens, routes, gates, w_gate, w_up, w_down):
    experts = lax.axis_size("expert")
    tile_count = lax.axis_size("tile")
    own_expert = lax.axis_index("expert")
    half_width = tokens.shape[1]
    tok_rows = tokens.shape[0]
    slot_count = max(2, tok_rows // 2)
    window_ids = lax.broadcasted_iota(jnp.int32, (1, 1, experts), 2)
    is_named = routes[:, :, None] == window_ids
    chosen = jnp.any(is_named, axis=1)
    weight = jnp.sum(jnp.where(is_named, gates[:, :, None], jnp.float32(0.0)), axis=1)
    position = jnp.cumsum(chosen.astype(jnp.int32), axis=0) - 1
    slot_ids = lax.broadcasted_iota(jnp.int32, (1, slot_count, 1), 1)
    dispatch = jnp.logical_and(chosen.T[:, None, :], position.T[:, None, :] == slot_ids)
    placing = dispatch.astype(jnp.bfloat16)
    outgoing = jnp.einsum(
        "ecr,rd->ecd", placing, tokens, preferred_element_type=jnp.float32
    ).astype(jnp.bfloat16)
    slot_weight = jnp.einsum("ecr,re->ec", dispatch.astype(jnp.float32), weight)
    everything = lax.all_gather(outgoing[None], ("expert", "tile"), axis=0, tiled=True)
    picked = lax.dynamic_slice_in_dim(everything, own_expert, 1, 1)[:, 0]
    picked = picked.reshape(experts, tile_count, slot_count, half_width)
    gathered = jnp.transpose(picked, (1, 2, 0, 3)).reshape(
        tile_count * slot_count, experts * half_width
    )
    gate_proj = jnp.dot(gathered, w_gate[0], preferred_element_type=jnp.float32)
    up_proj = jnp.dot(gathered, w_up[0], preferred_element_type=jnp.float32)
    hidden = (jax.nn.silu(gate_proj) * up_proj).astype(jnp.bfloat16)
    columns = w_down[0]
    summed = lax.dot_general(
        columns,
        lax.all_gather(hidden, "tile", axis=1, tiled=True),
        (((1,), (1,)), ((), ())),
        preferred_element_type=jnp.float32,
    )
    homeward = lax.all_to_all(summed, "tile", split_axis=1, concat_axis=0, tiled=True)
    returned = lax.all_to_all(homeward, "expert", split_axis=0, concat_axis=1, tiled=True)
    contribution = (slot_weight.reshape(1, experts * slot_count) * returned).astype(jnp.bfloat16)
    flat_places = placing.reshape(experts * slot_count, tok_rows)
    return jnp.einsum(
        "st,ds->td", flat_places, contribution, preferred_element_type=jnp.float32
    ).astype(jnp.bfloat16)


def solution(mesh):
    in_specs = (
        P(("group", "tile"), "expert"),
        P(("group", "tile"), None),
        P(("group", "tile"), None),
        P("expert", None, "tile"),
        P("expert", None, "tile"),
        P("expert", "tile", None),
    )
    out_specs = P(("group", "tile"), "expert")
    local = local_direct if mesh.shape["tile"] <= 8 else local_gathered
    return jax.shard_map(local, mesh=mesh, in_specs=in_specs, out_specs=out_specs, check_vma=False)
```

```python
import functools

import jax
import jax.numpy as jnp
from jax import lax
from jax.experimental import pallas as pl
from jax.experimental.pallas import tpu as pltpu
from jax.sharding import PartitionSpec as P

MIB = 1 << 20
SLOTS = 2
VMEM = pl.BlockSpec(memory_space=pltpu.VMEM)
SMEM = pl.BlockSpec(memory_space=pltpu.SMEM)
ANY = pl.BlockSpec(memory_space=pl.ANY)


def in_vmem(x):
    return pltpu.with_memory_space_constraint(x, pltpu.VMEM)


def in_hbm(x):
    return pltpu.with_memory_space_constraint(x, pltpu.HBM)


def call(kernel, name, out, in_specs, limit, seconds=0.0, scratch=()):
    return pl.pallas_call(
        kernel,
        out_shape=out,
        in_specs=in_specs,
        out_specs=jax.tree.map(lambda _: VMEM, out),
        scratch_shapes=scratch,
        compiler_params=pltpu.CompilerParams(vmem_limit_bytes=limit),
        cost_estimate=pl.CostEstimate(flops=int(seconds*1e15), bytes_accessed=0, transcendentals=0),
        name=name,
    )


def slot_rows(routes_ref, e, rows):
    taken = jnp.int32(0)
    found = []
    for r in range(rows):
        named = jnp.logical_or(routes_ref[0, r] == e, routes_ref[1, r] == e)
        found.append((named, taken))
        taken = taken + named.astype(jnp.int32)
    return found


def dispatch_kernel(tokens_hbm, routes_hbm, sends_ref, tokens_ref, routes_ref, sems):
    copies = [
        pltpu.make_async_copy(routes_hbm, routes_ref, sems.at[0]),
        pltpu.make_async_copy(tokens_hbm, tokens_ref, sems.at[1]),
    ]
    for copy in copies:
        copy.start()
    for copy in copies:
        copy.wait()
    tokens = tokens_ref[...].astype(jnp.float32)
    rows = tokens.shape[0]
    blocks = []
    for e in range(sends_ref.shape[1] // SLOTS):
        found = slot_rows(routes_ref, e, rows)
        for c in range(SLOTS):
            row = jnp.zeros((1, tokens.shape[1]), jnp.float32)
            for r, (named, slot) in enumerate(found):
                here = jnp.logical_and(named, slot == c).astype(jnp.float32)
                row = row + here * tokens[r:r + 1, :]
            blocks.append(row)
    block = jnp.concatenate(blocks, axis=0).astype(jnp.bfloat16)
    for t in range(sends_ref.shape[0]):
        sends_ref[t] = block


def merge_kernel(blocks_ref, own_ref, other_ref, first_f32, second_f32):
    mine = lax.axis_index("expert")
    for t in range(blocks_ref.shape[0]):
        rows = blocks_ref[t].astype(jnp.float32)
        first_f32[t] = rows[:SLOTS]
        second_f32[t] = rows[SLOTS:]
    first = first_f32[...].reshape(own_ref.shape).astype(jnp.bfloat16)
    second = second_f32[...].reshape(own_ref.shape).astype(jnp.bfloat16)
    own_ref[...] = jnp.where(mine == 0, first, second)
    other_ref[...] = jnp.where(mine == 0, second, first)


def project_kernel(own_ref, other_ref, w_gate_ref, w_up_hbm, gate_ref, up_ref, ring, sems):
    mine = lax.axis_index("expert")
    half = own_ref.shape[1]
    depth, chunk = ring.shape[0], ring.shape[1]
    steps = 2 * half // chunk

    def first_row(i):
        part, k = divmod(i * chunk, half)
        return pl.multiple_of((mine if part == 0 else 1 - mine) * half + k, chunk)

    def copy(i):
        return pltpu.make_async_copy(
            w_up_hbm.at[0, pl.ds(first_row(i), chunk)], ring.at[i % depth], sems.at[i % depth])

    for i in range(depth):
        copy(i).start()
    for i in range(steps):
        part, k = divmod(i * chunk, half)
        x = (own_ref if part == 0 else other_ref)[:, k:k + chunk]
        gate = jnp.dot(x, w_gate_ref[0, pl.ds(first_row(i), chunk), :], preferred_element_type=jnp.float32)
        copy(i).wait()
        up = jnp.dot(x, ring[i % depth], preferred_element_type=jnp.float32)
        if i + depth < steps:
            copy(i + depth).start()
        gate_ref[...] = gate if i == 0 else gate_ref[...] + gate
        up_ref[...] = up if i == 0 else up_ref[...] + up


def activate_kernel(gate_ref, up_ref, hidden_ref):
    gate = gate_ref[...]
    hidden_ref[...] = (gate / (1.0 + jnp.exp(-gate)) * up_ref[...]).astype(jnp.bfloat16)


def down_kernel(n, *refs):
    blocks, w_ref, sends_ref, total_ref = refs[:n], refs[n], refs[n + 1], refs[n + 2]
    me = lax.axis_index("tile")
    width = blocks[0].shape[1]
    slots = blocks[0].shape[0]
    part = 128
    contract = (((1,), (1,)), ((), ()))

    def step(i, carry):
        rows = [pl.ds(pl.multiple_of((2 * i + h) * part, part), part) for h in range(2)]
        first = jnp.zeros((slots, part), jnp.float32)
        second = jnp.zeros((part, slots), jnp.float32)
        for k in range(n):
            columns = pl.ds(pl.multiple_of((me ^ k) * width, width), width)
            x = blocks[k][...]
            first += lax.dot_general(x, w_ref[0, rows[0], columns], contract, preferred_element_type=jnp.float32)
            second += lax.dot_general(w_ref[0, rows[1], columns], x, contract, preferred_element_type=jnp.float32)
        total_ref[:, rows[0]] = first
        total_ref[:, rows[1]] = second.T
        return carry

    lax.fori_loop(0, w_ref.shape[1] // (2 * part), step, 0)
    for t in range(sends_ref.shape[0]):
        sends_ref[t] = total_ref[t * SLOTS:(t + 1) * SLOTS, :]


def combine_kernel(own_ref, other_ref, routes_ref, gates_ref, out_ref):
    mine = lax.axis_index("expert")
    tiles, _, features = own_ref.shape
    halves = tiles // 2
    rows = out_ref.shape[0]
    found = [slot_rows(routes_ref, e, rows) for e in range(2)]
    weight = [[
        jnp.where(routes_ref[0, r] == e, gates_ref[0, r], 0.0)
        + jnp.where(routes_ref[1, r] == e, gates_ref[1, r], 0.0)
        for r in range(rows)
    ] for e in range(2)]
    for i in range(halves):
        own, other = own_ref[mine * halves + i], other_ref[mine * halves + i]
        lines = []
        for r in range(rows):
            line = jnp.zeros((1, features), jnp.float32)
            for e in range(2):
                named, slot = found[e][r]
                both = jnp.where(mine == e, own, other)
                value = jnp.where(slot == 0, both[0:1], both[1:2])
                value = (weight[e][r] * value).astype(jnp.bfloat16).astype(jnp.float32)
                line = line + jnp.where(named, value, 0.0)
            lines.append(line)
        out_ref[:, i * features:(i + 1) * features] = jnp.concatenate(lines, axis=0).astype(jnp.bfloat16)


def local_direct(tokens, routes, gates, w_gate, w_up, w_down):
    tiles = lax.axis_size("tile")
    rows, half_width = tokens.shape
    width, features = w_gate.shape[2], w_down.shape[1]
    slots = tiles * SLOTS
    routes, gates = routes.T, gates.T

    def to_tiles(x):
        return [x] + [lax.ppermute(x, "tile", [(t, t ^ k) for t in range(tiles)]) for k in range(1, tiles)]

    def to_core(x):
        return lax.ppermute(x, "expert", [(0, 1), (1, 0)])

    f32 = lambda *shape: jax.ShapeDtypeStruct(shape, jnp.float32)
    bf16 = lambda *shape: jax.ShapeDtypeStruct(shape, jnp.bfloat16)
    sends = call(
        dispatch_kernel, "dispatch", bf16(tiles, 2 * SLOTS, half_width), [ANY, ANY], 4 * MIB, 300e-6,
        [pltpu.VMEM((rows, half_width), jnp.bfloat16), pltpu.SMEM((2, rows), jnp.int32), pltpu.SemaphoreType.DMA((2,))],
    )(in_hbm(tokens), in_hbm(routes))
    blocks = lax.all_to_all(sends, "tile", split_axis=0, concat_axis=0, tiled=True)
    own, other = call(
        merge_kernel, "merge", (bf16(slots, half_width),) * 2, [VMEM], 4 * MIB, 0e-6,
        [pltpu.VMEM((tiles, SLOTS, half_width), jnp.float32)] * 2,
    )(blocks)
    other = to_core(other)
    chunk, depth = half_width // 4, 3
    gate, up = call(
        project_kernel, "project", (f32(slots, width),) * 2, [VMEM, VMEM, VMEM, ANY], 20 * MIB, 0,
        [pltpu.VMEM((depth, chunk, width), jnp.bfloat16), pltpu.SemaphoreType.DMA((depth,))],
    )(own, other, in_vmem(w_gate), in_hbm(w_up))
    hidden = call(activate_kernel, "activate", bf16(slots, width), [VMEM, VMEM], 4 * MIB, 200e-6)(gate, up)
    result = call(
        functools.partial(down_kernel, tiles), "down", f32(tiles, SLOTS, features), [VMEM] * (tiles + 1), 8 * MIB, 0,
        [pltpu.VMEM((slots, features), jnp.float32)],
    )(*to_tiles(hidden), in_vmem(w_down))
    back = lax.all_to_all(result, "tile", split_axis=0, concat_axis=0, tiled=True)
    return call(combine_kernel, "combine", bf16(rows, half_width), [VMEM, VMEM, SMEM, SMEM], 4 * MIB)(
        back, to_core(back), routes, gates)


def local_gathered(tokens, routes, gates, w_gate, w_up, w_down):
    experts = lax.axis_size("expert")
    tile_count = lax.axis_size("tile")
    own_expert = lax.axis_index("expert")
    half_width = tokens.shape[1]
    tok_rows = tokens.shape[0]
    slot_count = max(2, tok_rows // 2)
    window_ids = lax.broadcasted_iota(jnp.int32, (1, 1, experts), 2)
    is_named = routes[:, :, None] == window_ids
    chosen = jnp.any(is_named, axis=1)
    weight = jnp.sum(jnp.where(is_named, gates[:, :, None], jnp.float32(0.0)), axis=1)
    position = jnp.cumsum(chosen.astype(jnp.int32), axis=0) - 1
    slot_ids = lax.broadcasted_iota(jnp.int32, (1, slot_count, 1), 1)
    dispatch = jnp.logical_and(chosen.T[:, None, :], position.T[:, None, :] == slot_ids)
    placing = dispatch.astype(jnp.bfloat16)
    outgoing = jnp.einsum(
        "ecr,rd->ecd", placing, tokens, preferred_element_type=jnp.float32
    ).astype(jnp.bfloat16)
    slot_weight = jnp.einsum("ecr,re->ec", dispatch.astype(jnp.float32), weight)
    everything = lax.all_gather(outgoing[None], ("expert", "tile"), axis=0, tiled=True)
    picked = lax.dynamic_slice_in_dim(everything, own_expert, 1, 1)[:, 0]
    picked = picked.reshape(experts, tile_count, slot_count, half_width)
    gathered = jnp.transpose(picked, (1, 2, 0, 3)).reshape(
        tile_count * slot_count, experts * half_width
    )
    gate_proj = jnp.dot(gathered, w_gate[0], preferred_element_type=jnp.float32)
    up_proj = jnp.dot(gathered, w_up[0], preferred_element_type=jnp.float32)
    hidden = (jax.nn.silu(gate_proj) * up_proj).astype(jnp.bfloat16)
    columns = w_down[0]
    summed = lax.dot_general(
        columns,
        lax.all_gather(hidden, "tile", axis=1, tiled=True),
        (((1,), (1,)), ((), ())),
        preferred_element_type=jnp.float32,
    )
    homeward = lax.all_to_all(summed, "tile", split_axis=1, concat_axis=0, tiled=True)
    returned = lax.all_to_all(homeward, "expert", split_axis=0, concat_axis=1, tiled=True)
    contribution = (slot_weight.reshape(1, experts * slot_count) * returned).astype(jnp.bfloat16)
    flat_places = placing.reshape(experts * slot_count, tok_rows)
    return jnp.einsum(
        "st,ds->td", flat_places, contribution, preferred_element_type=jnp.float32
    ).astype(jnp.bfloat16)


def solution(mesh):
    in_specs = (
        P(("group", "tile"), "expert"),
        P(("group", "tile"), None),
        P(("group", "tile"), None),
        P("expert", None, "tile"),
        P("expert", None, "tile"),
        P("expert", "tile", None),
    )
    out_specs = P(("group", "tile"), "expert")
    local = local_direct if mesh.shape["tile"] <= 8 else local_gathered
    return jax.shard_map(local, mesh=mesh, in_specs=in_specs, out_specs=out_specs, check_vma=False)
```

```python
import functools

import jax
import jax.numpy as jnp
from jax import lax
from jax.experimental import pallas as pl
from jax.experimental.pallas import tpu as pltpu
from jax.sharding import PartitionSpec as P

MIB = 1 << 20
SLOTS = 2
VMEM = pl.BlockSpec(memory_space=pltpu.VMEM)
ANY = pl.BlockSpec(memory_space=pl.ANY)


def in_vmem(x):
    return pltpu.with_memory_space_constraint(x, pltpu.VMEM)


def in_hbm(x):
    return pltpu.with_memory_space_constraint(x, pltpu.HBM)


def call(kernel, name, out, in_specs, limit, seconds=0.0, scratch=()):
    return pl.pallas_call(
        kernel,
        out_shape=out,
        in_specs=in_specs,
        out_specs=jax.tree.map(lambda _: VMEM, out),
        scratch_shapes=scratch,
        compiler_params=pltpu.CompilerParams(vmem_limit_bytes=limit),
        cost_estimate=pl.CostEstimate(flops=int(seconds*1e15), bytes_accessed=0, transcendentals=0),
        name=name,
    )


def slot_rows(routes_ref, e, rows):
    taken = jnp.int32(0)
    found = []
    for r in range(rows):
        named = jnp.logical_or(routes_ref[0, r] == e, routes_ref[1, r] == e)
        found.append((named, taken))
        taken = taken + named.astype(jnp.int32)
    return found


def dispatch_kernel(tokens_hbm, routes_hbm, gates_hbm, sends_ref, table_ref, tokens_ref, routes_ref, gates_ref, sems):
    copies = [
        pltpu.make_async_copy(routes_hbm, routes_ref, sems.at[0]),
        pltpu.make_async_copy(gates_hbm, gates_ref, sems.at[1]),
        pltpu.make_async_copy(tokens_hbm, tokens_ref, sems.at[2]),
    ]
    for copy in copies:
        copy.start()
    for copy in copies:
        copy.wait()
    tokens = tokens_ref[...].astype(jnp.float32)
    rows = tokens.shape[0]
    tiles = sends_ref.shape[0] // 2
    for e in range(2):
        found = slot_rows(routes_ref, e, rows)
        base = e * (1 + SLOTS)
        line = (1, table_ref.shape[2])
        for r in range(rows):
            weight = jnp.where(routes_ref[0, r] == e, gates_ref[0, r], 0.0)
            weight = weight + jnp.where(routes_ref[1, r] == e, gates_ref[1, r], 0.0)
            table_ref[base, r:r + 1, :] = jnp.full(line, weight, jnp.float32)
        slots = []
        for c in range(SLOTS):
            row = jnp.zeros((1, tokens.shape[1]), jnp.float32)
            for r, (named, slot) in enumerate(found):
                here = jnp.logical_and(named, slot == c).astype(jnp.float32)
                row = row + here * tokens[r:r + 1, :]
                table_ref[base + 1 + c, r:r + 1, :] = jnp.full(line, here, jnp.float32)
            slots.append(row)
        block = jnp.concatenate(slots, axis=0).astype(jnp.bfloat16)
        for t in range(tiles):
            sends_ref[e * tiles + t] = block


def merge_kernel(blocks_ref, rows_ref):
    rows_ref[...] = blocks_ref[...].reshape(rows_ref.shape)


def project(rows_ref, w_ref, columns):
    slots, half = rows_ref.shape[0] // 2, rows_ref.shape[1]
    total = jnp.dot(rows_ref[:slots, :], w_ref[0, :half, columns], preferred_element_type=jnp.float32)
    return total + jnp.dot(rows_ref[slots:, :], w_ref[0, half:, columns], preferred_element_type=jnp.float32)


def over_columns(width, body):
    tile = 256

    def step(i, carry):
        body(pl.ds(pl.multiple_of(i * tile, tile), tile))
        return carry

    lax.fori_loop(0, width // tile, step, 0)


def gate_kernel(rows_ref, w_ref, out_ref):
    def body(columns):
        out_ref[:, columns] = project(rows_ref, w_ref, columns)

    over_columns(out_ref.shape[1], body)


def hidden_kernel(rows_ref, w_ref, gate_ref, hidden_ref):
    def body(columns):
        up = project(rows_ref, w_ref, columns)
        gate = gate_ref[:, columns]
        hidden_ref[:, columns] = (gate / (1.0 + jnp.exp(-gate)) * up).astype(jnp.bfloat16)

    over_columns(hidden_ref.shape[1], body)


def down_kernel(steps, order, first, last, *refs):
    n = len(steps)
    blocks, w_ref, rest = refs[:n], refs[n], refs[n + 1:]
    out_ref = rest[-1]
    me = lax.axis_index("tile")
    slots, width = blocks[0].shape
    part = 256
    starts = []
    for step in steps:
        tile = jnp.int32(0)
        for i, t in enumerate(order):
            tile = jnp.where(me == t, order[(i + step) % len(order)], tile)
        starts.append(pl.multiple_of(tile * width, width))
    for i in range(w_ref.shape[1] // part):
        rows = slice(i * part, (i + 1) * part)
        total = None if first else rest[0][rows, :]
        for block, start in zip(blocks, starts):
            term = lax.dot_general(
                w_ref[0, rows, pl.ds(start, width)], block[...], (((1,), (1,)), ((), ())),
                preferred_element_type=jnp.float32,
            )
            total = term if total is None else total + term
        if not last:
            out_ref[rows, :] = total
        else:
            total = total.T
            for t in range(out_ref.shape[0]):
                out_ref[t, :, rows] = total[t * SLOTS:(t + 1) * SLOTS, :]


def combine_kernel(own_ref, other_ref, table_ref, out_ref):
    mine = lax.axis_index("expert")
    halves, features = own_ref.shape[0] // 2, own_ref.shape[2]
    weight = [table_ref[e * (1 + SLOTS)][:, :1] for e in range(2)]
    inside = [[table_ref[e * (1 + SLOTS) + 1 + c][:, :1] for c in range(SLOTS)] for e in range(2)]
    for i in range(halves):
        own, other = own_ref[mine * halves + i], other_ref[mine * halves + i]
        mixed = jnp.zeros((out_ref.shape[0], features), jnp.float32)
        for e in range(2):
            both = jnp.where(mine == e, own, other)
            for c in range(SLOTS):
                value = (weight[e] * both[c:c + 1]).astype(jnp.bfloat16).astype(jnp.float32)
                mixed = mixed + jnp.where(inside[e][c] != 0.0, value, 0.0)
        out_ref[:, i * features:(i + 1) * features] = mixed.astype(jnp.bfloat16)


def local_direct(tokens, routes, gates, w_gate, w_up, w_down):
    tiles = lax.axis_size("tile")
    rows, half_width = tokens.shape
    width, features = w_gate.shape[2], w_down.shape[1]
    slots = tiles * SLOTS
    routes, gates = routes.T, gates.T

    def to_core(x):
        return lax.ppermute(x, "expert", [(0, 1), (1, 0)])

    f32 = lambda *shape: jax.ShapeDtypeStruct(shape, jnp.float32)
    bf16 = lambda *shape: jax.ShapeDtypeStruct(shape, jnp.bfloat16)
    sends, table = call(
        dispatch_kernel, "dispatch",
        (bf16(2 * tiles, SLOTS, half_width), f32(2 * (1 + SLOTS), rows, 128)), [ANY] * 3, 4 * MIB, 600e-6,
        [
            pltpu.VMEM((rows, half_width), jnp.bfloat16),
            pltpu.SMEM((2, rows), jnp.int32),
            pltpu.SMEM((2, rows), jnp.float32),
            pltpu.SemaphoreType.DMA((3,)),
        ],
    )(in_hbm(tokens), in_hbm(routes), in_hbm(gates))
    blocks = lax.all_to_all(sends, ("expert", "tile"), split_axis=0, concat_axis=0, tiled=True)
    x = call(merge_kernel, "merge", bf16(2 * slots, half_width), [VMEM], 4 * MIB, 0e-6)(blocks)
    gate = call(gate_kernel, "gate", f32(slots, width), [VMEM] * 2, 4 * MIB, 0e-6)(x, in_vmem(w_gate))
    hidden = call(hidden_kernel, "hidden", bf16(slots, width), [VMEM] * 3, 4 * MIB, 200e-6)(x, in_vmem(w_up), gate)
    order = list(range(0, tiles, 2)) + list(range(tiles - 1, 0, -2))
    ahead = [(t, order[(i + 1) % tiles]) for i, t in enumerate(order)]
    back = [(t, order[i - 1]) for i, t in enumerate(order)]

    def down(total, steps, blocks):
        first, last = total is None, -(tiles // 2) in steps
        out = f32(tiles, SLOTS, features) if last else f32(features, slots)
        return call(
            functools.partial(down_kernel, steps, order, first, last), "down", out,
            [VMEM] * (len(blocks) + 2 - first), 8 * MIB, 0e-6,
        )(*blocks, in_vmem(w_down), *(() if first else (total,)))

    below, above = hidden, hidden
    total, steps, blocks = None, [0], [hidden]
    for i in range(1, tiles // 2 + 1):
        below = lax.ppermute(below, "tile", ahead)
        if 2 * i < tiles:
            above = lax.ppermute(above, "tile", back)
        if i >= 3:
            total, steps, blocks = down(total, steps, blocks), [], []
        steps, blocks = steps + [-i], blocks + [below]
        if 2 * i < tiles:
            steps, blocks = steps + [i], blocks + [above]
    result = down(total, steps, blocks)
    back = lax.all_to_all(result, "tile", split_axis=0, concat_axis=0, tiled=True)
    return call(combine_kernel, "combine", bf16(rows, half_width), [VMEM] * 3, 4 * MIB)(back, to_core(back), table)


def local_gathered(tokens, routes, gates, w_gate, w_up, w_down):
    experts = lax.axis_size("expert")
    tile_count = lax.axis_size("tile")
    own_expert = lax.axis_index("expert")
    half_width = tokens.shape[1]
    tok_rows = tokens.shape[0]
    slot_count = max(2, tok_rows // 2)
    window_ids = lax.broadcasted_iota(jnp.int32, (1, 1, experts), 2)
    is_named = routes[:, :, None] == window_ids
    chosen = jnp.any(is_named, axis=1)
    weight = jnp.sum(jnp.where(is_named, gates[:, :, None], jnp.float32(0.0)), axis=1)
    position = jnp.cumsum(chosen.astype(jnp.int32), axis=0) - 1
    slot_ids = lax.broadcasted_iota(jnp.int32, (1, slot_count, 1), 1)
    dispatch = jnp.logical_and(chosen.T[:, None, :], position.T[:, None, :] == slot_ids)
    placing = dispatch.astype(jnp.bfloat16)
    outgoing = jnp.einsum(
        "ecr,rd->ecd", placing, tokens, preferred_element_type=jnp.float32
    ).astype(jnp.bfloat16)
    slot_weight = jnp.einsum("ecr,re->ec", dispatch.astype(jnp.float32), weight)
    everything = lax.all_gather(outgoing[None], ("expert", "tile"), axis=0, tiled=True)
    picked = lax.dynamic_slice_in_dim(everything, own_expert, 1, 1)[:, 0]
    picked = picked.reshape(experts, tile_count, slot_count, half_width)
    gathered = jnp.transpose(picked, (1, 2, 0, 3)).reshape(
        tile_count * slot_count, experts * half_width
    )
    gate_proj = jnp.dot(gathered, w_gate[0], preferred_element_type=jnp.float32)
    up_proj = jnp.dot(gathered, w_up[0], preferred_element_type=jnp.float32)
    hidden = (jax.nn.silu(gate_proj) * up_proj).astype(jnp.bfloat16)
    columns = w_down[0]
    summed = lax.dot_general(
        columns,
        lax.all_gather(hidden, "tile", axis=1, tiled=True),
        (((1,), (1,)), ((), ())),
        preferred_element_type=jnp.float32,
    )
    homeward = lax.all_to_all(summed, "tile", split_axis=1, concat_axis=0, tiled=True)
    returned = lax.all_to_all(homeward, "expert", split_axis=0, concat_axis=1, tiled=True)
    contribution = (slot_weight.reshape(1, experts * slot_count) * returned).astype(jnp.bfloat16)
    flat_places = placing.reshape(experts * slot_count, tok_rows)
    return jnp.einsum(
        "st,ds->td", flat_places, contribution, preferred_element_type=jnp.float32
    ).astype(jnp.bfloat16)


def solution(mesh):
    in_specs = (
        P(("group", "tile"), "expert"),
        P(("group", "tile"), None),
        P(("group", "tile"), None),
        P("expert", None, "tile"),
        P("expert", None, "tile"),
        P("expert", "tile", None),
    )
    out_specs = P(("group", "tile"), "expert")
    local = local_direct if mesh.shape["tile"] <= 8 else local_gathered
    return jax.shard_map(local, mesh=mesh, in_specs=in_specs, out_specs=out_specs, check_vma=False)
```

```python
import functools

import jax
import jax.numpy as jnp
from jax import lax
from jax.experimental import pallas as pl
from jax.experimental.pallas import tpu as pltpu
from jax.sharding import PartitionSpec as P

MIB = 1 << 20
SLOTS = 2
VMEM = pl.BlockSpec(memory_space=pltpu.VMEM)
ANY = pl.BlockSpec(memory_space=pl.ANY)


def in_vmem(x):
    return pltpu.with_memory_space_constraint(x, pltpu.VMEM)


def in_hbm(x):
    return pltpu.with_memory_space_constraint(x, pltpu.HBM)


def call(kernel, name, out, in_specs, limit, seconds=0.0, scratch=()):
    return pl.pallas_call(
        kernel,
        out_shape=out,
        in_specs=in_specs,
        out_specs=jax.tree.map(lambda _: VMEM, out),
        scratch_shapes=scratch,
        compiler_params=pltpu.CompilerParams(vmem_limit_bytes=limit),
        cost_estimate=pl.CostEstimate(flops=int(seconds*1e15), bytes_accessed=0, transcendentals=0),
        name=name,
    )


def slot_rows(routes_ref, e, rows):
    taken = jnp.int32(0)
    found = []
    for r in range(rows):
        named = jnp.logical_or(routes_ref[0, r] == e, routes_ref[1, r] == e)
        found.append((named, taken))
        taken = taken + named.astype(jnp.int32)
    return found


def dispatch_kernel(tokens_hbm, routes_hbm, gates_hbm, sends_ref, table_ref, tokens_ref, routes_ref, gates_ref, sems):
    copies = [
        pltpu.make_async_copy(routes_hbm, routes_ref, sems.at[0]),
        pltpu.make_async_copy(gates_hbm, gates_ref, sems.at[1]),
        pltpu.make_async_copy(tokens_hbm, tokens_ref, sems.at[2]),
    ]
    for copy in copies:
        copy.start()
    for copy in copies:
        copy.wait()
    tokens = tokens_ref[...].astype(jnp.float32)
    rows = tokens.shape[0]
    tiles = sends_ref.shape[0] // 2
    for e in range(2):
        found = slot_rows(routes_ref, e, rows)
        base = e * (1 + SLOTS)
        line = (1, table_ref.shape[2])
        for r in range(rows):
            weight = jnp.where(routes_ref[0, r] == e, gates_ref[0, r], 0.0)
            weight = weight + jnp.where(routes_ref[1, r] == e, gates_ref[1, r], 0.0)
            table_ref[base, r:r + 1, :] = jnp.full(line, weight, jnp.float32)
        slots = []
        for c in range(SLOTS):
            row = jnp.zeros((1, tokens.shape[1]), jnp.float32)
            for r, (named, slot) in enumerate(found):
                here = jnp.logical_and(named, slot == c).astype(jnp.float32)
                row = row + here * tokens[r:r + 1, :]
                table_ref[base + 1 + c, r:r + 1, :] = jnp.full(line, here, jnp.float32)
            slots.append(row)
        block = jnp.concatenate(slots, axis=0).astype(jnp.bfloat16)
        for t in range(tiles):
            sends_ref[e * tiles + t] = block


def merge_kernel(blocks_ref, rows_ref):
    rows_ref[...] = blocks_ref[...].reshape(rows_ref.shape)


def project(rows_ref, w_ref, columns):
    slots, half = rows_ref.shape[0] // 2, rows_ref.shape[1]
    total = jnp.dot(rows_ref[:slots, :], w_ref[0, :half, columns], preferred_element_type=jnp.float32)
    return total + jnp.dot(rows_ref[slots:, :], w_ref[0, half:, columns], preferred_element_type=jnp.float32)


def over_columns(width, body):
    tile = 256

    def step(i, carry):
        body(pl.ds(pl.multiple_of(i * tile, tile), tile))
        return carry

    lax.fori_loop(0, width // tile, step, 0)


def gate_kernel(rows_ref, w_ref, out_ref):
    def body(columns):
        out_ref[:, columns] = project(rows_ref, w_ref, columns)

    over_columns(out_ref.shape[1], body)


def hidden_kernel(rows_ref, w_ref, gate_ref, hidden_ref):
    def body(columns):
        up = project(rows_ref, w_ref, columns)
        gate = gate_ref[:, columns]
        hidden_ref[:, columns] = (gate / (1.0 + jnp.exp(-gate)) * up).astype(jnp.bfloat16)

    over_columns(hidden_ref.shape[1], body)


def down_kernel(steps, order, first, last, *refs):
    n = len(steps)
    blocks, w_ref, rest = refs[:n], refs[n], refs[n + 1:]
    out_ref = rest[-1]
    me = lax.axis_index("tile")
    slots, width = blocks[0].shape
    high = me // (len(order) // 2)
    part = 256
    starts = []
    for step in steps:
        tile = jnp.int32(0)
        for i, t in enumerate(order):
            tile = jnp.where(me == t, order[(i + step) % len(order)], tile)
        starts.append(pl.multiple_of(tile * width, width))
    for i in range(w_ref.shape[1] // part):
        rows = slice(i * part, (i + 1) * part)
        total = None if first else rest[0][rows, :]
        for block, start in zip(blocks, starts):
            term = lax.dot_general(
                w_ref[0, rows, pl.ds(start, width)], block[...], (((1,), (1,)), ((), ())),
                preferred_element_type=jnp.float32,
            )
            total = term if total is None else total + term
        if not last:
            out_ref[rows, :] = total
        else:
            total = total.T
            keep_ref, send_ref = rest[-2:]
            for t in range(keep_ref.shape[0]):
                low_rows = total[t * SLOTS:(t + 1) * SLOTS, :]
                high_rows = total[slots // 2 + t * SLOTS:slots // 2 + (t + 1) * SLOTS, :]
                keep_ref[t, :, rows] = jnp.where(high == 0, low_rows, high_rows)
                send_ref[t, :, rows] = jnp.where(high == 0, high_rows, low_rows)


def core_kernel(kept_ref, got_ref, keep_ref, send_ref):
    swap = lax.axis_index("tile") // 4 != lax.axis_index("expert")
    kept, got = kept_ref[...], got_ref[...]
    keep_ref[...] = jnp.where(swap, got, kept)
    send_ref[...] = jnp.where(swap, kept, got)


def split_kernel(bit, kept_ref, got_ref, keep_ref, send_ref):
    mine = (lax.axis_index("tile") // bit) % 2
    for i, ref in enumerate((kept_ref, got_ref)):
        n = ref.shape[0] // 2
        for j in range(n):
            low, high = ref[j], ref[n + j]
            keep_ref[j, i] = jnp.where(mine == 0, low, high)
            send_ref[j, i] = jnp.where(mine == 0, high, low)


def combine_kernel(kept_ref, got_ref, table_ref, out_ref):
    me, mine = lax.axis_index("tile"), lax.axis_index("expert")
    features = kept_ref.shape[-1]
    weight = [table_ref[e * (1 + SLOTS)][:, :1] for e in range(2)]
    inside = [[table_ref[e * (1 + SLOTS) + 1 + c][:, :1] for c in range(SLOTS)] for e in range(2)]
    for i in range(4):
        far = (me // 2) % 2 ^ i // 2
        kept, got = kept_ref[0, far], got_ref[0, far]
        parts = jnp.where(me % 2 == i % 2, kept, got)
        mixed = jnp.zeros((out_ref.shape[0], features), jnp.float32)
        for e in range(2):
            both = jnp.where(mine == e, parts[0], parts[1])
            for c in range(SLOTS):
                value = (weight[e] * both[c:c + 1]).astype(jnp.bfloat16).astype(jnp.float32)
                mixed = mixed + jnp.where(inside[e][c] != 0.0, value, 0.0)
        out_ref[:, i * features:(i + 1) * features] = mixed.astype(jnp.bfloat16)


def local_direct(tokens, routes, gates, w_gate, w_up, w_down):
    tiles = lax.axis_size("tile")
    rows, half_width = tokens.shape
    width, features = w_gate.shape[2], w_down.shape[1]
    slots = tiles * SLOTS
    routes, gates = routes.T, gates.T

    def swap(x, bit):
        return lax.ppermute(x, "tile", [(t, t ^ bit) for t in range(tiles)])

    def to_core(x):
        return lax.ppermute(x, "expert", [(0, 1), (1, 0)])

    f32 = lambda *shape: jax.ShapeDtypeStruct(shape, jnp.float32)
    bf16 = lambda *shape: jax.ShapeDtypeStruct(shape, jnp.bfloat16)
    sends, table = call(
        dispatch_kernel, "dispatch",
        (bf16(2 * tiles, SLOTS, half_width), f32(2 * (1 + SLOTS), rows, 128)), [ANY] * 3, 4 * MIB, 600e-6,
        [
            pltpu.VMEM((rows, half_width), jnp.bfloat16),
            pltpu.SMEM((2, rows), jnp.int32),
            pltpu.SMEM((2, rows), jnp.float32),
            pltpu.SemaphoreType.DMA((3,)),
        ],
    )(in_hbm(tokens), in_hbm(routes), in_hbm(gates))
    blocks = lax.all_to_all(sends, ("expert", "tile"), split_axis=0, concat_axis=0, tiled=True)
    x = call(merge_kernel, "merge", bf16(2 * slots, half_width), [VMEM], 4 * MIB, 0e-6)(blocks)
    gate = call(gate_kernel, "gate", f32(slots, width), [VMEM] * 2, 4 * MIB, 0e-6)(x, in_vmem(w_gate))
    hidden = call(hidden_kernel, "hidden", bf16(slots, width), [VMEM] * 3, 4 * MIB, 200e-6)(x, in_vmem(w_up), gate)
    order = list(range(0, tiles, 2)) + list(range(tiles - 1, 0, -2))
    ahead = [(t, order[(i + 1) % tiles]) for i, t in enumerate(order)]
    behind = [(t, order[i - 1]) for i, t in enumerate(order)]

    def down(total, steps, blocks):
        first, last = total is None, -(tiles // 2) in steps
        out = (f32(tiles // 2, SLOTS, features),) * 2 if last else f32(features, slots)
        return call(
            functools.partial(down_kernel, steps, order, first, last), "down", out,
            [VMEM] * (len(blocks) + 2 - first), 8 * MIB, 0e-6,
        )(*blocks, in_vmem(w_down), *(() if first else (total,)))

    below, above = hidden, hidden
    total, steps, blocks = None, [0], [hidden]
    for i in range(1, tiles // 2 + 1):
        below = lax.ppermute(below, "tile", ahead)
        if 2 * i < tiles:
            above = lax.ppermute(above, "tile", behind)
        if i >= 2:
            total, steps, blocks = down(total, steps, blocks), [], []
            total, below, above = lax.optimization_barrier((total, below, above))
        steps, blocks = steps + [-i], blocks + [below]
        if 2 * i < tiles:
            steps, blocks = steps + [i], blocks + [above]
    result = down(total, steps, blocks)
    keep, send = result
    keep, send = call(core_kernel, "core", (f32(*keep.shape),) * 2, [VMEM] * 2, 4 * MIB)(keep, swap(send, 4))
    got = to_core(send)
    keep, send = call(
        functools.partial(split_kernel, 2), "split", (f32(2, 2, SLOTS, features),) * 2, [VMEM] * 2, 4 * MIB
    )(keep, got)
    got = swap(send, 2)
    keep, send = call(
        functools.partial(split_kernel, 1), "split", (f32(1, 2, 2, SLOTS, features),) * 2, [VMEM] * 2, 4 * MIB
    )(keep, got)
    got = swap(send, 1)
    return call(combine_kernel, "combine", bf16(rows, half_width), [VMEM] * 3, 4 * MIB)(keep, got, table)


def local_gathered(tokens, routes, gates, w_gate, w_up, w_down):
    experts = lax.axis_size("expert")
    tile_count = lax.axis_size("tile")
    own_expert = lax.axis_index("expert")
    half_width = tokens.shape[1]
    tok_rows = tokens.shape[0]
    slot_count = max(2, tok_rows // 2)
    window_ids = lax.broadcasted_iota(jnp.int32, (1, 1, experts), 2)
    is_named = routes[:, :, None] == window_ids
    chosen = jnp.any(is_named, axis=1)
    weight = jnp.sum(jnp.where(is_named, gates[:, :, None], jnp.float32(0.0)), axis=1)
    position = jnp.cumsum(chosen.astype(jnp.int32), axis=0) - 1
    slot_ids = lax.broadcasted_iota(jnp.int32, (1, slot_count, 1), 1)
    dispatch = jnp.logical_and(chosen.T[:, None, :], position.T[:, None, :] == slot_ids)
    placing = dispatch.astype(jnp.bfloat16)
    outgoing = jnp.einsum(
        "ecr,rd->ecd", placing, tokens, preferred_element_type=jnp.float32
    ).astype(jnp.bfloat16)
    slot_weight = jnp.einsum("ecr,re->ec", dispatch.astype(jnp.float32), weight)
    everything = lax.all_gather(outgoing[None], ("expert", "tile"), axis=0, tiled=True)
    picked = lax.dynamic_slice_in_dim(everything, own_expert, 1, 1)[:, 0]
    picked = picked.reshape(experts, tile_count, slot_count, half_width)
    gathered = jnp.transpose(picked, (1, 2, 0, 3)).reshape(
        tile_count * slot_count, experts * half_width
    )
    gate_proj = jnp.dot(gathered, w_gate[0], preferred_element_type=jnp.float32)
    up_proj = jnp.dot(gathered, w_up[0], preferred_element_type=jnp.float32)
    hidden = (jax.nn.silu(gate_proj) * up_proj).astype(jnp.bfloat16)
    columns = w_down[0]
    summed = lax.dot_general(
        columns,
        lax.all_gather(hidden, "tile", axis=1, tiled=True),
        (((1,), (1,)), ((), ())),
        preferred_element_type=jnp.float32,
    )
    homeward = lax.all_to_all(summed, "tile", split_axis=1, concat_axis=0, tiled=True)
    returned = lax.all_to_all(homeward, "expert", split_axis=0, concat_axis=1, tiled=True)
    contribution = (slot_weight.reshape(1, experts * slot_count) * returned).astype(jnp.bfloat16)
    flat_places = placing.reshape(experts * slot_count, tok_rows)
    return jnp.einsum(
        "st,ds->td", flat_places, contribution, preferred_element_type=jnp.float32
    ).astype(jnp.bfloat16)


def solution(mesh):
    in_specs = (
        P(("group", "tile"), "expert"),
        P(("group", "tile"), None),
        P(("group", "tile"), None),
        P("expert", None, "tile"),
        P("expert", None, "tile"),
        P("expert", "tile", None),
    )
    out_specs = P(("group", "tile"), "expert")
    local = local_direct if mesh.shape["tile"] == 8 else local_gathered
    return jax.shard_map(local, mesh=mesh, in_specs=in_specs, out_specs=out_specs, check_vma=False)
```

```python
import functools

import jax
import jax.numpy as jnp
from jax import lax
from jax.experimental import pallas as pl
from jax.experimental.pallas import tpu as pltpu
from jax.sharding import PartitionSpec as P

MIB = 1 << 20
SLOTS = 2
VMEM = pl.BlockSpec(memory_space=pltpu.VMEM)
ANY = pl.BlockSpec(memory_space=pl.ANY)


def in_vmem(x):
    return pltpu.with_memory_space_constraint(x, pltpu.VMEM)


def in_hbm(x):
    return pltpu.with_memory_space_constraint(x, pltpu.HBM)


def call(kernel, name, out, in_specs, limit, seconds=0.0, scratch=()):
    return pl.pallas_call(
        kernel,
        out_shape=out,
        in_specs=in_specs,
        out_specs=jax.tree.map(lambda _: VMEM, out),
        scratch_shapes=scratch,
        compiler_params=pltpu.CompilerParams(vmem_limit_bytes=limit),
        cost_estimate=pl.CostEstimate(flops=int(seconds*1e15), bytes_accessed=0, transcendentals=0),
        name=name,
    )


def slot_rows(routes_ref, e, rows):
    taken = jnp.int32(0)
    found = []
    for r in range(rows):
        named = jnp.logical_or(routes_ref[0, r] == e, routes_ref[1, r] == e)
        found.append((named, taken))
        taken = taken + named.astype(jnp.int32)
    return found


def dispatch_kernel(tokens_hbm, routes_hbm, gates_hbm, sends_ref, table_ref, tokens_ref, routes_ref, gates_ref, sems):
    copies = [
        pltpu.make_async_copy(routes_hbm, routes_ref, sems.at[0]),
        pltpu.make_async_copy(gates_hbm, gates_ref, sems.at[1]),
        pltpu.make_async_copy(tokens_hbm, tokens_ref, sems.at[2]),
    ]
    for copy in copies:
        copy.start()
    for copy in copies:
        copy.wait()
    tokens = tokens_ref[...].astype(jnp.float32)
    rows = tokens.shape[0]
    tiles = sends_ref.shape[0] // 2
    for e in range(2):
        found = slot_rows(routes_ref, e, rows)
        base = e * (1 + SLOTS)
        line = (1, table_ref.shape[2])
        for r in range(rows):
            weight = jnp.where(routes_ref[0, r] == e, gates_ref[0, r], 0.0)
            weight = weight + jnp.where(routes_ref[1, r] == e, gates_ref[1, r], 0.0)
            table_ref[base, r:r + 1, :] = jnp.full(line, weight, jnp.float32)
        slots = []
        for c in range(SLOTS):
            row = jnp.zeros((1, tokens.shape[1]), jnp.float32)
            for r, (named, slot) in enumerate(found):
                here = jnp.logical_and(named, slot == c).astype(jnp.float32)
                row = row + here * tokens[r:r + 1, :]
                table_ref[base + 1 + c, r:r + 1, :] = jnp.full(line, here, jnp.float32)
            slots.append(row)
        block = jnp.concatenate(slots, axis=0).astype(jnp.bfloat16)
        for t in range(tiles):
            sends_ref[e * tiles + t] = block


def merge_kernel(blocks_ref, rows_ref):
    rows_ref[...] = blocks_ref[...].reshape(rows_ref.shape)


def project(rows_ref, w_ref, columns):
    slots, half = rows_ref.shape[0] // 2, rows_ref.shape[1]
    total = jnp.dot(rows_ref[:slots, :], w_ref[0, :half, columns], preferred_element_type=jnp.float32)
    return total + jnp.dot(rows_ref[slots:, :], w_ref[0, half:, columns], preferred_element_type=jnp.float32)


def over_columns(width, body):
    tile = 256

    def step(i, carry):
        body(pl.ds(pl.multiple_of(i * tile, tile), tile))
        return carry

    lax.fori_loop(0, width // tile, step, 0, unroll=4)


def gate_kernel(rows_ref, w_ref, out_ref):
    def body(columns):
        out_ref[:, columns] = project(rows_ref, w_ref, columns)

    over_columns(out_ref.shape[1], body)


def hidden_kernel(rows_ref, w_ref, gate_ref, hidden_ref):
    def body(columns):
        up = project(rows_ref, w_ref, columns)
        gate = gate_ref[:, columns]
        hidden_ref[:, columns] = (gate / (1.0 + jnp.exp(-gate)) * up).astype(jnp.bfloat16)

    over_columns(hidden_ref.shape[1], body)


def down_kernel(steps, order, first, last, *refs):
    n = len(steps)
    blocks, w_ref, rest = refs[:n], refs[n], refs[n + 1:]
    out_ref = rest[-1]
    me = lax.axis_index("tile")
    slots, width = blocks[0].shape
    part = 256
    starts = []
    for step in steps:
        tile = jnp.int32(0)
        for i, t in enumerate(order):
            tile = jnp.where(me == t, order[(i + step) % len(order)], tile)
        starts.append(pl.multiple_of(tile * width, width))
    for i in range(w_ref.shape[1] // part):
        rows = slice(i * part, (i + 1) * part)
        total = None if first else rest[0][rows, :]
        for block, start in zip(blocks, starts):
            term = lax.dot_general(
                w_ref[0, rows, pl.ds(start, width)], block[...], (((1,), (1,)), ((), ())),
                preferred_element_type=jnp.float32,
            )
            total = term if total is None else total + term
        if not last:
            out_ref[rows, :] = total
        else:
            total = total.T
            for t in range(out_ref.shape[0]):
                out_ref[t, :, rows] = total[t * SLOTS:(t + 1) * SLOTS, :]


def combine_kernel(own_ref, other_ref, table_ref, out_ref):
    mine = lax.axis_index("expert")
    halves, features = own_ref.shape[0] // 2, own_ref.shape[2]
    weight = [table_ref[e * (1 + SLOTS)][:, :1] for e in range(2)]
    inside = [[table_ref[e * (1 + SLOTS) + 1 + c][:, :1] for c in range(SLOTS)] for e in range(2)]
    for i in range(halves):
        own, other = own_ref[mine * halves + i], other_ref[mine * halves + i]
        mixed = jnp.zeros((out_ref.shape[0], features), jnp.float32)
        for e in range(2):
            both = jnp.where(mine == e, own, other)
            for c in range(SLOTS):
                value = (weight[e] * both[c:c + 1]).astype(jnp.bfloat16).astype(jnp.float32)
                mixed = mixed + jnp.where(inside[e][c] != 0.0, value, 0.0)
        out_ref[:, i * features:(i + 1) * features] = mixed.astype(jnp.bfloat16)


def local_direct(tokens, routes, gates, w_gate, w_up, w_down):
    tiles = lax.axis_size("tile")
    rows, half_width = tokens.shape
    width, features = w_gate.shape[2], w_down.shape[1]
    slots = tiles * SLOTS
    routes, gates = routes.T, gates.T

    def to_core(x):
        return lax.ppermute(x, "expert", [(0, 1), (1, 0)])

    f32 = lambda *shape: jax.ShapeDtypeStruct(shape, jnp.float32)
    bf16 = lambda *shape: jax.ShapeDtypeStruct(shape, jnp.bfloat16)
    sends, table = call(
        dispatch_kernel, "dispatch",
        (bf16(2 * tiles, SLOTS, half_width), f32(2 * (1 + SLOTS), rows, 128)), [ANY] * 3, 4 * MIB, 600e-6,
        [
            pltpu.VMEM((rows, half_width), jnp.bfloat16),
            pltpu.SMEM((2, rows), jnp.int32),
            pltpu.SMEM((2, rows), jnp.float32),
            pltpu.SemaphoreType.DMA((3,)),
        ],
    )(in_hbm(tokens), in_hbm(routes), in_hbm(gates))
    blocks = lax.all_to_all(sends, ("expert", "tile"), split_axis=0, concat_axis=0, tiled=True)
    x = call(merge_kernel, "merge", bf16(2 * slots, half_width), [VMEM], 4 * MIB, 0e-6)(blocks)
    gate = call(gate_kernel, "gate", f32(slots, width), [VMEM] * 2, 4 * MIB, 0e-6)(x, in_vmem(w_gate))
    hidden = call(hidden_kernel, "hidden", bf16(slots, width), [VMEM] * 3, 4 * MIB, 200e-6)(x, in_vmem(w_up), gate)
    order = list(range(0, tiles, 2)) + list(range(tiles - 1, 0, -2))
    ahead = [(t, order[(i + 1) % tiles]) for i, t in enumerate(order)]
    behind = [(t, order[i - 1]) for i, t in enumerate(order)]

    def down(total, steps, blocks):
        first, last = total is None, -(tiles // 2) in steps
        out = f32(tiles, SLOTS, features) if last else f32(features, slots)
        return call(
            functools.partial(down_kernel, steps, order, first, last), "down", out,
            [VMEM] * (len(blocks) + 2 - first), 8 * MIB, 0e-6,
        )(*blocks, in_vmem(w_down), *(() if first else (total,)))

    below, above = hidden, hidden
    total, steps, blocks = None, [0], [hidden]
    for i in range(1, tiles // 2 + 1):
        below = lax.ppermute(below, "tile", ahead)
        if 2 * i < tiles:
            above = lax.ppermute(above, "tile", behind)
        if i >= 2:
            total, steps, blocks = down(total, steps, blocks), [], []
            total, below, above = lax.optimization_barrier((total, below, above))
        steps, blocks = steps + [-i], blocks + [below]
        if 2 * i < tiles:
            steps, blocks = steps + [i], blocks + [above]
    result = down(total, steps, blocks)
    back = lax.all_to_all(result, "tile", split_axis=0, concat_axis=0, tiled=True)
    return call(combine_kernel, "combine", bf16(rows, half_width), [VMEM] * 3, 4 * MIB)(back, to_core(back), table)


def local_gathered(tokens, routes, gates, w_gate, w_up, w_down):
    experts = lax.axis_size("expert")
    tile_count = lax.axis_size("tile")
    own_expert = lax.axis_index("expert")
    half_width = tokens.shape[1]
    tok_rows = tokens.shape[0]
    slot_count = max(2, tok_rows // 2)
    window_ids = lax.broadcasted_iota(jnp.int32, (1, 1, experts), 2)
    is_named = routes[:, :, None] == window_ids
    chosen = jnp.any(is_named, axis=1)
    weight = jnp.sum(jnp.where(is_named, gates[:, :, None], jnp.float32(0.0)), axis=1)
    position = jnp.cumsum(chosen.astype(jnp.int32), axis=0) - 1
    slot_ids = lax.broadcasted_iota(jnp.int32, (1, slot_count, 1), 1)
    dispatch = jnp.logical_and(chosen.T[:, None, :], position.T[:, None, :] == slot_ids)
    placing = dispatch.astype(jnp.bfloat16)
    outgoing = jnp.einsum(
        "ecr,rd->ecd", placing, tokens, preferred_element_type=jnp.float32
    ).astype(jnp.bfloat16)
    slot_weight = jnp.einsum("ecr,re->ec", dispatch.astype(jnp.float32), weight)
    everything = lax.all_gather(outgoing[None], ("expert", "tile"), axis=0, tiled=True)
    picked = lax.dynamic_slice_in_dim(everything, own_expert, 1, 1)[:, 0]
    picked = picked.reshape(experts, tile_count, slot_count, half_width)
    gathered = jnp.transpose(picked, (1, 2, 0, 3)).reshape(
        tile_count * slot_count, experts * half_width
    )
    gate_proj = jnp.dot(gathered, w_gate[0], preferred_element_type=jnp.float32)
    up_proj = jnp.dot(gathered, w_up[0], preferred_element_type=jnp.float32)
    hidden = (jax.nn.silu(gate_proj) * up_proj).astype(jnp.bfloat16)
    columns = w_down[0]
    summed = lax.dot_general(
        columns,
        lax.all_gather(hidden, "tile", axis=1, tiled=True),
        (((1,), (1,)), ((), ())),
        preferred_element_type=jnp.float32,
    )
    homeward = lax.all_to_all(summed, "tile", split_axis=1, concat_axis=0, tiled=True)
    returned = lax.all_to_all(homeward, "expert", split_axis=0, concat_axis=1, tiled=True)
    contribution = (slot_weight.reshape(1, experts * slot_count) * returned).astype(jnp.bfloat16)
    flat_places = placing.reshape(experts * slot_count, tok_rows)
    return jnp.einsum(
        "st,ds->td", flat_places, contribution, preferred_element_type=jnp.float32
    ).astype(jnp.bfloat16)


def solution(mesh):
    in_specs = (
        P(("group", "tile"), "expert"),
        P(("group", "tile"), None),
        P(("group", "tile"), None),
        P("expert", None, "tile"),
        P("expert", None, "tile"),
        P("expert", "tile", None),
    )
    out_specs = P(("group", "tile"), "expert")
    local = local_direct if mesh.shape["tile"] == 8 else local_gathered
    return jax.shard_map(local, mesh=mesh, in_specs=in_specs, out_specs=out_specs, check_vma=False)
```

```python
import functools

import jax
import jax.numpy as jnp
from jax import lax
from jax.experimental import pallas as pl
from jax.experimental.pallas import tpu as pltpu
from jax.sharding import PartitionSpec as P

MIB = 1 << 20
SLOTS = 2
VMEM = pl.BlockSpec(memory_space=pltpu.VMEM)
ANY = pl.BlockSpec(memory_space=pl.ANY)


def in_vmem(x):
    return pltpu.with_memory_space_constraint(x, pltpu.VMEM)


def in_hbm(x):
    return pltpu.with_memory_space_constraint(x, pltpu.HBM)


def call(kernel, name, out, in_specs, limit, seconds=0.0, scratch=()):
    return pl.pallas_call(
        kernel,
        out_shape=out,
        in_specs=in_specs,
        out_specs=jax.tree.map(lambda _: VMEM, out),
        scratch_shapes=scratch,
        compiler_params=pltpu.CompilerParams(vmem_limit_bytes=limit),
        cost_estimate=pl.CostEstimate(flops=int(seconds*1e15), bytes_accessed=0, transcendentals=0),
        name=name,
    )


def slot_rows(routes_ref, e, rows):
    taken = jnp.int32(0)
    found = []
    for r in range(rows):
        named = jnp.logical_or(routes_ref[0, r] == e, routes_ref[1, r] == e)
        found.append((named, taken))
        taken = taken + named.astype(jnp.int32)
    return found


def dispatch_kernel(tokens_hbm, routes_hbm, gates_hbm, sends_ref, table_ref, tokens_ref, routes_ref, gates_ref, sems):
    copies = [
        pltpu.make_async_copy(routes_hbm, routes_ref, sems.at[0]),
        pltpu.make_async_copy(gates_hbm, gates_ref, sems.at[1]),
        pltpu.make_async_copy(tokens_hbm, tokens_ref, sems.at[2]),
    ]
    for copy in copies:
        copy.start()
    for copy in copies:
        copy.wait()
    tokens = tokens_ref[...].astype(jnp.float32)
    rows = tokens.shape[0]
    tiles = sends_ref.shape[0] // 2
    for e in range(2):
        found = slot_rows(routes_ref, e, rows)
        base = e * (1 + SLOTS)
        line = (1, table_ref.shape[2])
        for r in range(rows):
            weight = jnp.where(routes_ref[0, r] == e, gates_ref[0, r], 0.0)
            weight = weight + jnp.where(routes_ref[1, r] == e, gates_ref[1, r], 0.0)
            table_ref[base, r:r + 1, :] = jnp.full(line, weight, jnp.float32)
        slots = []
        for c in range(SLOTS):
            row = jnp.zeros((1, tokens.shape[1]), jnp.float32)
            for r, (named, slot) in enumerate(found):
                here = jnp.logical_and(named, slot == c).astype(jnp.float32)
                row = row + here * tokens[r:r + 1, :]
                table_ref[base + 1 + c, r:r + 1, :] = jnp.full(line, here, jnp.float32)
            slots.append(row)
        block = jnp.concatenate(slots, axis=0).astype(jnp.bfloat16)
        for t in range(tiles):
            sends_ref[e * tiles + t] = block


def merge_kernel(blocks_ref, rows_ref):
    rows_ref[...] = blocks_ref[...].reshape(rows_ref.shape)


def project(rows_ref, w_ref, columns):
    slots, half = rows_ref.shape[0] // 2, rows_ref.shape[1]
    total = jnp.dot(rows_ref[:slots, :], w_ref[0, :half, columns], preferred_element_type=jnp.float32)
    return total + jnp.dot(rows_ref[slots:, :], w_ref[0, half:, columns], preferred_element_type=jnp.float32)


def over_columns(width, body):
    tile = 256

    def step(i, carry):
        body(pl.ds(pl.multiple_of(i * tile, tile), tile))
        return carry

    lax.fori_loop(0, width // tile, step, 0, unroll=8)


def gate_kernel(rows_ref, w_ref, out_ref):
    def body(columns):
        out_ref[:, columns] = project(rows_ref, w_ref, columns)

    over_columns(out_ref.shape[1], body)


def hidden_kernel(rows_ref, w_ref, gate_ref, hidden_ref):
    def body(columns):
        up = project(rows_ref, w_ref, columns)
        gate = gate_ref[:, columns]
        hidden_ref[:, columns] = (gate / (1.0 + jnp.exp(-gate)) * up).astype(jnp.bfloat16)

    over_columns(hidden_ref.shape[1], body)


def down_kernel(steps, first, last, *refs):
    n = len(steps)
    blocks, w_ref, rest = refs[:n], refs[n], refs[n + 1:]
    out_ref = rest[-1]
    me = lax.axis_index("tile")
    slots, width = blocks[0].shape
    part = 256
    starts = [pl.multiple_of((me ^ step) * width, width) for step in steps]
    for i in range(w_ref.shape[1] // part):
        rows = slice(i * part, (i + 1) * part)
        total = None if first else rest[0][rows, :]
        for block, start in zip(blocks, starts):
            term = lax.dot_general(
                w_ref[0, rows, pl.ds(start, width)], block[...], (((1,), (1,)), ((), ())),
                preferred_element_type=jnp.float32,
            )
            total = term if total is None else total + term
        if not last:
            out_ref[rows, :] = total
        else:
            total = total.T
            for t in range(out_ref.shape[0]):
                out_ref[t, :, rows] = total[t * SLOTS:(t + 1) * SLOTS, :]


def combine_kernel(own_ref, other_ref, table_ref, out_ref):
    mine = lax.axis_index("expert")
    halves, features = own_ref.shape[0] // 2, own_ref.shape[2]
    weight = [table_ref[e * (1 + SLOTS)][:, :1] for e in range(2)]
    inside = [[table_ref[e * (1 + SLOTS) + 1 + c][:, :1] for c in range(SLOTS)] for e in range(2)]
    for i in range(halves):
        own, other = own_ref[mine * halves + i], other_ref[mine * halves + i]
        mixed = jnp.zeros((out_ref.shape[0], features), jnp.float32)
        for e in range(2):
            both = jnp.where(mine == e, own, other)
            for c in range(SLOTS):
                value = (weight[e] * both[c:c + 1]).astype(jnp.bfloat16).astype(jnp.float32)
                mixed = mixed + jnp.where(inside[e][c] != 0.0, value, 0.0)
        out_ref[:, i * features:(i + 1) * features] = mixed.astype(jnp.bfloat16)


def local_direct(tokens, routes, gates, w_gate, w_up, w_down):
    tiles = lax.axis_size("tile")
    rows, half_width = tokens.shape
    width, features = w_gate.shape[2], w_down.shape[1]
    slots = tiles * SLOTS
    routes, gates = routes.T, gates.T

    def to_core(x):
        return lax.ppermute(x, "expert", [(0, 1), (1, 0)])

    f32 = lambda *shape: jax.ShapeDtypeStruct(shape, jnp.float32)
    bf16 = lambda *shape: jax.ShapeDtypeStruct(shape, jnp.bfloat16)
    sends, table = call(
        dispatch_kernel, "dispatch",
        (bf16(2 * tiles, SLOTS, half_width), f32(2 * (1 + SLOTS), rows, 128)), [ANY] * 3, 4 * MIB, 600e-6,
        [
            pltpu.VMEM((rows, half_width), jnp.bfloat16),
            pltpu.SMEM((2, rows), jnp.int32),
            pltpu.SMEM((2, rows), jnp.float32),
            pltpu.SemaphoreType.DMA((3,)),
        ],
    )(in_hbm(tokens), in_hbm(routes), in_hbm(gates))
    blocks = lax.all_to_all(sends, ("expert", "tile"), split_axis=0, concat_axis=0, tiled=True)
    x = call(merge_kernel, "merge", bf16(2 * slots, half_width), [VMEM], 4 * MIB, 0e-6)(blocks)
    gate = call(gate_kernel, "gate", f32(slots, width), [VMEM] * 2, 4 * MIB, 0e-6)(x, in_vmem(w_gate))
    hidden = call(hidden_kernel, "hidden", bf16(slots, width), [VMEM] * 3, 4 * MIB, 200e-6)(x, in_vmem(w_up), gate)
    def down(total, steps, blocks, last):
        first = total is None
        out = f32(tiles, SLOTS, features) if last else f32(features, slots)
        return call(
            functools.partial(down_kernel, steps, first, last), "down", out,
            [VMEM] * (len(blocks) + 2 - first), 8 * MIB, 0e-6,
        )(*blocks, in_vmem(w_down), *(() if first else (total,)))

    far_first = range(tiles - 1, 0, -1)
    blocks = [(0, hidden)] + [
        (k, lax.ppermute(hidden, "tile", [(t, t ^ k) for t in range(tiles)])) for k in far_first]
    total = None
    for first, last in ((0, 4), (4, 6), (6, 8)):
        part = blocks[first:last]
        total = down(total, [k for k, _ in part], [block for _, block in part], last == tiles)
    result = total
    back = lax.all_to_all(result, "tile", split_axis=0, concat_axis=0, tiled=True)
    return call(combine_kernel, "combine", bf16(rows, half_width), [VMEM] * 3, 4 * MIB)(back, to_core(back), table)


def local_gathered(tokens, routes, gates, w_gate, w_up, w_down):
    experts = lax.axis_size("expert")
    tile_count = lax.axis_size("tile")
    own_expert = lax.axis_index("expert")
    half_width = tokens.shape[1]
    tok_rows = tokens.shape[0]
    slot_count = max(2, tok_rows // 2)
    window_ids = lax.broadcasted_iota(jnp.int32, (1, 1, experts), 2)
    is_named = routes[:, :, None] == window_ids
    chosen = jnp.any(is_named, axis=1)
    weight = jnp.sum(jnp.where(is_named, gates[:, :, None], jnp.float32(0.0)), axis=1)
    position = jnp.cumsum(chosen.astype(jnp.int32), axis=0) - 1
    slot_ids = lax.broadcasted_iota(jnp.int32, (1, slot_count, 1), 1)
    dispatch = jnp.logical_and(chosen.T[:, None, :], position.T[:, None, :] == slot_ids)
    placing = dispatch.astype(jnp.bfloat16)
    outgoing = jnp.einsum(
        "ecr,rd->ecd", placing, tokens, preferred_element_type=jnp.float32
    ).astype(jnp.bfloat16)
    slot_weight = jnp.einsum("ecr,re->ec", dispatch.astype(jnp.float32), weight)
    everything = lax.all_gather(outgoing[None], ("expert", "tile"), axis=0, tiled=True)
    picked = lax.dynamic_slice_in_dim(everything, own_expert, 1, 1)[:, 0]
    picked = picked.reshape(experts, tile_count, slot_count, half_width)
    gathered = jnp.transpose(picked, (1, 2, 0, 3)).reshape(
        tile_count * slot_count, experts * half_width
    )
    gate_proj = jnp.dot(gathered, w_gate[0], preferred_element_type=jnp.float32)
    up_proj = jnp.dot(gathered, w_up[0], preferred_element_type=jnp.float32)
    hidden = (jax.nn.silu(gate_proj) * up_proj).astype(jnp.bfloat16)
    columns = w_down[0]
    summed = lax.dot_general(
        columns,
        lax.all_gather(hidden, "tile", axis=1, tiled=True),
        (((1,), (1,)), ((), ())),
        preferred_element_type=jnp.float32,
    )
    homeward = lax.all_to_all(summed, "tile", split_axis=1, concat_axis=0, tiled=True)
    returned = lax.all_to_all(homeward, "expert", split_axis=0, concat_axis=1, tiled=True)
    contribution = (slot_weight.reshape(1, experts * slot_count) * returned).astype(jnp.bfloat16)
    flat_places = placing.reshape(experts * slot_count, tok_rows)
    return jnp.einsum(
        "st,ds->td", flat_places, contribution, preferred_element_type=jnp.float32
    ).astype(jnp.bfloat16)


def solution(mesh):
    in_specs = (
        P(("group", "tile"), "expert"),
        P(("group", "tile"), None),
        P(("group", "tile"), None),
        P("expert", None, "tile"),
        P("expert", None, "tile"),
        P("expert", "tile", None),
    )
    out_specs = P(("group", "tile"), "expert")
    local = local_direct if mesh.shape["tile"] == 8 else local_gathered
    return jax.shard_map(local, mesh=mesh, in_specs=in_specs, out_specs=out_specs, check_vma=False)
```

```python
import functools

import jax
import jax.numpy as jnp
from jax import lax
from jax.experimental import pallas as pl
from jax.experimental.pallas import tpu as pltpu
from jax.sharding import PartitionSpec as P

MIB = 1 << 20
SLOTS = 2
VMEM = pl.BlockSpec(memory_space=pltpu.VMEM)
ANY = pl.BlockSpec(memory_space=pl.ANY)


def in_vmem(x):
    return pltpu.with_memory_space_constraint(x, pltpu.VMEM)


def in_hbm(x):
    return pltpu.with_memory_space_constraint(x, pltpu.HBM)


def call(kernel, name, out, in_specs, limit, seconds=0.0, scratch=()):
    return pl.pallas_call(
        kernel,
        out_shape=out,
        in_specs=in_specs,
        out_specs=jax.tree.map(lambda _: VMEM, out),
        scratch_shapes=scratch,
        compiler_params=pltpu.CompilerParams(vmem_limit_bytes=limit),
        cost_estimate=pl.CostEstimate(flops=int(seconds*1e15), bytes_accessed=0, transcendentals=0),
        name=name,
    )


def slot_rows(routes_ref, e, rows):
    taken = jnp.int32(0)
    found = []
    for r in range(rows):
        named = jnp.logical_or(routes_ref[0, r] == e, routes_ref[1, r] == e)
        found.append((named, taken))
        taken = taken + named.astype(jnp.int32)
    return found


def dispatch_kernel(tokens_hbm, routes_hbm, gates_hbm, sends_ref, table_ref, tokens_ref, routes_ref, gates_ref, sems):
    copies = [
        pltpu.make_async_copy(routes_hbm, routes_ref, sems.at[0]),
        pltpu.make_async_copy(gates_hbm, gates_ref, sems.at[1]),
        pltpu.make_async_copy(tokens_hbm, tokens_ref, sems.at[2]),
    ]
    for copy in copies:
        copy.start()
    for copy in copies:
        copy.wait()
    tokens = tokens_ref[...].astype(jnp.float32)
    rows = tokens.shape[0]
    tiles = sends_ref.shape[0] // 2
    for e in range(2):
        found = slot_rows(routes_ref, e, rows)
        base = e * (1 + SLOTS)
        line = (1, table_ref.shape[2])
        for r in range(rows):
            weight = jnp.where(routes_ref[0, r] == e, gates_ref[0, r], 0.0)
            weight = weight + jnp.where(routes_ref[1, r] == e, gates_ref[1, r], 0.0)
            table_ref[base, r:r + 1, :] = jnp.full(line, weight, jnp.float32)
        slots = []
        for c in range(SLOTS):
            row = jnp.zeros((1, tokens.shape[1]), jnp.float32)
            for r, (named, slot) in enumerate(found):
                here = jnp.logical_and(named, slot == c).astype(jnp.float32)
                row = row + here * tokens[r:r + 1, :]
                table_ref[base + 1 + c, r:r + 1, :] = jnp.full(line, here, jnp.float32)
            slots.append(row)
        block = jnp.concatenate(slots, axis=0).astype(jnp.bfloat16)
        for t in range(tiles):
            sends_ref[e * tiles + t] = block


def merge_kernel(blocks_ref, rows_ref):
    rows_ref[...] = blocks_ref[...].reshape(rows_ref.shape)


def project(rows_ref, w_ref, columns):
    slots, half = rows_ref.shape[0] // 2, rows_ref.shape[1]
    total = jnp.dot(rows_ref[:slots, :], w_ref[0, :half, columns], preferred_element_type=jnp.float32)
    return total + jnp.dot(rows_ref[slots:, :], w_ref[0, half:, columns], preferred_element_type=jnp.float32)


def over_columns(width, body):
    tile = 256

    def step(i, carry):
        body(pl.ds(pl.multiple_of(i * tile, tile), tile))
        return carry

    lax.fori_loop(0, width // tile, step, 0, unroll=8)


def gate_kernel(rows_ref, w_ref, out_ref):
    def body(columns):
        out_ref[:, columns] = project(rows_ref, w_ref, columns)

    over_columns(out_ref.shape[1], body)


def hidden_kernel(rows_ref, w_ref, gate_ref, hidden_ref):
    def body(columns):
        up = project(rows_ref, w_ref, columns)
        gate = gate_ref[:, columns]
        hidden_ref[:, columns] = (gate / (1.0 + jnp.exp(-gate)) * up).astype(jnp.bfloat16)

    over_columns(hidden_ref.shape[1], body)


def join_kernel(*refs):
    *blocks, _, out_ref = refs
    for i, block in enumerate(blocks):
        out_ref[i] = block[...]


def down_kernel(held, steps, first, last, *refs):
    blocks, w_ref, rest = refs[:held], refs[held], refs[held + 1:]
    if len(blocks) < len(steps):
        blocks = [blocks[0].at[i] for i in range(len(steps))]
    out_ref = rest[-1]
    me = lax.axis_index("tile")
    slots, width = blocks[0].shape
    part = 256
    starts = [pl.multiple_of((me ^ step) * width, width) for step in steps]
    for i in range(w_ref.shape[1] // part):
        rows = slice(i * part, (i + 1) * part)
        total = None if first else rest[0][rows, :]
        for block, start in zip(blocks, starts):
            term = lax.dot_general(
                w_ref[0, rows, pl.ds(start, width)], block[...], (((1,), (1,)), ((), ())),
                preferred_element_type=jnp.float32,
            )
            total = term if total is None else total + term
        if not last:
            out_ref[rows, :] = total
        else:
            total = total.T
            for t in range(out_ref.shape[0]):
                out_ref[t, :, rows] = total[t * SLOTS:(t + 1) * SLOTS, :]


def combine_kernel(own_ref, other_ref, table_ref, out_ref):
    mine = lax.axis_index("expert")
    halves, features = own_ref.shape[0] // 2, own_ref.shape[2]
    weight = [table_ref[e * (1 + SLOTS)][:, :1] for e in range(2)]
    inside = [[table_ref[e * (1 + SLOTS) + 1 + c][:, :1] for c in range(SLOTS)] for e in range(2)]
    for i in range(halves):
        own, other = own_ref[mine * halves + i], other_ref[mine * halves + i]
        mixed = jnp.zeros((out_ref.shape[0], features), jnp.float32)
        for e in range(2):
            both = jnp.where(mine == e, own, other)
            for c in range(SLOTS):
                value = (weight[e] * both[c:c + 1]).astype(jnp.bfloat16).astype(jnp.float32)
                mixed = mixed + jnp.where(inside[e][c] != 0.0, value, 0.0)
        out_ref[:, i * features:(i + 1) * features] = mixed.astype(jnp.bfloat16)


def local_direct(tokens, routes, gates, w_gate, w_up, w_down):
    tiles = lax.axis_size("tile")
    rows, half_width = tokens.shape
    width, features = w_gate.shape[2], w_down.shape[1]
    slots = tiles * SLOTS
    routes, gates = routes.T, gates.T

    def swap(x, bit):
        return lax.ppermute(x, "tile", [(t, t ^ bit) for t in range(tiles)])

    def to_core(x):
        return lax.ppermute(x, "expert", [(0, 1), (1, 0)])

    f32 = lambda *shape: jax.ShapeDtypeStruct(shape, jnp.float32)
    bf16 = lambda *shape: jax.ShapeDtypeStruct(shape, jnp.bfloat16)
    sends, table = call(
        dispatch_kernel, "dispatch",
        (bf16(2 * tiles, SLOTS, half_width), f32(2 * (1 + SLOTS), rows, 128)), [ANY] * 3, 4 * MIB, 600e-6,
        [
            pltpu.VMEM((rows, half_width), jnp.bfloat16),
            pltpu.SMEM((2, rows), jnp.int32),
            pltpu.SMEM((2, rows), jnp.float32),
            pltpu.SemaphoreType.DMA((3,)),
        ],
    )(in_hbm(tokens), in_hbm(routes), in_hbm(gates))
    blocks = lax.all_to_all(sends, ("expert", "tile"), split_axis=0, concat_axis=0, tiled=True)
    x = call(merge_kernel, "merge", bf16(2 * slots, half_width), [VMEM], 4 * MIB, 0e-6)(blocks)
    gate = call(gate_kernel, "gate", f32(slots, width), [VMEM] * 2, 4 * MIB, 0e-6)(x, in_vmem(w_gate))
    hidden = call(hidden_kernel, "hidden", bf16(slots, width), [VMEM] * 3, 4 * MIB, 200e-6)(x, in_vmem(w_up), gate)

    def down(total, steps, blocks, last):
        first = total is None
        out = f32(tiles, SLOTS, features) if last else f32(features, slots)
        return call(
            functools.partial(down_kernel, len(blocks), steps, first, last), "down", out,
            [VMEM] * (len(blocks) + 2 - first), 8 * MIB, 0e-6,
        )(*blocks, in_vmem(w_down), *(() if first else (total,)))

    near = [swap(hidden, k) for k in (6, 4, 2)]
    beside = swap(hidden, 1)
    column = call(join_kernel, "join", bf16(3, slots, width), [VMEM] * 4, 4 * MIB)(*near, beside)
    other_column = swap(column, 1)
    total = down(None, [0, 1], [hidden, beside], False)
    total = down(total, [6, 4, 2], [column], False)
    result = down(total, [7, 5, 3], [other_column], True)
    back = lax.all_to_all(result, "tile", split_axis=0, concat_axis=0, tiled=True)
    return call(combine_kernel, "combine", bf16(rows, half_width), [VMEM] * 3, 4 * MIB)(back, to_core(back), table)


def local_gathered(tokens, routes, gates, w_gate, w_up, w_down):
    experts = lax.axis_size("expert")
    tile_count = lax.axis_size("tile")
    own_expert = lax.axis_index("expert")
    half_width = tokens.shape[1]
    tok_rows = tokens.shape[0]
    slot_count = max(2, tok_rows // 2)
    window_ids = lax.broadcasted_iota(jnp.int32, (1, 1, experts), 2)
    is_named = routes[:, :, None] == window_ids
    chosen = jnp.any(is_named, axis=1)
    weight = jnp.sum(jnp.where(is_named, gates[:, :, None], jnp.float32(0.0)), axis=1)
    position = jnp.cumsum(chosen.astype(jnp.int32), axis=0) - 1
    slot_ids = lax.broadcasted_iota(jnp.int32, (1, slot_count, 1), 1)
    dispatch = jnp.logical_and(chosen.T[:, None, :], position.T[:, None, :] == slot_ids)
    placing = dispatch.astype(jnp.bfloat16)
    outgoing = jnp.einsum(
        "ecr,rd->ecd", placing, tokens, preferred_element_type=jnp.float32
    ).astype(jnp.bfloat16)
    slot_weight = jnp.einsum("ecr,re->ec", dispatch.astype(jnp.float32), weight)
    everything = lax.all_gather(outgoing[None], ("expert", "tile"), axis=0, tiled=True)
    picked = lax.dynamic_slice_in_dim(everything, own_expert, 1, 1)[:, 0]
    picked = picked.reshape(experts, tile_count, slot_count, half_width)
    gathered = jnp.transpose(picked, (1, 2, 0, 3)).reshape(
        tile_count * slot_count, experts * half_width
    )
    gate_proj = jnp.dot(gathered, w_gate[0], preferred_element_type=jnp.float32)
    up_proj = jnp.dot(gathered, w_up[0], preferred_element_type=jnp.float32)
    hidden = (jax.nn.silu(gate_proj) * up_proj).astype(jnp.bfloat16)
    columns = w_down[0]
    summed = lax.dot_general(
        columns,
        lax.all_gather(hidden, "tile", axis=1, tiled=True),
        (((1,), (1,)), ((), ())),
        preferred_element_type=jnp.float32,
    )
    homeward = lax.all_to_all(summed, "tile", split_axis=1, concat_axis=0, tiled=True)
    returned = lax.all_to_all(homeward, "expert", split_axis=0, concat_axis=1, tiled=True)
    contribution = (slot_weight.reshape(1, experts * slot_count) * returned).astype(jnp.bfloat16)
    flat_places = placing.reshape(experts * slot_count, tok_rows)
    return jnp.einsum(
        "st,ds->td", flat_places, contribution, preferred_element_type=jnp.float32
    ).astype(jnp.bfloat16)


def solution(mesh):
    in_specs = (
        P(("group", "tile"), "expert"),
        P(("group", "tile"), None),
        P(("group", "tile"), None),
        P("expert", None, "tile"),
        P("expert", None, "tile"),
        P("expert", "tile", None),
    )
    out_specs = P(("group", "tile"), "expert")
    local = local_direct if mesh.shape["tile"] == 8 else local_gathered
    return jax.shard_map(local, mesh=mesh, in_specs=in_specs, out_specs=out_specs, check_vma=False)
```

```python
import functools

import jax
import jax.numpy as jnp
from jax import lax
from jax.experimental import pallas as pl
from jax.experimental.pallas import tpu as pltpu
from jax.sharding import PartitionSpec as P

MIB = 1 << 20
SLOTS = 2
VMEM = pl.BlockSpec(memory_space=pltpu.VMEM)
ANY = pl.BlockSpec(memory_space=pl.ANY)


def in_vmem(x):
    return pltpu.with_memory_space_constraint(x, pltpu.VMEM)


def in_hbm(x):
    return pltpu.with_memory_space_constraint(x, pltpu.HBM)


def call(kernel, name, out, in_specs, limit, seconds=0.0, scratch=()):
    return pl.pallas_call(
        kernel,
        out_shape=out,
        in_specs=in_specs,
        out_specs=jax.tree.map(lambda _: VMEM, out),
        scratch_shapes=scratch,
        compiler_params=pltpu.CompilerParams(vmem_limit_bytes=limit),
        cost_estimate=pl.CostEstimate(flops=int(seconds*1e15), bytes_accessed=0, transcendentals=0),
        name=name,
    )


def slot_rows(routes_ref, e, rows):
    taken = jnp.int32(0)
    found = []
    for r in range(rows):
        named = jnp.logical_or(routes_ref[0, r] == e, routes_ref[1, r] == e)
        found.append((named, taken))
        taken = taken + named.astype(jnp.int32)
    return found


def dispatch_kernel(tokens_hbm, routes_hbm, gates_hbm, sends_ref, table_ref, tokens_ref, routes_ref, gates_ref, sems):
    copies = [
        pltpu.make_async_copy(routes_hbm, routes_ref, sems.at[0]),
        pltpu.make_async_copy(gates_hbm, gates_ref, sems.at[1]),
        pltpu.make_async_copy(tokens_hbm, tokens_ref, sems.at[2]),
    ]
    for copy in copies:
        copy.start()
    for copy in copies:
        copy.wait()
    tokens = tokens_ref[...].astype(jnp.float32)
    rows = tokens.shape[0]
    tiles = sends_ref.shape[0] // 2
    for e in range(2):
        found = slot_rows(routes_ref, e, rows)
        base = e * (1 + SLOTS)
        line = (1, table_ref.shape[2])
        for r in range(rows):
            weight = jnp.where(routes_ref[0, r] == e, gates_ref[0, r], 0.0)
            weight = weight + jnp.where(routes_ref[1, r] == e, gates_ref[1, r], 0.0)
            table_ref[base, r:r + 1, :] = jnp.full(line, weight, jnp.float32)
        slots = []
        for c in range(SLOTS):
            row = jnp.zeros((1, tokens.shape[1]), jnp.float32)
            for r, (named, slot) in enumerate(found):
                here = jnp.logical_and(named, slot == c).astype(jnp.float32)
                row = row + here * tokens[r:r + 1, :]
                table_ref[base + 1 + c, r:r + 1, :] = jnp.full(line, here, jnp.float32)
            slots.append(row)
        block = jnp.concatenate(slots, axis=0).astype(jnp.bfloat16)
        for t in range(tiles):
            sends_ref[e * tiles + t] = block


def merge_kernel(blocks_ref, rows_ref):
    rows_ref[...] = blocks_ref[...].reshape(rows_ref.shape)


def project(rows_ref, w_ref, columns):
    slots, half = rows_ref.shape[0] // 2, rows_ref.shape[1]
    total = jnp.dot(rows_ref[:slots, :], w_ref[0, :half, columns], preferred_element_type=jnp.float32)
    return total + jnp.dot(rows_ref[slots:, :], w_ref[0, half:, columns], preferred_element_type=jnp.float32)


def over_columns(width, body):
    tile = 256

    def step(i, carry):
        body(pl.ds(pl.multiple_of(i * tile, tile), tile))
        return carry

    lax.fori_loop(0, width // tile, step, 0, unroll=8)


def gate_kernel(rows_ref, w_ref, out_ref):
    def body(columns):
        out_ref[:, columns] = project(rows_ref, w_ref, columns)

    over_columns(out_ref.shape[1], body)


def hidden_kernel(rows_ref, w_ref, gate_ref, hidden_ref):
    def body(columns):
        up = project(rows_ref, w_ref, columns)
        gate = gate_ref[:, columns]
        hidden_ref[:, columns] = (gate / (1.0 + jnp.exp(-gate)) * up).astype(jnp.bfloat16)

    over_columns(hidden_ref.shape[1], body)


def down_kernel(steps, first, last, *refs):
    n = len(steps)
    blocks, w_ref, rest = refs[:n], refs[n], refs[n + 1:]
    out_ref = rest[-1]
    me = lax.axis_index("tile")
    slots, width = blocks[0].shape
    part = 256
    starts = [pl.multiple_of((me ^ step) * width, width) for step in steps]
    for i in range(w_ref.shape[1] // part):
        rows = slice(i * part, (i + 1) * part)
        total = None if first else rest[0][rows, :]
        for block, start in zip(blocks, starts):
            term = lax.dot_general(
                w_ref[0, rows, pl.ds(start, width)], block[...], (((1,), (1,)), ((), ())),
                preferred_element_type=jnp.float32,
            )
            total = term if total is None else total + term
        if not last:
            out_ref[rows, :] = total
        else:
            total = total.T
            for t in range(out_ref.shape[0]):
                out_ref[t, :, rows] = total[t * SLOTS:(t + 1) * SLOTS, :]


def combine_kernel(own_ref, other_ref, table_ref, out_ref):
    mine = lax.axis_index("expert")
    halves, features = own_ref.shape[0] // 2, own_ref.shape[2]
    weight = [table_ref[e * (1 + SLOTS)][:, :1] for e in range(2)]
    inside = [[table_ref[e * (1 + SLOTS) + 1 + c][:, :1] for c in range(SLOTS)] for e in range(2)]
    for i in range(halves):
        own, other = own_ref[mine * halves + i], other_ref[mine * halves + i]
        mixed = jnp.zeros((out_ref.shape[0], features), jnp.float32)
        for e in range(2):
            both = jnp.where(mine == e, own, other)
            for c in range(SLOTS):
                value = (weight[e] * both[c:c + 1]).astype(jnp.bfloat16).astype(jnp.float32)
                mixed = mixed + jnp.where(inside[e][c] != 0.0, value, 0.0)
        out_ref[:, i * features:(i + 1) * features] = mixed.astype(jnp.bfloat16)


def local_direct(tokens, routes, gates, w_gate, w_up, w_down):
    tiles = lax.axis_size("tile")
    rows, half_width = tokens.shape
    width, features = w_gate.shape[2], w_down.shape[1]
    slots = tiles * SLOTS
    routes, gates = routes.T, gates.T

    def swap(x, bit):
        return lax.ppermute(x, "tile", [(t, t ^ bit) for t in range(tiles)])

    def to_core(x):
        return lax.ppermute(x, "expert", [(0, 1), (1, 0)])

    f32 = lambda *shape: jax.ShapeDtypeStruct(shape, jnp.float32)
    bf16 = lambda *shape: jax.ShapeDtypeStruct(shape, jnp.bfloat16)
    sends, table = call(
        dispatch_kernel, "dispatch",
        (bf16(2 * tiles, SLOTS, half_width), f32(2 * (1 + SLOTS), rows, 128)), [ANY] * 3, 4 * MIB, 600e-6,
        [
            pltpu.VMEM((rows, half_width), jnp.bfloat16),
            pltpu.SMEM((2, rows), jnp.int32),
            pltpu.SMEM((2, rows), jnp.float32),
            pltpu.SemaphoreType.DMA((3,)),
        ],
    )(in_hbm(tokens), in_hbm(routes), in_hbm(gates))
    blocks = lax.all_to_all(sends, ("expert", "tile"), split_axis=0, concat_axis=0, tiled=True)
    x = call(merge_kernel, "merge", bf16(2 * slots, half_width), [VMEM], 4 * MIB, 0e-6)(blocks)
    gate = call(gate_kernel, "gate", f32(slots, width), [VMEM] * 2, 4 * MIB, 0e-6)(x, in_vmem(w_gate))
    hidden = call(hidden_kernel, "hidden", bf16(slots, width), [VMEM] * 3, 4 * MIB, 200e-6)(x, in_vmem(w_up), gate)

    def down(total, steps, blocks, last):
        first = total is None
        out = f32(tiles, SLOTS, features) if last else f32(features, slots)
        return call(
            functools.partial(down_kernel, steps, first, last), "down", out,
            [VMEM] * (len(blocks) + 2 - first), 8 * MIB, 0e-6,
        )(*blocks, in_vmem(w_down), *(() if first else (total,)))

    beside = swap(hidden, 1)
    column = [swap(hidden, k) for k in (6, 4, 2)]
    total = down(None, [0, 1], [hidden, beside], False)
    total, first = lax.optimization_barrier((total, column[0]))
    column = [first] + column[1:]
    other_column = [swap(block, 1) for block in column]
    total = down(total, [6, 4, 2], column, False)
    result = down(total, [7, 5, 3], other_column, True)
    back = lax.all_to_all(result, "tile", split_axis=0, concat_axis=0, tiled=True)
    return call(combine_kernel, "combine", bf16(rows, half_width), [VMEM] * 3, 4 * MIB)(back, to_core(back), table)


def local_gathered(tokens, routes, gates, w_gate, w_up, w_down):
    experts = lax.axis_size("expert")
    tile_count = lax.axis_size("tile")
    own_expert = lax.axis_index("expert")
    half_width = tokens.shape[1]
    tok_rows = tokens.shape[0]
    slot_count = max(2, tok_rows // 2)
    window_ids = lax.broadcasted_iota(jnp.int32, (1, 1, experts), 2)
    is_named = routes[:, :, None] == window_ids
    chosen = jnp.any(is_named, axis=1)
    weight = jnp.sum(jnp.where(is_named, gates[:, :, None], jnp.float32(0.0)), axis=1)
    position = jnp.cumsum(chosen.astype(jnp.int32), axis=0) - 1
    slot_ids = lax.broadcasted_iota(jnp.int32, (1, slot_count, 1), 1)
    dispatch = jnp.logical_and(chosen.T[:, None, :], position.T[:, None, :] == slot_ids)
    placing = dispatch.astype(jnp.bfloat16)
    outgoing = jnp.einsum(
        "ecr,rd->ecd", placing, tokens, preferred_element_type=jnp.float32
    ).astype(jnp.bfloat16)
    slot_weight = jnp.einsum("ecr,re->ec", dispatch.astype(jnp.float32), weight)
    everything = lax.all_gather(outgoing[None], ("expert", "tile"), axis=0, tiled=True)
    picked = lax.dynamic_slice_in_dim(everything, own_expert, 1, 1)[:, 0]
    picked = picked.reshape(experts, tile_count, slot_count, half_width)
    gathered = jnp.transpose(picked, (1, 2, 0, 3)).reshape(
        tile_count * slot_count, experts * half_width
    )
    gate_proj = jnp.dot(gathered, w_gate[0], preferred_element_type=jnp.float32)
    up_proj = jnp.dot(gathered, w_up[0], preferred_element_type=jnp.float32)
    hidden = (jax.nn.silu(gate_proj) * up_proj).astype(jnp.bfloat16)
    columns = w_down[0]
    summed = lax.dot_general(
        columns,
        lax.all_gather(hidden, "tile", axis=1, tiled=True),
        (((1,), (1,)), ((), ())),
        preferred_element_type=jnp.float32,
    )
    homeward = lax.all_to_all(summed, "tile", split_axis=1, concat_axis=0, tiled=True)
    returned = lax.all_to_all(homeward, "expert", split_axis=0, concat_axis=1, tiled=True)
    contribution = (slot_weight.reshape(1, experts * slot_count) * returned).astype(jnp.bfloat16)
    flat_places = placing.reshape(experts * slot_count, tok_rows)
    return jnp.einsum(
        "st,ds->td", flat_places, contribution, preferred_element_type=jnp.float32
    ).astype(jnp.bfloat16)


def solution(mesh):
    in_specs = (
        P(("group", "tile"), "expert"),
        P(("group", "tile"), None),
        P(("group", "tile"), None),
        P("expert", None, "tile"),
        P("expert", None, "tile"),
        P("expert", "tile", None),
    )
    out_specs = P(("group", "tile"), "expert")
    local = local_direct if mesh.shape["tile"] == 8 else local_gathered
    return jax.shard_map(local, mesh=mesh, in_specs=in_specs, out_specs=out_specs, check_vma=False)
```

```python
import functools

import jax
import jax.numpy as jnp
from jax import lax
from jax.experimental import pallas as pl
from jax.experimental.pallas import tpu as pltpu
from jax.sharding import PartitionSpec as P

MIB = 1 << 20
SLOTS = 2
VMEM = pl.BlockSpec(memory_space=pltpu.VMEM)
ANY = pl.BlockSpec(memory_space=pl.ANY)


def in_vmem(x):
    return pltpu.with_memory_space_constraint(x, pltpu.VMEM)


def in_hbm(x):
    return pltpu.with_memory_space_constraint(x, pltpu.HBM)


def call(kernel, name, out, in_specs, limit, seconds=0.0, scratch=()):
    return pl.pallas_call(
        kernel,
        out_shape=out,
        in_specs=in_specs,
        out_specs=jax.tree.map(lambda _: VMEM, out),
        scratch_shapes=scratch,
        compiler_params=pltpu.CompilerParams(vmem_limit_bytes=limit),
        cost_estimate=pl.CostEstimate(flops=int(seconds*1e15), bytes_accessed=0, transcendentals=0),
        name=name,
    )


def slot_rows(routes_ref, e, rows):
    taken = jnp.int32(0)
    found = []
    for r in range(rows):
        named = jnp.logical_or(routes_ref[0, r] == e, routes_ref[1, r] == e)
        found.append((named, taken))
        taken = taken + named.astype(jnp.int32)
    return found


def dispatch_kernel(tokens_hbm, routes_hbm, gates_hbm, sends_ref, table_ref, tokens_ref, routes_ref, gates_ref, sems):
    copies = [
        pltpu.make_async_copy(routes_hbm, routes_ref, sems.at[0]),
        pltpu.make_async_copy(gates_hbm, gates_ref, sems.at[1]),
        pltpu.make_async_copy(tokens_hbm, tokens_ref, sems.at[2]),
    ]
    for copy in copies:
        copy.start()
    for copy in copies:
        copy.wait()
    tokens = tokens_ref[...].astype(jnp.float32)
    rows = tokens.shape[0]
    tiles = sends_ref.shape[0] // 2
    for e in range(2):
        found = slot_rows(routes_ref, e, rows)
        base = e * (1 + SLOTS)
        line = (1, table_ref.shape[2])
        for r in range(rows):
            weight = jnp.where(routes_ref[0, r] == e, gates_ref[0, r], 0.0)
            weight = weight + jnp.where(routes_ref[1, r] == e, gates_ref[1, r], 0.0)
            table_ref[base, r:r + 1, :] = jnp.full(line, weight, jnp.float32)
        slots = []
        for c in range(SLOTS):
            row = jnp.zeros((1, tokens.shape[1]), jnp.float32)
            for r, (named, slot) in enumerate(found):
                here = jnp.logical_and(named, slot == c).astype(jnp.float32)
                row = row + here * tokens[r:r + 1, :]
                table_ref[base + 1 + c, r:r + 1, :] = jnp.full(line, here, jnp.float32)
            slots.append(row)
        block = jnp.concatenate(slots, axis=0).astype(jnp.bfloat16)
        for t in range(tiles):
            sends_ref[e * tiles + t] = block


def merge_kernel(blocks_ref, rows_ref):
    rows_ref[...] = blocks_ref[...].reshape(rows_ref.shape)


def project(rows_ref, w_ref, columns):
    slots, half = rows_ref.shape[0] // 2, rows_ref.shape[1]
    total = jnp.dot(rows_ref[:slots, :], w_ref[0, :half, columns], preferred_element_type=jnp.float32)
    return total + jnp.dot(rows_ref[slots:, :], w_ref[0, half:, columns], preferred_element_type=jnp.float32)


def over_columns(width, body):
    tile = 256

    def step(i, carry):
        body(pl.ds(pl.multiple_of(i * tile, tile), tile))
        return carry

    lax.fori_loop(0, width // tile, step, 0, unroll=8)


def gate_kernel(rows_ref, w_ref, out_ref):
    def body(columns):
        out_ref[:, columns] = project(rows_ref, w_ref, columns)

    over_columns(out_ref.shape[1], body)


def hidden_kernel(rows_ref, w_ref, gate_ref, hidden_ref):
    def body(columns):
        up = project(rows_ref, w_ref, columns)
        gate = gate_ref[:, columns]
        hidden_ref[:, columns] = (gate / (1.0 + jnp.exp(-gate)) * up).astype(jnp.bfloat16)

    over_columns(hidden_ref.shape[1], body)


def down_kernel(steps, first, last, *refs):
    n = len(steps)
    blocks, w_ref, rest = refs[:n], refs[n], refs[n + 1:]
    out_ref = rest[-1]
    me = lax.axis_index("tile")
    slots, width = blocks[0].shape
    total = None if first else rest[0][...]
    for step, block in zip(steps, blocks):
        columns = pl.ds(pl.multiple_of((me ^ step) * width, width), width)
        term = lax.dot_general(
            w_ref[0, :, columns], block[...], (((1,), (1,)), ((), ())), preferred_element_type=jnp.float32)
        total = term if total is None else total + term
    if not last:
        out_ref[...] = total
    else:
        total = total.T
        for t in range(out_ref.shape[0]):
            out_ref[t] = total[t * SLOTS:(t + 1) * SLOTS, :]


def combine_kernel(own_ref, other_ref, table_ref, out_ref):
    mine = lax.axis_index("expert")
    halves, features = own_ref.shape[0] // 2, own_ref.shape[2]
    weight = [table_ref[e * (1 + SLOTS)][:, :1] for e in range(2)]
    inside = [[table_ref[e * (1 + SLOTS) + 1 + c][:, :1] for c in range(SLOTS)] for e in range(2)]
    for i in range(halves):
        own, other = own_ref[mine * halves + i], other_ref[mine * halves + i]
        mixed = jnp.zeros((out_ref.shape[0], features), jnp.float32)
        for e in range(2):
            both = jnp.where(mine == e, own, other)
            for c in range(SLOTS):
                value = (weight[e] * both[c:c + 1]).astype(jnp.bfloat16).astype(jnp.float32)
                mixed = mixed + jnp.where(inside[e][c] != 0.0, value, 0.0)
        out_ref[:, i * features:(i + 1) * features] = mixed.astype(jnp.bfloat16)


def local_direct(tokens, routes, gates, w_gate, w_up, w_down):
    tiles = lax.axis_size("tile")
    rows, half_width = tokens.shape
    width, features = w_gate.shape[2], w_down.shape[1]
    slots = tiles * SLOTS
    routes, gates = routes.T, gates.T

    def swap(x, bit):
        return lax.ppermute(x, "tile", [(t, t ^ bit) for t in range(tiles)])

    def to_core(x):
        return lax.ppermute(x, "expert", [(0, 1), (1, 0)])

    f32 = lambda *shape: jax.ShapeDtypeStruct(shape, jnp.float32)
    bf16 = lambda *shape: jax.ShapeDtypeStruct(shape, jnp.bfloat16)
    sends, table = call(
        dispatch_kernel, "dispatch",
        (bf16(2 * tiles, SLOTS, half_width), f32(2 * (1 + SLOTS), rows, 128)), [ANY] * 3, 4 * MIB, 600e-6,
        [
            pltpu.VMEM((rows, half_width), jnp.bfloat16),
            pltpu.SMEM((2, rows), jnp.int32),
            pltpu.SMEM((2, rows), jnp.float32),
            pltpu.SemaphoreType.DMA((3,)),
        ],
    )(in_hbm(tokens), in_hbm(routes), in_hbm(gates))
    blocks = lax.all_to_all(sends, ("expert", "tile"), split_axis=0, concat_axis=0, tiled=True)
    x = call(merge_kernel, "merge", bf16(2 * slots, half_width), [VMEM], 4 * MIB, 0e-6)(blocks)
    gate = call(gate_kernel, "gate", f32(slots, width), [VMEM] * 2, 4 * MIB, 0e-6)(x, in_vmem(w_gate))
    hidden = call(hidden_kernel, "hidden", bf16(slots, width), [VMEM] * 3, 4 * MIB, 200e-6)(x, in_vmem(w_up), gate)

    def down(total, steps, blocks, last):
        first = total is None
        out = f32(tiles, SLOTS, features) if last else f32(features, slots)
        return call(
            functools.partial(down_kernel, steps, first, last), "down", out,
            [VMEM] * (len(blocks) + 2 - first), 10 * MIB, 0e-6,
        )(*blocks, in_vmem(w_down), *(() if first else (total,)))

    column = [swap(hidden, k) for k in (6, 4, 2)]
    beside = swap(hidden, 1)
    total = down(None, [0], [hidden], False)
    total = down(total, [1], [beside], False)
    total, column[0] = lax.optimization_barrier((total, column[0]))
    other_column = [swap(block, 1) for block in column]
    total = down(total, [6, 4], column[:2], False)
    total = down(total, [2], column[2:], False)
    total = down(total, [7, 5], other_column[:2], False)
    result = down(total, [3], other_column[2:], True)
    back = lax.all_to_all(result, "tile", split_axis=0, concat_axis=0, tiled=True)
    return call(combine_kernel, "combine", bf16(rows, half_width), [VMEM] * 3, 4 * MIB)(back, to_core(back), table)


def local_gathered(tokens, routes, gates, w_gate, w_up, w_down):
    experts = lax.axis_size("expert")
    tile_count = lax.axis_size("tile")
    own_expert = lax.axis_index("expert")
    half_width = tokens.shape[1]
    tok_rows = tokens.shape[0]
    slot_count = max(2, tok_rows // 2)
    window_ids = lax.broadcasted_iota(jnp.int32, (1, 1, experts), 2)
    is_named = routes[:, :, None] == window_ids
    chosen = jnp.any(is_named, axis=1)
    weight = jnp.sum(jnp.where(is_named, gates[:, :, None], jnp.float32(0.0)), axis=1)
    position = jnp.cumsum(chosen.astype(jnp.int32), axis=0) - 1
    slot_ids = lax.broadcasted_iota(jnp.int32, (1, slot_count, 1), 1)
    dispatch = jnp.logical_and(chosen.T[:, None, :], position.T[:, None, :] == slot_ids)
    placing = dispatch.astype(jnp.bfloat16)
    outgoing = jnp.einsum(
        "ecr,rd->ecd", placing, tokens, preferred_element_type=jnp.float32
    ).astype(jnp.bfloat16)
    slot_weight = jnp.einsum("ecr,re->ec", dispatch.astype(jnp.float32), weight)
    everything = lax.all_gather(outgoing[None], ("expert", "tile"), axis=0, tiled=True)
    picked = lax.dynamic_slice_in_dim(everything, own_expert, 1, 1)[:, 0]
    picked = picked.reshape(experts, tile_count, slot_count, half_width)
    gathered = jnp.transpose(picked, (1, 2, 0, 3)).reshape(
        tile_count * slot_count, experts * half_width
    )
    gate_proj = jnp.dot(gathered, w_gate[0], preferred_element_type=jnp.float32)
    up_proj = jnp.dot(gathered, w_up[0], preferred_element_type=jnp.float32)
    hidden = (jax.nn.silu(gate_proj) * up_proj).astype(jnp.bfloat16)
    columns = w_down[0]
    summed = lax.dot_general(
        columns,
        lax.all_gather(hidden, "tile", axis=1, tiled=True),
        (((1,), (1,)), ((), ())),
        preferred_element_type=jnp.float32,
    )
    homeward = lax.all_to_all(summed, "tile", split_axis=1, concat_axis=0, tiled=True)
    returned = lax.all_to_all(homeward, "expert", split_axis=0, concat_axis=1, tiled=True)
    contribution = (slot_weight.reshape(1, experts * slot_count) * returned).astype(jnp.bfloat16)
    flat_places = placing.reshape(experts * slot_count, tok_rows)
    return jnp.einsum(
        "st,ds->td", flat_places, contribution, preferred_element_type=jnp.float32
    ).astype(jnp.bfloat16)


def solution(mesh):
    in_specs = (
        P(("group", "tile"), "expert"),
        P(("group", "tile"), None),
        P(("group", "tile"), None),
        P("expert", None, "tile"),
        P("expert", None, "tile"),
        P("expert", "tile", None),
    )
    out_specs = P(("group", "tile"), "expert")
    local = local_direct if mesh.shape["tile"] == 8 else local_gathered
    return jax.shard_map(local, mesh=mesh, in_specs=in_specs, out_specs=out_specs, check_vma=False)
```

```python
import functools

import jax
import jax.numpy as jnp
from jax import lax
from jax.experimental import pallas as pl
from jax.experimental.pallas import tpu as pltpu
from jax.sharding import PartitionSpec as P

MIB = 1 << 20
SLOTS = 2
VMEM = pl.BlockSpec(memory_space=pltpu.VMEM)
ANY = pl.BlockSpec(memory_space=pl.ANY)


def in_vmem(x):
    return pltpu.with_memory_space_constraint(x, pltpu.VMEM)


def in_hbm(x):
    return pltpu.with_memory_space_constraint(x, pltpu.HBM)


def call(kernel, name, out, in_specs, limit, seconds=0.0, scratch=()):
    return pl.pallas_call(
        kernel,
        out_shape=out,
        in_specs=in_specs,
        out_specs=jax.tree.map(lambda _: VMEM, out),
        scratch_shapes=scratch,
        compiler_params=pltpu.CompilerParams(vmem_limit_bytes=limit),
        cost_estimate=pl.CostEstimate(flops=int(seconds*1e15), bytes_accessed=0, transcendentals=0),
        name=name,
    )


def slot_rows(routes_ref, e, rows):
    taken = jnp.int32(0)
    found = []
    for r in range(rows):
        named = jnp.logical_or(routes_ref[0, r] == e, routes_ref[1, r] == e)
        found.append((named, taken))
        taken = taken + named.astype(jnp.int32)
    return found


def dispatch_kernel(tokens_hbm, routes_hbm, gates_hbm, sends_ref, table_ref, tokens_ref, routes_ref, gates_ref, sems):
    copies = [
        pltpu.make_async_copy(routes_hbm, routes_ref, sems.at[0]),
        pltpu.make_async_copy(gates_hbm, gates_ref, sems.at[1]),
        pltpu.make_async_copy(tokens_hbm, tokens_ref, sems.at[2]),
    ]
    for copy in copies:
        copy.start()
    for copy in copies:
        copy.wait()
    tokens = tokens_ref[...].astype(jnp.float32)
    rows = tokens.shape[0]
    tiles = sends_ref.shape[0] // 2
    for e in range(2):
        found = slot_rows(routes_ref, e, rows)
        base = e * (1 + SLOTS)
        line = (1, table_ref.shape[2])
        for r in range(rows):
            weight = jnp.where(routes_ref[0, r] == e, gates_ref[0, r], 0.0)
            weight = weight + jnp.where(routes_ref[1, r] == e, gates_ref[1, r], 0.0)
            table_ref[base, r:r + 1, :] = jnp.full(line, weight, jnp.float32)
        slots = []
        for c in range(SLOTS):
            row = jnp.zeros((1, tokens.shape[1]), jnp.float32)
            for r, (named, slot) in enumerate(found):
                here = jnp.logical_and(named, slot == c).astype(jnp.float32)
                row = row + here * tokens[r:r + 1, :]
                table_ref[base + 1 + c, r:r + 1, :] = jnp.full(line, here, jnp.float32)
            slots.append(row)
        block = jnp.concatenate(slots, axis=0).astype(jnp.bfloat16)
        for t in range(tiles):
            sends_ref[e * tiles + t] = block


def merge_kernel(blocks_ref, rows_ref):
    rows_ref[...] = blocks_ref[...].reshape(rows_ref.shape)


def project(rows_ref, w_ref, columns):
    slots, half = rows_ref.shape[0] // 2, rows_ref.shape[1]
    total = jnp.dot(rows_ref[:slots, :], w_ref[0, :half, columns], preferred_element_type=jnp.float32)
    return total + jnp.dot(rows_ref[slots:, :], w_ref[0, half:, columns], preferred_element_type=jnp.float32)


def over_columns(width, body):
    tile = 256

    def step(i, carry):
        body(pl.ds(pl.multiple_of(i * tile, tile), tile))
        return carry

    lax.fori_loop(0, width // tile, step, 0, unroll=8)


def gate_kernel(rows_ref, w_ref, out_ref):
    def body(columns):
        out_ref[:, columns] = project(rows_ref, w_ref, columns)

    over_columns(out_ref.shape[1], body)


def hidden_kernel(rows_ref, w_ref, gate_ref, hidden_ref):
    def body(columns):
        up = project(rows_ref, w_ref, columns)
        gate = gate_ref[:, columns]
        hidden_ref[:, columns] = (gate / (1.0 + jnp.exp(-gate)) * up).astype(jnp.bfloat16)

    over_columns(hidden_ref.shape[1], body)


def down_kernel(steps, first, last, *refs):
    n = len(steps)
    blocks, w_ref, rest = refs[:n], refs[n], refs[n + 1:]
    out_ref = rest[-1]
    me = lax.axis_index("tile")
    slots, width = blocks[0].shape
    total = None if first else rest[0][...]
    for step, block in zip(steps, blocks):
        columns = pl.ds(pl.multiple_of((me ^ step) * width, width), width)
        term = lax.dot_general(
            w_ref[0, :, columns], block[...], (((1,), (1,)), ((), ())), preferred_element_type=jnp.float32)
        total = term if total is None else total + term
    if not last:
        out_ref[...] = total
    else:
        total = total.T
        for t in range(2 * out_ref.shape[0]):
            out_ref[t // 2, t % 2] = total[t * SLOTS:(t + 1) * SLOTS, :]


def split_kernel(blocks_ref, *out_refs):
    x, core = lax.axis_index("tile") % 2, lax.axis_index("expert")
    for i, out_ref in enumerate(out_refs):
        to_x, to_core = x ^ (i % 2), core ^ (i // 2)
        for z in range(out_ref.shape[0]):
            out_ref[z] = blocks_ref[to_core * out_ref.shape[0] + z, to_x]


def combine_kernel(own_ref, own_x_ref, other_ref, other_x_ref, table_ref, out_ref):
    x, mine = lax.axis_index("tile") % 2, lax.axis_index("expert")
    features = own_ref.shape[2]
    weight = [table_ref[e * (1 + SLOTS)][:, :1] for e in range(2)]
    inside = [[table_ref[e * (1 + SLOTS) + 1 + c][:, :1] for c in range(SLOTS)] for e in range(2)]
    for i in range(2 * own_ref.shape[0]):
        z, at = i // 2, i % 2
        own = jnp.where(x == at, own_ref[z], own_x_ref[z])
        other = jnp.where(x == at, other_ref[z], other_x_ref[z])
        mixed = jnp.zeros((out_ref.shape[0], features), jnp.float32)
        for e in range(2):
            both = jnp.where(mine == e, own, other)
            for c in range(SLOTS):
                value = (weight[e] * both[c:c + 1]).astype(jnp.bfloat16).astype(jnp.float32)
                mixed = mixed + jnp.where(inside[e][c] != 0.0, value, 0.0)
        out_ref[:, i * features:(i + 1) * features] = mixed.astype(jnp.bfloat16)


def local_direct(tokens, routes, gates, w_gate, w_up, w_down):
    tiles = lax.axis_size("tile")
    rows, half_width = tokens.shape
    width, features = w_gate.shape[2], w_down.shape[1]
    slots = tiles * SLOTS
    routes, gates = routes.T, gates.T

    def swap(x, bit):
        return lax.ppermute(x, "tile", [(t, t ^ bit) for t in range(tiles)])

    def to_core(x):
        return lax.ppermute(x, "expert", [(0, 1), (1, 0)])

    f32 = lambda *shape: jax.ShapeDtypeStruct(shape, jnp.float32)
    bf16 = lambda *shape: jax.ShapeDtypeStruct(shape, jnp.bfloat16)
    sends, table = call(
        dispatch_kernel, "dispatch",
        (bf16(2 * tiles, SLOTS, half_width), f32(2 * (1 + SLOTS), rows, 128)), [ANY] * 3, 4 * MIB, 600e-6,
        [
            pltpu.VMEM((rows, half_width), jnp.bfloat16),
            pltpu.SMEM((2, rows), jnp.int32),
            pltpu.SMEM((2, rows), jnp.float32),
            pltpu.SemaphoreType.DMA((3,)),
        ],
    )(in_hbm(tokens), in_hbm(routes), in_hbm(gates))
    blocks = lax.all_to_all(sends, ("expert", "tile"), split_axis=0, concat_axis=0, tiled=True)
    x = call(merge_kernel, "merge", bf16(2 * slots, half_width), [VMEM], 4 * MIB, 0e-6)(blocks)
    gate = call(gate_kernel, "gate", f32(slots, width), [VMEM] * 2, 4 * MIB, 0e-6)(x, in_vmem(w_gate))
    hidden = call(hidden_kernel, "hidden", bf16(slots, width), [VMEM] * 3, 4 * MIB, 200e-6)(x, in_vmem(w_up), gate)

    def down(total, steps, blocks, last):
        first = total is None
        out = f32(tiles // 2, 2, SLOTS, features) if last else f32(features, slots)
        return call(
            functools.partial(down_kernel, steps, first, last), "down", out,
            [VMEM] * (len(blocks) + 2 - first), 10 * MIB, 0e-6,
        )(*blocks, in_vmem(w_down), *(() if first else (total,)))

    column = [swap(hidden, k) for k in (6, 4, 2)]
    beside = swap(hidden, 1)
    total = down(None, [0], [hidden], False)
    total = down(total, [1], [beside], False)
    total, column[0] = lax.optimization_barrier((total, column[0]))
    other_column = [swap(block, 1) for block in column]
    total = down(total, [6, 4], column[:2], False)
    total = down(total, [2], column[2:], False)
    total = down(total, [7, 5], other_column[:2], False)
    result = down(total, [3], other_column[2:], True)
    columns = [list(range(x, tiles, 2)) for x in range(2)]
    back = lax.all_to_all(result, "tile", split_axis=0, concat_axis=0, axis_index_groups=columns, tiled=True)
    quarter = f32(tiles // 4, SLOTS, features)
    own, to_x, to_other, to_both = call(split_kernel, "split", (quarter,) * 4, [VMEM], 4 * MIB)(back)
    pairs = [(e * tiles + t, (1 - e) * tiles + (t ^ 1)) for e in range(2) for t in range(tiles)]
    both = lax.ppermute(to_both, ("expert", "tile"), pairs)
    return call(combine_kernel, "combine", bf16(rows, half_width), [VMEM] * 5, 4 * MIB)(
        own, swap(to_x, 1), to_core(to_other), both, table)


def local_gathered(tokens, routes, gates, w_gate, w_up, w_down):
    experts = lax.axis_size("expert")
    tile_count = lax.axis_size("tile")
    own_expert = lax.axis_index("expert")
    half_width = tokens.shape[1]
    tok_rows = tokens.shape[0]
    slot_count = max(2, tok_rows // 2)
    window_ids = lax.broadcasted_iota(jnp.int32, (1, 1, experts), 2)
    is_named = routes[:, :, None] == window_ids
    chosen = jnp.any(is_named, axis=1)
    weight = jnp.sum(jnp.where(is_named, gates[:, :, None], jnp.float32(0.0)), axis=1)
    position = jnp.cumsum(chosen.astype(jnp.int32), axis=0) - 1
    slot_ids = lax.broadcasted_iota(jnp.int32, (1, slot_count, 1), 1)
    dispatch = jnp.logical_and(chosen.T[:, None, :], position.T[:, None, :] == slot_ids)
    placing = dispatch.astype(jnp.bfloat16)
    outgoing = jnp.einsum(
        "ecr,rd->ecd", placing, tokens, preferred_element_type=jnp.float32
    ).astype(jnp.bfloat16)
    slot_weight = jnp.einsum("ecr,re->ec", dispatch.astype(jnp.float32), weight)
    everything = lax.all_gather(outgoing[None], ("expert", "tile"), axis=0, tiled=True)
    picked = lax.dynamic_slice_in_dim(everything, own_expert, 1, 1)[:, 0]
    picked = picked.reshape(experts, tile_count, slot_count, half_width)
    gathered = jnp.transpose(picked, (1, 2, 0, 3)).reshape(
        tile_count * slot_count, experts * half_width
    )
    gate_proj = jnp.dot(gathered, w_gate[0], preferred_element_type=jnp.float32)
    up_proj = jnp.dot(gathered, w_up[0], preferred_element_type=jnp.float32)
    hidden = (jax.nn.silu(gate_proj) * up_proj).astype(jnp.bfloat16)
    columns = w_down[0]
    summed = lax.dot_general(
        columns,
        lax.all_gather(hidden, "tile", axis=1, tiled=True),
        (((1,), (1,)), ((), ())),
        preferred_element_type=jnp.float32,
    )
    homeward = lax.all_to_all(summed, "tile", split_axis=1, concat_axis=0, tiled=True)
    returned = lax.all_to_all(homeward, "expert", split_axis=0, concat_axis=1, tiled=True)
    contribution = (slot_weight.reshape(1, experts * slot_count) * returned).astype(jnp.bfloat16)
    flat_places = placing.reshape(experts * slot_count, tok_rows)
    return jnp.einsum(
        "st,ds->td", flat_places, contribution, preferred_element_type=jnp.float32
    ).astype(jnp.bfloat16)


def solution(mesh):
    in_specs = (
        P(("group", "tile"), "expert"),
        P(("group", "tile"), None),
        P(("group", "tile"), None),
        P("expert", None, "tile"),
        P("expert", None, "tile"),
        P("expert", "tile", None),
    )
    out_specs = P(("group", "tile"), "expert")
    local = local_direct if mesh.shape["tile"] == 8 else local_gathered
    return jax.shard_map(local, mesh=mesh, in_specs=in_specs, out_specs=out_specs, check_vma=False)
```

```python
import functools

import jax
import jax.numpy as jnp
from jax import lax
from jax.experimental import pallas as pl
from jax.experimental.pallas import tpu as pltpu
from jax.sharding import PartitionSpec as P

MIB = 1 << 20
SLOTS = 2
VMEM = pl.BlockSpec(memory_space=pltpu.VMEM)
ANY = pl.BlockSpec(memory_space=pl.ANY)


def in_vmem(x):
    return pltpu.with_memory_space_constraint(x, pltpu.VMEM)


def in_hbm(x):
    return pltpu.with_memory_space_constraint(x, pltpu.HBM)


def call(kernel, name, out, in_specs, limit, seconds=0.0, scratch=()):
    return pl.pallas_call(
        kernel,
        out_shape=out,
        in_specs=in_specs,
        out_specs=jax.tree.map(lambda _: VMEM, out),
        scratch_shapes=scratch,
        compiler_params=pltpu.CompilerParams(vmem_limit_bytes=limit),
        cost_estimate=pl.CostEstimate(flops=int(seconds*1e15), bytes_accessed=0, transcendentals=0),
        name=name,
    )


def slot_rows(routes_ref, e, rows):
    taken = jnp.int32(0)
    found = []
    for r in range(rows):
        named = jnp.logical_or(routes_ref[0, r] == e, routes_ref[1, r] == e)
        found.append((named, taken))
        taken = taken + named.astype(jnp.int32)
    return found


def dispatch_kernel(tokens_hbm, routes_hbm, gates_hbm, sends_ref, table_ref, tokens_ref, routes_ref, gates_ref, sems):
    copies = [
        pltpu.make_async_copy(routes_hbm, routes_ref, sems.at[0]),
        pltpu.make_async_copy(gates_hbm, gates_ref, sems.at[1]),
        pltpu.make_async_copy(tokens_hbm, tokens_ref, sems.at[2]),
    ]
    for copy in copies:
        copy.start()
    for copy in copies:
        copy.wait()
    tokens = tokens_ref[...].astype(jnp.float32)
    rows = tokens.shape[0]
    tiles = sends_ref.shape[0] // 2
    for e in range(2):
        found = slot_rows(routes_ref, e, rows)
        base = e * (1 + SLOTS)
        line = (1, table_ref.shape[2])
        for r in range(rows):
            weight = jnp.where(routes_ref[0, r] == e, gates_ref[0, r], 0.0)
            weight = weight + jnp.where(routes_ref[1, r] == e, gates_ref[1, r], 0.0)
            table_ref[base, r:r + 1, :] = jnp.full(line, weight, jnp.float32)
        slots = []
        for c in range(SLOTS):
            row = jnp.zeros((1, tokens.shape[1]), jnp.float32)
            for r, (named, slot) in enumerate(found):
                here = jnp.logical_and(named, slot == c).astype(jnp.float32)
                row = row + here * tokens[r:r + 1, :]
                table_ref[base + 1 + c, r:r + 1, :] = jnp.full(line, here, jnp.float32)
            slots.append(row)
        block = jnp.concatenate(slots, axis=0).astype(jnp.bfloat16)
        for t in range(tiles):
            sends_ref[e * tiles + t] = block


def merge_kernel(blocks_ref, rows_ref):
    rows_ref[...] = blocks_ref[...].reshape(rows_ref.shape)


def project(rows_ref, w_ref, columns):
    slots, half = rows_ref.shape[0] // 2, rows_ref.shape[1]
    total = jnp.dot(rows_ref[:slots, :], w_ref[0, :half, columns], preferred_element_type=jnp.float32)
    return total + jnp.dot(rows_ref[slots:, :], w_ref[0, half:, columns], preferred_element_type=jnp.float32)


def over_columns(width, body):
    tile = 256

    def step(i, carry):
        body(pl.ds(pl.multiple_of(i * tile, tile), tile))
        return carry

    lax.fori_loop(0, width // tile, step, 0, unroll=8)


def gate_kernel(rows_ref, w_ref, out_ref):
    def body(columns):
        out_ref[:, columns] = project(rows_ref, w_ref, columns)

    over_columns(out_ref.shape[1], body)


def hidden_kernel(rows_ref, w_ref, gate_ref, hidden_ref):
    def body(columns):
        up = project(rows_ref, w_ref, columns)
        gate = gate_ref[:, columns]
        hidden_ref[:, columns] = (gate / (1.0 + jnp.exp(-gate)) * up).astype(jnp.bfloat16)

    over_columns(hidden_ref.shape[1], body)


def join_kernel(first_ref, second_ref, out_ref):
    out_ref[0] = first_ref[...]
    out_ref[1] = second_ref[...]


def down_kernel(held, steps, first, last, *refs):
    blocks, w_ref, rest = refs[:held], refs[held], refs[held + 1:]
    if held < len(steps):
        blocks = [blocks[0].at[i] for i in range(len(steps))]
    out_ref = rest[-1]
    me = lax.axis_index("tile")
    slots, width = blocks[0].shape
    total = None if first else rest[0][...]
    for step, block in zip(steps, blocks):
        columns = pl.ds(pl.multiple_of((me ^ step) * width, width), width)
        term = lax.dot_general(
            w_ref[0, :, columns], block[...], (((1,), (1,)), ((), ())), preferred_element_type=jnp.float32)
        total = term if total is None else total + term
    if not last:
        out_ref[...] = total
    else:
        total = total.T
        for t in range(out_ref.shape[0]):
            out_ref[t] = total[t * SLOTS:(t + 1) * SLOTS, :]


def combine_kernel(own_ref, other_ref, table_ref, out_ref):
    mine = lax.axis_index("expert")
    halves, features = own_ref.shape[0] // 2, own_ref.shape[2]
    weight = [table_ref[e * (1 + SLOTS)][:, :1] for e in range(2)]
    inside = [[table_ref[e * (1 + SLOTS) + 1 + c][:, :1] for c in range(SLOTS)] for e in range(2)]
    for i in range(halves):
        own, other = own_ref[mine * halves + i], other_ref[mine * halves + i]
        mixed = jnp.zeros((out_ref.shape[0], features), jnp.float32)
        for e in range(2):
            both = jnp.where(mine == e, own, other)
            for c in range(SLOTS):
                value = (weight[e] * both[c:c + 1]).astype(jnp.bfloat16).astype(jnp.float32)
                mixed = mixed + jnp.where(inside[e][c] != 0.0, value, 0.0)
        out_ref[:, i * features:(i + 1) * features] = mixed.astype(jnp.bfloat16)


def local_direct(tokens, routes, gates, w_gate, w_up, w_down):
    tiles = lax.axis_size("tile")
    rows, half_width = tokens.shape
    width, features = w_gate.shape[2], w_down.shape[1]
    slots = tiles * SLOTS
    routes, gates = routes.T, gates.T

    def swap(x, bit):
        return lax.ppermute(x, "tile", [(t, t ^ bit) for t in range(tiles)])

    def to_core(x):
        return lax.ppermute(x, "expert", [(0, 1), (1, 0)])

    f32 = lambda *shape: jax.ShapeDtypeStruct(shape, jnp.float32)
    bf16 = lambda *shape: jax.ShapeDtypeStruct(shape, jnp.bfloat16)
    sends, table = call(
        dispatch_kernel, "dispatch",
        (bf16(2 * tiles, SLOTS, half_width), f32(2 * (1 + SLOTS), rows, 128)), [ANY] * 3, 4 * MIB, 600e-6,
        [
            pltpu.VMEM((rows, half_width), jnp.bfloat16),
            pltpu.SMEM((2, rows), jnp.int32),
            pltpu.SMEM((2, rows), jnp.float32),
            pltpu.SemaphoreType.DMA((3,)),
        ],
    )(in_hbm(tokens), in_hbm(routes), in_hbm(gates))
    blocks = lax.all_to_all(sends, ("expert", "tile"), split_axis=0, concat_axis=0, tiled=True)
    x = call(merge_kernel, "merge", bf16(2 * slots, half_width), [VMEM], 4 * MIB, 0e-6)(blocks)
    gate = call(gate_kernel, "gate", f32(slots, width), [VMEM] * 2, 4 * MIB, 0e-6)(x, in_vmem(w_gate))
    hidden = call(hidden_kernel, "hidden", bf16(slots, width), [VMEM] * 3, 4 * MIB, 200e-6)(x, in_vmem(w_up), gate)

    def down(total, steps, blocks, last):
        first = total is None
        out = f32(tiles, SLOTS, features) if last else f32(features, slots)
        return call(
            functools.partial(down_kernel, len(blocks), steps, first, last), "down", out,
            [VMEM] * (len(blocks) + 2 - first), 10 * MIB, 0e-6,
        )(*blocks, in_vmem(w_down), *(() if first else (total,)))

    beside, near, middle, far = (swap(hidden, k) for k in (1, 2, 4, 6))
    near_beside = swap(near, 1)
    total = down(None, [0, 1], [hidden, beside], False)
    total, middle, far, near_beside = lax.optimization_barrier((total, middle, far, near_beside))
    joined = call(join_kernel, "join", bf16(2, slots, width), [VMEM] * 2, 4 * MIB)(middle, far)
    joined_beside = swap(joined, 1)
    total = down(total, [4, 6], [joined], False)
    total = down(total, [2, 3], [near, near_beside], False)
    result = down(total, [5, 7], [joined_beside], True)
    back = lax.all_to_all(result, "tile", split_axis=0, concat_axis=0, tiled=True)
    return call(combine_kernel, "combine", bf16(rows, half_width), [VMEM] * 3, 4 * MIB)(back, to_core(back), table)


def local_gathered(tokens, routes, gates, w_gate, w_up, w_down):
    experts = lax.axis_size("expert")
    tile_count = lax.axis_size("tile")
    own_expert = lax.axis_index("expert")
    half_width = tokens.shape[1]
    tok_rows = tokens.shape[0]
    slot_count = max(2, tok_rows // 2)
    window_ids = lax.broadcasted_iota(jnp.int32, (1, 1, experts), 2)
    is_named = routes[:, :, None] == window_ids
    chosen = jnp.any(is_named, axis=1)
    weight = jnp.sum(jnp.where(is_named, gates[:, :, None], jnp.float32(0.0)), axis=1)
    position = jnp.cumsum(chosen.astype(jnp.int32), axis=0) - 1
    slot_ids = lax.broadcasted_iota(jnp.int32, (1, slot_count, 1), 1)
    dispatch = jnp.logical_and(chosen.T[:, None, :], position.T[:, None, :] == slot_ids)
    placing = dispatch.astype(jnp.bfloat16)
    outgoing = jnp.einsum(
        "ecr,rd->ecd", placing, tokens, preferred_element_type=jnp.float32
    ).astype(jnp.bfloat16)
    slot_weight = jnp.einsum("ecr,re->ec", dispatch.astype(jnp.float32), weight)
    everything = lax.all_gather(outgoing[None], ("expert", "tile"), axis=0, tiled=True)
    picked = lax.dynamic_slice_in_dim(everything, own_expert, 1, 1)[:, 0]
    picked = picked.reshape(experts, tile_count, slot_count, half_width)
    gathered = jnp.transpose(picked, (1, 2, 0, 3)).reshape(
        tile_count * slot_count, experts * half_width
    )
    gate_proj = jnp.dot(gathered, w_gate[0], preferred_element_type=jnp.float32)
    up_proj = jnp.dot(gathered, w_up[0], preferred_element_type=jnp.float32)
    hidden = (jax.nn.silu(gate_proj) * up_proj).astype(jnp.bfloat16)
    columns = w_down[0]
    summed = lax.dot_general(
        columns,
        lax.all_gather(hidden, "tile", axis=1, tiled=True),
        (((1,), (1,)), ((), ())),
        preferred_element_type=jnp.float32,
    )
    homeward = lax.all_to_all(summed, "tile", split_axis=1, concat_axis=0, tiled=True)
    returned = lax.all_to_all(homeward, "expert", split_axis=0, concat_axis=1, tiled=True)
    contribution = (slot_weight.reshape(1, experts * slot_count) * returned).astype(jnp.bfloat16)
    flat_places = placing.reshape(experts * slot_count, tok_rows)
    return jnp.einsum(
        "st,ds->td", flat_places, contribution, preferred_element_type=jnp.float32
    ).astype(jnp.bfloat16)


def solution(mesh):
    in_specs = (
        P(("group", "tile"), "expert"),
        P(("group", "tile"), None),
        P(("group", "tile"), None),
        P("expert", None, "tile"),
        P("expert", None, "tile"),
        P("expert", "tile", None),
    )
    out_specs = P(("group", "tile"), "expert")
    local = local_direct if mesh.shape["tile"] == 8 else local_gathered
    return jax.shard_map(local, mesh=mesh, in_specs=in_specs, out_specs=out_specs, check_vma=False)
```

```python
import functools

import jax
import jax.numpy as jnp
from jax import lax
from jax.experimental import pallas as pl
from jax.experimental.pallas import tpu as pltpu
from jax.sharding import PartitionSpec as P

MIB = 1 << 20
SLOTS = 2
VMEM = pl.BlockSpec(memory_space=pltpu.VMEM)
ANY = pl.BlockSpec(memory_space=pl.ANY)


def in_vmem(x):
    return pltpu.with_memory_space_constraint(x, pltpu.VMEM)


def in_hbm(x):
    return pltpu.with_memory_space_constraint(x, pltpu.HBM)


def call(kernel, name, out, in_specs, limit, seconds=0.0, scratch=()):
    return pl.pallas_call(
        kernel,
        out_shape=out,
        in_specs=in_specs,
        out_specs=jax.tree.map(lambda _: VMEM, out),
        scratch_shapes=scratch,
        compiler_params=pltpu.CompilerParams(vmem_limit_bytes=limit),
        cost_estimate=pl.CostEstimate(flops=int(seconds*1e15), bytes_accessed=0, transcendentals=0),
        name=name,
    )


def slot_rows(routes_ref, e, rows):
    taken = jnp.int32(0)
    found = []
    for r in range(rows):
        named = jnp.logical_or(routes_ref[0, r] == e, routes_ref[1, r] == e)
        found.append((named, taken))
        taken = taken + named.astype(jnp.int32)
    return found


def dispatch_kernel(tokens_hbm, routes_hbm, gates_hbm, sends_ref, table_ref, tokens_ref, routes_ref, gates_ref, sems):
    copies = [
        pltpu.make_async_copy(routes_hbm, routes_ref, sems.at[0]),
        pltpu.make_async_copy(gates_hbm, gates_ref, sems.at[1]),
        pltpu.make_async_copy(tokens_hbm, tokens_ref, sems.at[2]),
    ]
    for copy in copies:
        copy.start()
    for copy in copies:
        copy.wait()
    tokens = tokens_ref[...].astype(jnp.float32)
    rows = tokens.shape[0]
    tiles = sends_ref.shape[0] // 2
    for e in range(2):
        found = slot_rows(routes_ref, e, rows)
        base = e * (1 + SLOTS)
        line = (1, table_ref.shape[2])
        for r in range(rows):
            weight = jnp.where(routes_ref[0, r] == e, gates_ref[0, r], 0.0)
            weight = weight + jnp.where(routes_ref[1, r] == e, gates_ref[1, r], 0.0)
            table_ref[base, r:r + 1, :] = jnp.full(line, weight, jnp.float32)
        slots = []
        for c in range(SLOTS):
            row = jnp.zeros((1, tokens.shape[1]), jnp.float32)
            for r, (named, slot) in enumerate(found):
                here = jnp.logical_and(named, slot == c).astype(jnp.float32)
                row = row + here * tokens[r:r + 1, :]
                table_ref[base + 1 + c, r:r + 1, :] = jnp.full(line, here, jnp.float32)
            slots.append(row)
        block = jnp.concatenate(slots, axis=0).astype(jnp.bfloat16)
        for t in range(tiles):
            sends_ref[e * tiles + t] = block


def merge_kernel(blocks_ref, rows_ref):
    rows_ref[...] = blocks_ref[...].reshape(rows_ref.shape)


def project(rows_ref, w_ref, columns):
    slots, half = rows_ref.shape[0] // 2, rows_ref.shape[1]
    total = jnp.dot(rows_ref[:slots, :], w_ref[0, :half, columns], preferred_element_type=jnp.float32)
    return total + jnp.dot(rows_ref[slots:, :], w_ref[0, half:, columns], preferred_element_type=jnp.float32)


def over_columns(width, body):
    tile = 256

    def step(i, carry):
        body(pl.ds(pl.multiple_of(i * tile, tile), tile))
        return carry

    lax.fori_loop(0, width // tile, step, 0, unroll=8)


def gate_kernel(rows_ref, w_ref, out_ref):
    def body(columns):
        out_ref[:, columns] = project(rows_ref, w_ref, columns)

    over_columns(out_ref.shape[1], body)


def hidden_kernel(rows_ref, w_ref, gate_ref, hidden_ref):
    def body(columns):
        up = project(rows_ref, w_ref, columns)
        gate = gate_ref[:, columns]
        hidden_ref[:, columns] = (gate / (1.0 + jnp.exp(-gate)) * up).astype(jnp.bfloat16)

    over_columns(hidden_ref.shape[1], body)


def down_kernel(steps, first, last, *refs):
    n = len(steps)
    blocks, w_ref, rest = refs[:n], refs[n], refs[n + 1:]
    out_ref = rest[-1]
    me = lax.axis_index("tile")
    slots, width = blocks[0].shape
    total = None if first else rest[0][...]
    for step, block in zip(steps, blocks):
        columns = pl.ds(pl.multiple_of((me ^ step) * width, width), width)
        term = lax.dot_general(
            w_ref[0, :, columns], block[...], (((1,), (1,)), ((), ())), preferred_element_type=jnp.float32)
        total = term if total is None else total + term
    if not last:
        out_ref[...] = total
    else:
        total = total.T
        for t in range(out_ref.shape[0]):
            out_ref[t] = total[t * SLOTS:(t + 1) * SLOTS, :]


def combine_kernel(own_ref, other_ref, table_ref, out_ref):
    mine = lax.axis_index("expert")
    halves, features = own_ref.shape[0] // 2, own_ref.shape[2]
    weight = [table_ref[e * (1 + SLOTS)][:, :1] for e in range(2)]
    inside = [[table_ref[e * (1 + SLOTS) + 1 + c][:, :1] for c in range(SLOTS)] for e in range(2)]
    for i in range(halves):
        own, other = own_ref[mine * halves + i], other_ref[mine * halves + i]
        mixed = jnp.zeros((out_ref.shape[0], features), jnp.float32)
        for e in range(2):
            both = jnp.where(mine == e, own, other)
            for c in range(SLOTS):
                value = (weight[e] * both[c:c + 1]).astype(jnp.bfloat16).astype(jnp.float32)
                mixed = mixed + jnp.where(inside[e][c] != 0.0, value, 0.0)
        out_ref[:, i * features:(i + 1) * features] = mixed.astype(jnp.bfloat16)


def local_direct(tokens, routes, gates, w_gate, w_up, w_down):
    tiles = lax.axis_size("tile")
    rows, half_width = tokens.shape
    width, features = w_gate.shape[2], w_down.shape[1]
    slots = tiles * SLOTS
    routes, gates = routes.T, gates.T

    def swap(x, bit):
        return lax.ppermute(x, "tile", [(t, t ^ bit) for t in range(tiles)])

    def to_core(x):
        return lax.ppermute(x, "expert", [(0, 1), (1, 0)])

    f32 = lambda *shape: jax.ShapeDtypeStruct(shape, jnp.float32)
    bf16 = lambda *shape: jax.ShapeDtypeStruct(shape, jnp.bfloat16)
    sends, table = call(
        dispatch_kernel, "dispatch",
        (bf16(2 * tiles, SLOTS, half_width), f32(2 * (1 + SLOTS), rows, 128)), [ANY] * 3, 4 * MIB, 600e-6,
        [
            pltpu.VMEM((rows, half_width), jnp.bfloat16),
            pltpu.SMEM((2, rows), jnp.int32),
            pltpu.SMEM((2, rows), jnp.float32),
            pltpu.SemaphoreType.DMA((3,)),
        ],
    )(in_hbm(tokens), in_hbm(routes), in_hbm(gates))
    blocks = lax.all_to_all(sends, ("expert", "tile"), split_axis=0, concat_axis=0, tiled=True)
    x = call(merge_kernel, "merge", bf16(2 * slots, half_width), [VMEM], 4 * MIB, 0e-6)(blocks)
    gate = call(gate_kernel, "gate", f32(slots, width), [VMEM] * 2, 4 * MIB, 0e-6)(x, in_vmem(w_gate))
    hidden = call(hidden_kernel, "hidden", bf16(slots, width), [VMEM] * 3, 4 * MIB, 200e-6)(x, in_vmem(w_up), gate)

    def down(total, steps, block, last):
        first = total is None
        out = f32(tiles, SLOTS, features) if last else f32(features, slots)
        return call(
            functools.partial(down_kernel, steps, first, last), "down", out,
            [VMEM] * (len(steps) + 2 - first), 10 * MIB, 0e-6,
        )(*(block[k] for k in steps), in_vmem(w_down), *(() if first else (total,)))

    block = {0: hidden}
    for k in (4, 2, 1):
        block[k] = swap(hidden, k)
    block[3] = swap(block[2], 1)
    block[6] = swap(block[4], 2)
    block[5] = swap(block[4], 1)
    total = down(None, [0, 1], block, False)
    total, block[6] = lax.optimization_barrier((total, block[6]))
    block[7] = swap(block[6], 1)
    total = down(total, [2, 4], block, False)
    total = down(total, [3, 6], block, False)
    total = down(total, [5], block, False)
    result = down(total, [7], block, True)
    back = lax.all_to_all(result, "tile", split_axis=0, concat_axis=0, tiled=True)
    return call(combine_kernel, "combine", bf16(rows, half_width), [VMEM] * 3, 4 * MIB)(back, to_core(back), table)


def local_gathered(tokens, routes, gates, w_gate, w_up, w_down):
    experts = lax.axis_size("expert")
    tile_count = lax.axis_size("tile")
    own_expert = lax.axis_index("expert")
    half_width = tokens.shape[1]
    tok_rows = tokens.shape[0]
    slot_count = max(2, tok_rows // 2)
    window_ids = lax.broadcasted_iota(jnp.int32, (1, 1, experts), 2)
    is_named = routes[:, :, None] == window_ids
    chosen = jnp.any(is_named, axis=1)
    weight = jnp.sum(jnp.where(is_named, gates[:, :, None], jnp.float32(0.0)), axis=1)
    position = jnp.cumsum(chosen.astype(jnp.int32), axis=0) - 1
    slot_ids = lax.broadcasted_iota(jnp.int32, (1, slot_count, 1), 1)
    dispatch = jnp.logical_and(chosen.T[:, None, :], position.T[:, None, :] == slot_ids)
    placing = dispatch.astype(jnp.bfloat16)
    outgoing = jnp.einsum(
        "ecr,rd->ecd", placing, tokens, preferred_element_type=jnp.float32
    ).astype(jnp.bfloat16)
    slot_weight = jnp.einsum("ecr,re->ec", dispatch.astype(jnp.float32), weight)
    everything = lax.all_gather(outgoing[None], ("expert", "tile"), axis=0, tiled=True)
    picked = lax.dynamic_slice_in_dim(everything, own_expert, 1, 1)[:, 0]
    picked = picked.reshape(experts, tile_count, slot_count, half_width)
    gathered = jnp.transpose(picked, (1, 2, 0, 3)).reshape(
        tile_count * slot_count, experts * half_width
    )
    gate_proj = jnp.dot(gathered, w_gate[0], preferred_element_type=jnp.float32)
    up_proj = jnp.dot(gathered, w_up[0], preferred_element_type=jnp.float32)
    hidden = (jax.nn.silu(gate_proj) * up_proj).astype(jnp.bfloat16)
    columns = w_down[0]
    summed = lax.dot_general(
        columns,
        lax.all_gather(hidden, "tile", axis=1, tiled=True),
        (((1,), (1,)), ((), ())),
        preferred_element_type=jnp.float32,
    )
    homeward = lax.all_to_all(summed, "tile", split_axis=1, concat_axis=0, tiled=True)
    returned = lax.all_to_all(homeward, "expert", split_axis=0, concat_axis=1, tiled=True)
    contribution = (slot_weight.reshape(1, experts * slot_count) * returned).astype(jnp.bfloat16)
    flat_places = placing.reshape(experts * slot_count, tok_rows)
    return jnp.einsum(
        "st,ds->td", flat_places, contribution, preferred_element_type=jnp.float32
    ).astype(jnp.bfloat16)


def solution(mesh):
    in_specs = (
        P(("group", "tile"), "expert"),
        P(("group", "tile"), None),
        P(("group", "tile"), None),
        P("expert", None, "tile"),
        P("expert", None, "tile"),
        P("expert", "tile", None),
    )
    out_specs = P(("group", "tile"), "expert")
    local = local_direct if mesh.shape["tile"] == 8 else local_gathered
    return jax.shard_map(local, mesh=mesh, in_specs=in_specs, out_specs=out_specs, check_vma=False)
```

```python
import functools

import jax
import jax.numpy as jnp
from jax import lax
from jax.experimental import pallas as pl
from jax.experimental.pallas import tpu as pltpu
from jax.sharding import PartitionSpec as P

MIB = 1 << 20
SLOTS = 2
VMEM = pl.BlockSpec(memory_space=pltpu.VMEM)
ANY = pl.BlockSpec(memory_space=pl.ANY)


def in_vmem(x):
    return pltpu.with_memory_space_constraint(x, pltpu.VMEM)


def in_hbm(x):
    return pltpu.with_memory_space_constraint(x, pltpu.HBM)


def call(kernel, name, out, in_specs, limit, seconds=0.0, scratch=()):
    return pl.pallas_call(
        kernel,
        out_shape=out,
        in_specs=in_specs,
        out_specs=jax.tree.map(lambda _: VMEM, out),
        scratch_shapes=scratch,
        compiler_params=pltpu.CompilerParams(vmem_limit_bytes=limit),
        cost_estimate=pl.CostEstimate(flops=int(seconds*1e15), bytes_accessed=0, transcendentals=0),
        name=name,
    )


def slot_rows(routes_ref, e, rows):
    taken = jnp.int32(0)
    found = []
    for r in range(rows):
        named = jnp.logical_or(routes_ref[0, r] == e, routes_ref[1, r] == e)
        found.append((named, taken))
        taken = taken + named.astype(jnp.int32)
    return found


def dispatch_kernel(tokens_hbm, routes_hbm, gates_hbm, sends_ref, table_ref, tokens_ref, routes_ref, gates_ref, sems):
    copies = [
        pltpu.make_async_copy(routes_hbm, routes_ref, sems.at[0]),
        pltpu.make_async_copy(gates_hbm, gates_ref, sems.at[1]),
        pltpu.make_async_copy(tokens_hbm, tokens_ref, sems.at[2]),
    ]
    for copy in copies:
        copy.start()
    for copy in copies:
        copy.wait()
    tokens = tokens_ref[...].astype(jnp.float32)
    rows = tokens.shape[0]
    tiles = sends_ref.shape[0] // 2
    for e in range(2):
        found = slot_rows(routes_ref, e, rows)
        base = e * (1 + SLOTS)
        line = (1, table_ref.shape[2])
        for r in range(rows):
            weight = jnp.where(routes_ref[0, r] == e, gates_ref[0, r], 0.0)
            weight = weight + jnp.where(routes_ref[1, r] == e, gates_ref[1, r], 0.0)
            table_ref[base, r:r + 1, :] = jnp.full(line, weight, jnp.float32)
        slots = []
        for c in range(SLOTS):
            row = jnp.zeros((1, tokens.shape[1]), jnp.float32)
            for r, (named, slot) in enumerate(found):
                here = jnp.logical_and(named, slot == c).astype(jnp.float32)
                row = row + here * tokens[r:r + 1, :]
                table_ref[base + 1 + c, r:r + 1, :] = jnp.full(line, here, jnp.float32)
            slots.append(row)
        block = jnp.concatenate(slots, axis=0).astype(jnp.bfloat16)
        for t in range(tiles):
            sends_ref[e * tiles + t] = block


def merge_kernel(blocks_ref, rows_ref):
    rows_ref[...] = blocks_ref[...].reshape(rows_ref.shape)


def project(rows_ref, w_ref, columns):
    slots, half = rows_ref.shape[0] // 2, rows_ref.shape[1]
    total = jnp.dot(rows_ref[:slots, :], w_ref[0, :half, columns], preferred_element_type=jnp.float32)
    return total + jnp.dot(rows_ref[slots:, :], w_ref[0, half:, columns], preferred_element_type=jnp.float32)


def over_columns(width, body):
    tile = 256

    def step(i, carry):
        body(pl.ds(pl.multiple_of(i * tile, tile), tile))
        return carry

    lax.fori_loop(0, width // tile, step, 0, unroll=8)


def gate_kernel(rows_ref, w_ref, out_ref):
    def body(columns):
        out_ref[:, columns] = project(rows_ref, w_ref, columns)

    over_columns(out_ref.shape[1], body)


def hidden_kernel(rows_ref, w_ref, gate_ref, hidden_ref):
    def body(columns):
        up = project(rows_ref, w_ref, columns)
        gate = gate_ref[:, columns]
        hidden_ref[:, columns] = (gate / (1.0 + jnp.exp(-gate)) * up).astype(jnp.bfloat16)

    over_columns(hidden_ref.shape[1], body)


def down_kernel(steps, first, last, *refs):
    n = len(steps)
    blocks, w_ref, rest = refs[:n], refs[n], refs[n + 1:]
    out_ref = rest[-1]
    me = lax.axis_index("tile")
    slots, width = blocks[0].shape
    total = None if first else rest[0][...]
    for step, block in zip(steps, blocks):
        columns = pl.ds(pl.multiple_of((me ^ step) * width, width), width)
        term = lax.dot_general(
            w_ref[0, :, columns], block[...], (((1,), (1,)), ((), ())), preferred_element_type=jnp.float32)
        total = term if total is None else total + term
    if not last:
        out_ref[...] = total
    else:
        total = total.T
        for t in range(out_ref.shape[0]):
            out_ref[t] = total[t * SLOTS:(t + 1) * SLOTS, :]


def combine_kernel(own_ref, other_ref, table_ref, out_ref):
    mine = lax.axis_index("expert")
    halves, features = own_ref.shape[0] // 2, own_ref.shape[2]
    weight = [table_ref[e * (1 + SLOTS)][:, :1] for e in range(2)]
    inside = [[table_ref[e * (1 + SLOTS) + 1 + c][:, :1] for c in range(SLOTS)] for e in range(2)]
    for i in range(halves):
        own, other = own_ref[mine * halves + i], other_ref[mine * halves + i]
        mixed = jnp.zeros((out_ref.shape[0], features), jnp.float32)
        for e in range(2):
            both = jnp.where(mine == e, own, other)
            for c in range(SLOTS):
                value = (weight[e] * both[c:c + 1]).astype(jnp.bfloat16).astype(jnp.float32)
                mixed = mixed + jnp.where(inside[e][c] != 0.0, value, 0.0)
        out_ref[:, i * features:(i + 1) * features] = mixed.astype(jnp.bfloat16)


def local_direct(tokens, routes, gates, w_gate, w_up, w_down):
    tiles = lax.axis_size("tile")
    rows, half_width = tokens.shape
    width, features = w_gate.shape[2], w_down.shape[1]
    slots = tiles * SLOTS
    routes, gates = routes.T, gates.T

    def swap(x, bit):
        return lax.ppermute(x, "tile", [(t, t ^ bit) for t in range(tiles)])

    def to_core(x):
        return lax.ppermute(x, "expert", [(0, 1), (1, 0)])

    f32 = lambda *shape: jax.ShapeDtypeStruct(shape, jnp.float32)
    bf16 = lambda *shape: jax.ShapeDtypeStruct(shape, jnp.bfloat16)
    sends, table = call(
        dispatch_kernel, "dispatch",
        (bf16(2 * tiles, SLOTS, half_width), f32(2 * (1 + SLOTS), rows, 128)), [ANY] * 3, 4 * MIB, 600e-6,
        [
            pltpu.VMEM((rows, half_width), jnp.bfloat16),
            pltpu.SMEM((2, rows), jnp.int32),
            pltpu.SMEM((2, rows), jnp.float32),
            pltpu.SemaphoreType.DMA((3,)),
        ],
    )(in_hbm(tokens), in_hbm(routes), in_hbm(gates))
    blocks = lax.all_to_all(sends, ("expert", "tile"), split_axis=0, concat_axis=0, tiled=True)
    x = call(merge_kernel, "merge", bf16(2 * slots, half_width), [VMEM], 4 * MIB, 0e-6)(blocks)
    gate = call(gate_kernel, "gate", f32(slots, width), [VMEM] * 2, 4 * MIB, 0e-6)(x, in_vmem(w_gate))
    hidden = call(hidden_kernel, "hidden", bf16(slots, width), [VMEM] * 3, 4 * MIB, 200e-6)(x, in_vmem(w_up), gate)

    def down(total, steps, block, last):
        first = total is None
        out = f32(tiles, SLOTS, features) if last else f32(features, slots)
        return call(
            functools.partial(down_kernel, steps, first, last), "down", out,
            [VMEM] * (len(steps) + 2 - first), 10 * MIB, 0e-6,
        )(*(block[k] for k in steps), in_vmem(w_down), *(() if first else (total,)))

    block = {0: hidden}
    for k in (4, 2, 1):
        block[k] = swap(hidden, k)
    block[3] = swap(block[2], 1)
    total = down(None, [0, 1], block, False)
    total, block[4] = lax.optimization_barrier((total, block[4]))
    block[6] = swap(block[4], 2)
    block[4], block[3] = lax.optimization_barrier((block[4], block[3]))
    block[5] = swap(block[4], 1)
    total = down(total, [2, 3], block, False)
    total, block[6] = lax.optimization_barrier((total, block[6]))
    block[7] = swap(block[6], 1)
    total = down(total, [4, 6], block, False)
    total = down(total, [5], block, False)
    result = down(total, [7], block, True)
    back = lax.all_to_all(result, "tile", split_axis=0, concat_axis=0, tiled=True)
    return call(combine_kernel, "combine", bf16(rows, half_width), [VMEM] * 3, 4 * MIB)(back, to_core(back), table)


def local_gathered(tokens, routes, gates, w_gate, w_up, w_down):
    experts = lax.axis_size("expert")
    tile_count = lax.axis_size("tile")
    own_expert = lax.axis_index("expert")
    half_width = tokens.shape[1]
    tok_rows = tokens.shape[0]
    slot_count = max(2, tok_rows // 2)
    window_ids = lax.broadcasted_iota(jnp.int32, (1, 1, experts), 2)
    is_named = routes[:, :, None] == window_ids
    chosen = jnp.any(is_named, axis=1)
    weight = jnp.sum(jnp.where(is_named, gates[:, :, None], jnp.float32(0.0)), axis=1)
    position = jnp.cumsum(chosen.astype(jnp.int32), axis=0) - 1
    slot_ids = lax.broadcasted_iota(jnp.int32, (1, slot_count, 1), 1)
    dispatch = jnp.logical_and(chosen.T[:, None, :], position.T[:, None, :] == slot_ids)
    placing = dispatch.astype(jnp.bfloat16)
    outgoing = jnp.einsum(
        "ecr,rd->ecd", placing, tokens, preferred_element_type=jnp.float32
    ).astype(jnp.bfloat16)
    slot_weight = jnp.einsum("ecr,re->ec", dispatch.astype(jnp.float32), weight)
    everything = lax.all_gather(outgoing[None], ("expert", "tile"), axis=0, tiled=True)
    picked = lax.dynamic_slice_in_dim(everything, own_expert, 1, 1)[:, 0]
    picked = picked.reshape(experts, tile_count, slot_count, half_width)
    gathered = jnp.transpose(picked, (1, 2, 0, 3)).reshape(
        tile_count * slot_count, experts * half_width
    )
    gate_proj = jnp.dot(gathered, w_gate[0], preferred_element_type=jnp.float32)
    up_proj = jnp.dot(gathered, w_up[0], preferred_element_type=jnp.float32)
    hidden = (jax.nn.silu(gate_proj) * up_proj).astype(jnp.bfloat16)
    columns = w_down[0]
    summed = lax.dot_general(
        columns,
        lax.all_gather(hidden, "tile", axis=1, tiled=True),
        (((1,), (1,)), ((), ())),
        preferred_element_type=jnp.float32,
    )
    homeward = lax.all_to_all(summed, "tile", split_axis=1, concat_axis=0, tiled=True)
    returned = lax.all_to_all(homeward, "expert", split_axis=0, concat_axis=1, tiled=True)
    contribution = (slot_weight.reshape(1, experts * slot_count) * returned).astype(jnp.bfloat16)
    flat_places = placing.reshape(experts * slot_count, tok_rows)
    return jnp.einsum(
        "st,ds->td", flat_places, contribution, preferred_element_type=jnp.float32
    ).astype(jnp.bfloat16)


def solution(mesh):
    in_specs = (
        P(("group", "tile"), "expert"),
        P(("group", "tile"), None),
        P(("group", "tile"), None),
        P("expert", None, "tile"),
        P("expert", None, "tile"),
        P("expert", "tile", None),
    )
    out_specs = P(("group", "tile"), "expert")
    local = local_direct if mesh.shape["tile"] == 8 else local_gathered
    return jax.shard_map(local, mesh=mesh, in_specs=in_specs, out_specs=out_specs, check_vma=False)
```

```python
import functools

import jax
import jax.numpy as jnp
from jax import lax
from jax.experimental import pallas as pl
from jax.experimental.pallas import tpu as pltpu
from jax.sharding import PartitionSpec as P

MIB = 1 << 20
SLOTS = 2
VMEM = pl.BlockSpec(memory_space=pltpu.VMEM)
ANY = pl.BlockSpec(memory_space=pl.ANY)


def in_vmem(x):
    return pltpu.with_memory_space_constraint(x, pltpu.VMEM)


def in_hbm(x):
    return pltpu.with_memory_space_constraint(x, pltpu.HBM)


def call(kernel, name, out, in_specs, limit, seconds=0.0, scratch=()):
    return pl.pallas_call(
        kernel,
        out_shape=out,
        in_specs=in_specs,
        out_specs=jax.tree.map(lambda _: VMEM, out),
        scratch_shapes=scratch,
        compiler_params=pltpu.CompilerParams(vmem_limit_bytes=limit),
        cost_estimate=pl.CostEstimate(flops=int(seconds*1e15), bytes_accessed=0, transcendentals=0),
        name=name,
    )


def slot_rows(routes_ref, e, rows):
    taken = jnp.int32(0)
    found = []
    for r in range(rows):
        named = jnp.logical_or(routes_ref[0, r] == e, routes_ref[1, r] == e)
        found.append((named, taken))
        taken = taken + named.astype(jnp.int32)
    return found


def dispatch_kernel(tokens_hbm, routes_hbm, gates_hbm, own_ref, other_ref, table_ref, tokens_ref, routes_ref, gates_ref, sems):
    copies = [
        pltpu.make_async_copy(routes_hbm, routes_ref, sems.at[0]),
        pltpu.make_async_copy(gates_hbm, gates_ref, sems.at[1]),
        pltpu.make_async_copy(tokens_hbm, tokens_ref, sems.at[2]),
    ]
    for copy in copies:
        copy.start()
    for copy in copies:
        copy.wait()
    tokens = tokens_ref[...].astype(jnp.float32)
    rows = tokens.shape[0]
    mine = lax.axis_index("expert")
    blocks = []
    for e in range(2):
        found = slot_rows(routes_ref, e, rows)
        base = e * (1 + SLOTS)
        line = (1, table_ref.shape[2])
        for r in range(rows):
            weight = jnp.where(routes_ref[0, r] == e, gates_ref[0, r], 0.0)
            weight = weight + jnp.where(routes_ref[1, r] == e, gates_ref[1, r], 0.0)
            table_ref[base, r:r + 1, :] = jnp.full(line, weight, jnp.float32)
        slots = []
        for c in range(SLOTS):
            row = jnp.zeros((1, tokens.shape[1]), jnp.float32)
            for r, (named, slot) in enumerate(found):
                here = jnp.logical_and(named, slot == c).astype(jnp.float32)
                row = row + here * tokens[r:r + 1, :]
                table_ref[base + 1 + c, r:r + 1, :] = jnp.full(line, here, jnp.float32)
            slots.append(row)
        blocks.append(jnp.concatenate(slots, axis=0).astype(jnp.bfloat16))
    own_ref[...] = jnp.where(mine == 0, blocks[0], blocks[1])
    other_ref[...] = jnp.where(mine == 0, blocks[1], blocks[0])


def pack_kernel(own_ref, got_ref, sends_ref):
    mine = lax.axis_index("expert")
    own, got = own_ref[...].astype(jnp.float32), got_ref[...].astype(jnp.float32)
    block = jnp.concatenate([jnp.where(mine == 0, own, got), jnp.where(mine == 0, got, own)], axis=0)
    for t in range(sends_ref.shape[0]):
        sends_ref[t] = block.astype(jnp.bfloat16)


def merge_kernel(blocks_ref, rows_ref, first_ref, second_ref):
    for t in range(blocks_ref.shape[0]):
        rows = blocks_ref[t].astype(jnp.float32)
        first_ref[t] = rows[:SLOTS]
        second_ref[t] = rows[SLOTS:]
    slots, half = rows_ref.shape[0] // 2, rows_ref.shape[1]
    rows_ref[:slots, :] = first_ref[...].reshape(slots, half).astype(jnp.bfloat16)
    rows_ref[slots:, :] = second_ref[...].reshape(slots, half).astype(jnp.bfloat16)


def project(rows_ref, w_ref, columns):
    slots, half = rows_ref.shape[0] // 2, rows_ref.shape[1]
    total = jnp.dot(rows_ref[:slots, :], w_ref[0, :half, columns], preferred_element_type=jnp.float32)
    return total + jnp.dot(rows_ref[slots:, :], w_ref[0, half:, columns], preferred_element_type=jnp.float32)


def over_columns(width, body):
    tile = 256

    def step(i, carry):
        body(pl.ds(pl.multiple_of(i * tile, tile), tile))
        return carry

    lax.fori_loop(0, width // tile, step, 0, unroll=8)


def gate_kernel(rows_ref, w_ref, out_ref):
    def body(columns):
        out_ref[:, columns] = project(rows_ref, w_ref, columns)

    over_columns(out_ref.shape[1], body)


def hidden_kernel(rows_ref, w_ref, gate_ref, hidden_ref):
    def body(columns):
        up = project(rows_ref, w_ref, columns)
        gate = gate_ref[:, columns]
        hidden_ref[:, columns] = (gate / (1.0 + jnp.exp(-gate)) * up).astype(jnp.bfloat16)

    over_columns(hidden_ref.shape[1], body)


def down_kernel(steps, first, last, *refs):
    n = len(steps)
    blocks, w_ref, rest = refs[:n], refs[n], refs[n + 1:]
    out_ref = rest[-1]
    me = lax.axis_index("tile")
    slots, width = blocks[0].shape
    total = None if first else rest[0][...]
    for step, block in zip(steps, blocks):
        columns = pl.ds(pl.multiple_of((me ^ step) * width, width), width)
        term = lax.dot_general(
            w_ref[0, :, columns], block[...], (((1,), (1,)), ((), ())), preferred_element_type=jnp.float32)
        total = term if total is None else total + term
    if not last:
        out_ref[...] = total
    else:
        total = total.T
        for t in range(out_ref.shape[0]):
            out_ref[t] = total[t * SLOTS:(t + 1) * SLOTS, :]


def combine_kernel(own_ref, other_ref, table_ref, out_ref):
    mine = lax.axis_index("expert")
    halves, features = own_ref.shape[0] // 2, own_ref.shape[2]
    weight = [table_ref[e * (1 + SLOTS)][:, :1] for e in range(2)]
    inside = [[table_ref[e * (1 + SLOTS) + 1 + c][:, :1] for c in range(SLOTS)] for e in range(2)]
    for i in range(halves):
        own, other = own_ref[mine * halves + i], other_ref[mine * halves + i]
        mixed = jnp.zeros((out_ref.shape[0], features), jnp.float32)
        for e in range(2):
            both = jnp.where(mine == e, own, other)
            for c in range(SLOTS):
                value = (weight[e] * both[c:c + 1]).astype(jnp.bfloat16).astype(jnp.float32)
                mixed = mixed + jnp.where(inside[e][c] != 0.0, value, 0.0)
        out_ref[:, i * features:(i + 1) * features] = mixed.astype(jnp.bfloat16)


def local_direct(tokens, routes, gates, w_gate, w_up, w_down):
    tiles = lax.axis_size("tile")
    rows, half_width = tokens.shape
    width, features = w_gate.shape[2], w_down.shape[1]
    slots = tiles * SLOTS
    routes, gates = routes.T, gates.T

    def swap(x, bit):
        return lax.ppermute(x, "tile", [(t, t ^ bit) for t in range(tiles)])

    def to_core(x):
        return lax.ppermute(x, "expert", [(0, 1), (1, 0)])

    f32 = lambda *shape: jax.ShapeDtypeStruct(shape, jnp.float32)
    bf16 = lambda *shape: jax.ShapeDtypeStruct(shape, jnp.bfloat16)
    own, other, table = call(
        dispatch_kernel, "dispatch",
        (bf16(SLOTS, half_width), bf16(SLOTS, half_width), f32(2 * (1 + SLOTS), rows, 128)), [ANY] * 3, 4 * MIB, 600e-6,
        [
            pltpu.VMEM((rows, half_width), jnp.bfloat16),
            pltpu.SMEM((2, rows), jnp.int32),
            pltpu.SMEM((2, rows), jnp.float32),
            pltpu.SemaphoreType.DMA((3,)),
        ],
    )(in_hbm(tokens), in_hbm(routes), in_hbm(gates))
    sends = call(pack_kernel, "pack", bf16(tiles, 2 * SLOTS, half_width), [VMEM] * 2, 4 * MIB, 0e-6)(own, to_core(other))
    blocks = lax.all_to_all(sends, "tile", split_axis=0, concat_axis=0, tiled=True)
    x = call(
        merge_kernel, "merge", bf16(2 * slots, half_width), [VMEM], 4 * MIB, 0e-6,
        [pltpu.VMEM((tiles, SLOTS, half_width), jnp.float32)] * 2,
    )(blocks)
    gate = call(gate_kernel, "gate", f32(slots, width), [VMEM] * 2, 4 * MIB, 0e-6)(x, in_vmem(w_gate))
    hidden = call(hidden_kernel, "hidden", bf16(slots, width), [VMEM] * 3, 4 * MIB, 200e-6)(x, in_vmem(w_up), gate)

    def down(total, steps, block, last):
        first = total is None
        out = f32(tiles, SLOTS, features) if last else f32(features, slots)
        return call(
            functools.partial(down_kernel, steps, first, last), "down", out,
            [VMEM] * (len(steps) + 2 - first), 10 * MIB, 0e-6,
        )(*(block[k] for k in steps), in_vmem(w_down), *(() if first else (total,)))

    block = {0: hidden}
    for k in (4, 2, 1):
        block[k] = swap(hidden, k)
    block[3] = swap(block[2], 1)
    total = down(None, [0, 1], block, False)
    total, block[4] = lax.optimization_barrier((total, block[4]))
    block[6] = swap(block[4], 2)
    block[4], block[3] = lax.optimization_barrier((block[4], block[3]))
    block[5] = swap(block[4], 1)
    total = down(total, [2, 3], block, False)
    total, block[6] = lax.optimization_barrier((total, block[6]))
    block[7] = swap(block[6], 1)
    total = down(total, [4, 6], block, False)
    total = down(total, [5], block, False)
    result = down(total, [7], block, True)
    back = lax.all_to_all(result, "tile", split_axis=0, concat_axis=0, tiled=True)
    return call(combine_kernel, "combine", bf16(rows, half_width), [VMEM] * 3, 4 * MIB)(back, to_core(back), table)


def local_gathered(tokens, routes, gates, w_gate, w_up, w_down):
    experts = lax.axis_size("expert")
    tile_count = lax.axis_size("tile")
    own_expert = lax.axis_index("expert")
    half_width = tokens.shape[1]
    tok_rows = tokens.shape[0]
    slot_count = max(2, tok_rows // 2)
    window_ids = lax.broadcasted_iota(jnp.int32, (1, 1, experts), 2)
    is_named = routes[:, :, None] == window_ids
    chosen = jnp.any(is_named, axis=1)
    weight = jnp.sum(jnp.where(is_named, gates[:, :, None], jnp.float32(0.0)), axis=1)
    position = jnp.cumsum(chosen.astype(jnp.int32), axis=0) - 1
    slot_ids = lax.broadcasted_iota(jnp.int32, (1, slot_count, 1), 1)
    dispatch = jnp.logical_and(chosen.T[:, None, :], position.T[:, None, :] == slot_ids)
    placing = dispatch.astype(jnp.bfloat16)
    outgoing = jnp.einsum(
        "ecr,rd->ecd", placing, tokens, preferred_element_type=jnp.float32
    ).astype(jnp.bfloat16)
    slot_weight = jnp.einsum("ecr,re->ec", dispatch.astype(jnp.float32), weight)
    everything = lax.all_gather(outgoing[None], ("expert", "tile"), axis=0, tiled=True)
    picked = lax.dynamic_slice_in_dim(everything, own_expert, 1, 1)[:, 0]
    picked = picked.reshape(experts, tile_count, slot_count, half_width)
    gathered = jnp.transpose(picked, (1, 2, 0, 3)).reshape(
        tile_count * slot_count, experts * half_width
    )
    gate_proj = jnp.dot(gathered, w_gate[0], preferred_element_type=jnp.float32)
    up_proj = jnp.dot(gathered, w_up[0], preferred_element_type=jnp.float32)
    hidden = (jax.nn.silu(gate_proj) * up_proj).astype(jnp.bfloat16)
    columns = w_down[0]
    summed = lax.dot_general(
        columns,
        lax.all_gather(hidden, "tile", axis=1, tiled=True),
        (((1,), (1,)), ((), ())),
        preferred_element_type=jnp.float32,
    )
    homeward = lax.all_to_all(summed, "tile", split_axis=1, concat_axis=0, tiled=True)
    returned = lax.all_to_all(homeward, "expert", split_axis=0, concat_axis=1, tiled=True)
    contribution = (slot_weight.reshape(1, experts * slot_count) * returned).astype(jnp.bfloat16)
    flat_places = placing.reshape(experts * slot_count, tok_rows)
    return jnp.einsum(
        "st,ds->td", flat_places, contribution, preferred_element_type=jnp.float32
    ).astype(jnp.bfloat16)


def solution(mesh):
    in_specs = (
        P(("group", "tile"), "expert"),
        P(("group", "tile"), None),
        P(("group", "tile"), None),
        P("expert", None, "tile"),
        P("expert", None, "tile"),
        P("expert", "tile", None),
    )
    out_specs = P(("group", "tile"), "expert")
    local = local_direct if mesh.shape["tile"] == 8 else local_gathered
    return jax.shard_map(local, mesh=mesh, in_specs=in_specs, out_specs=out_specs, check_vma=False)
```

```python
import functools

import jax
import jax.numpy as jnp
from jax import lax
from jax.experimental import pallas as pl
from jax.experimental.pallas import tpu as pltpu
from jax.sharding import PartitionSpec as P

MIB = 1 << 20
SLOTS = 2
VMEM = pl.BlockSpec(memory_space=pltpu.VMEM)
ANY = pl.BlockSpec(memory_space=pl.ANY)


def in_vmem(x):
    return pltpu.with_memory_space_constraint(x, pltpu.VMEM)


def in_hbm(x):
    return pltpu.with_memory_space_constraint(x, pltpu.HBM)


def call(kernel, name, out, in_specs, limit, seconds=0.0, scratch=()):
    return pl.pallas_call(
        kernel,
        out_shape=out,
        in_specs=in_specs,
        out_specs=jax.tree.map(lambda _: VMEM, out),
        scratch_shapes=scratch,
        compiler_params=pltpu.CompilerParams(vmem_limit_bytes=limit),
        cost_estimate=pl.CostEstimate(flops=int(seconds*1e15), bytes_accessed=0, transcendentals=0),
        name=name,
    )


def slot_rows(routes_ref, e, rows):
    taken = jnp.int32(0)
    found = []
    for r in range(rows):
        named = jnp.logical_or(routes_ref[0, r] == e, routes_ref[1, r] == e)
        found.append((named, taken))
        taken = taken + named.astype(jnp.int32)
    return found


def dispatch_kernel(tokens_hbm, routes_hbm, gates_hbm, sends_ref, table_ref, tokens_ref, routes_ref, gates_ref, sems):
    copies = [
        pltpu.make_async_copy(routes_hbm, routes_ref, sems.at[0]),
        pltpu.make_async_copy(gates_hbm, gates_ref, sems.at[1]),
        pltpu.make_async_copy(tokens_hbm, tokens_ref, sems.at[2]),
    ]
    for copy in copies:
        copy.start()
    for copy in copies:
        copy.wait()
    tokens = tokens_ref[...].astype(jnp.float32)
    rows = tokens.shape[0]
    tiles = sends_ref.shape[0] // 2
    for e in range(2):
        found = slot_rows(routes_ref, e, rows)
        base = e * (1 + SLOTS)
        line = (1, table_ref.shape[2])
        for r in range(rows):
            weight = jnp.where(routes_ref[0, r] == e, gates_ref[0, r], 0.0)
            weight = weight + jnp.where(routes_ref[1, r] == e, gates_ref[1, r], 0.0)
            table_ref[base, r:r + 1, :] = jnp.full(line, weight, jnp.float32)
        slots = []
        for c in range(SLOTS):
            row = jnp.zeros((1, tokens.shape[1]), jnp.float32)
            for r, (named, slot) in enumerate(found):
                here = jnp.logical_and(named, slot == c).astype(jnp.float32)
                row = row + here * tokens[r:r + 1, :]
                table_ref[base + 1 + c, r:r + 1, :] = jnp.full(line, here, jnp.float32)
            slots.append(row)
        block = jnp.concatenate(slots, axis=0).astype(jnp.bfloat16)
        for t in range(tiles):
            sends_ref[e * tiles + t] = block


def merge_kernel(blocks_ref, rows_ref):
    rows_ref[...] = blocks_ref[...].reshape(rows_ref.shape)


def project(rows_ref, w_ref, columns):
    slots, half = rows_ref.shape[0] // 2, rows_ref.shape[1]
    total = jnp.dot(rows_ref[:slots, :], w_ref[0, :half, columns], preferred_element_type=jnp.float32)
    return total + jnp.dot(rows_ref[slots:, :], w_ref[0, half:, columns], preferred_element_type=jnp.float32)


def over_columns(width, body):
    tile = 256

    def step(i, carry):
        body(pl.ds(pl.multiple_of(i * tile, tile), tile))
        return carry

    lax.fori_loop(0, width // tile, step, 0, unroll=8)


def gate_kernel(rows_ref, w_ref, out_ref):
    def body(columns):
        out_ref[:, columns] = project(rows_ref, w_ref, columns)

    over_columns(out_ref.shape[1], body)


def hidden_kernel(rows_ref, w_ref, gate_ref, hidden_ref):
    def body(columns):
        up = project(rows_ref, w_ref, columns)
        gate = gate_ref[:, columns]
        hidden_ref[:, columns] = (gate / (1.0 + jnp.exp(-gate)) * up).astype(jnp.bfloat16)

    over_columns(hidden_ref.shape[1], body)


def down_kernel(steps, first, last, *refs):
    n = len(steps)
    blocks, w_ref, rest = refs[:n], refs[n], refs[n + 1:]
    out_ref = rest[-1]
    me = lax.axis_index("tile")
    slots, width = blocks[0].shape
    total = None if first else rest[0][...]
    for step, block in zip(steps, blocks):
        columns = pl.ds(pl.multiple_of((me ^ step) * width, width), width)
        term = lax.dot_general(
            w_ref[0, :, columns], block[...], (((1,), (1,)), ((), ())), preferred_element_type=jnp.float32)
        total = term if total is None else total + term
    if not last:
        out_ref[...] = total
    else:
        total = total.T
        for t in range(out_ref.shape[0]):
            out_ref[t] = total[t * SLOTS:(t + 1) * SLOTS, :]


def combine_kernel(own_ref, other_ref, table_ref, out_ref):
    mine = lax.axis_index("expert")
    halves, features = own_ref.shape[0] // 2, own_ref.shape[2]
    weight = [table_ref[e * (1 + SLOTS)][:, :1] for e in range(2)]
    inside = [[table_ref[e * (1 + SLOTS) + 1 + c][:, :1] for c in range(SLOTS)] for e in range(2)]
    for i in range(halves):
        own, other = own_ref[mine * halves + i], other_ref[mine * halves + i]
        mixed = jnp.zeros((out_ref.shape[0], features), jnp.float32)
        for e in range(2):
            both = jnp.where(mine == e, own, other)
            for c in range(SLOTS):
                value = (weight[e] * both[c:c + 1]).astype(jnp.bfloat16).astype(jnp.float32)
                mixed = mixed + jnp.where(inside[e][c] != 0.0, value, 0.0)
        out_ref[:, i * features:(i + 1) * features] = mixed.astype(jnp.bfloat16)


def local_direct(tokens, routes, gates, w_gate, w_up, w_down):
    tiles = lax.axis_size("tile")
    rows, half_width = tokens.shape
    width, features = w_gate.shape[2], w_down.shape[1]
    slots = tiles * SLOTS
    routes, gates = routes.T, gates.T

    def swap(x, bit):
        return lax.ppermute(x, "tile", [(t, t ^ bit) for t in range(tiles)])

    def to_core(x):
        return lax.ppermute(x, "expert", [(0, 1), (1, 0)])

    f32 = lambda *shape: jax.ShapeDtypeStruct(shape, jnp.float32)
    bf16 = lambda *shape: jax.ShapeDtypeStruct(shape, jnp.bfloat16)
    sends, table = call(
        dispatch_kernel, "dispatch",
        (bf16(2 * tiles, SLOTS, half_width), f32(2 * (1 + SLOTS), rows, 128)), [ANY] * 3, 4 * MIB, 600e-6,
        [
            pltpu.VMEM((rows, half_width), jnp.bfloat16),
            pltpu.SMEM((2, rows), jnp.int32),
            pltpu.SMEM((2, rows), jnp.float32),
            pltpu.SemaphoreType.DMA((3,)),
        ],
    )(in_hbm(tokens), in_hbm(routes), in_hbm(gates))
    blocks = lax.all_to_all(sends, ("expert", "tile"), split_axis=0, concat_axis=0, tiled=True)
    x = call(merge_kernel, "merge", bf16(2 * slots, half_width), [VMEM], 4 * MIB, 0e-6)(blocks)
    gate = call(gate_kernel, "gate", f32(slots, width), [VMEM] * 2, 4 * MIB, 0e-6)(x, in_vmem(w_gate))
    hidden = call(hidden_kernel, "hidden", bf16(slots, width), [VMEM] * 3, 4 * MIB, 200e-6)(x, in_vmem(w_up), gate)

    def down(total, steps, block, last):
        first = total is None
        out = f32(tiles, SLOTS, features) if last else f32(features, slots)
        return call(
            functools.partial(down_kernel, steps, first, last), "down", out,
            [VMEM] * (len(steps) + 2 - first), 10 * MIB, 2e-6,
        )(*(block[k] for k in steps), in_vmem(w_down), *(() if first else (total,)))

    block = {0: hidden}
    for k in (2, 1, 6, 4):
        block[k] = swap(hidden, k)
    block[3] = swap(block[2], 1)
    total = down(None, [0, 1], block, False)
    total, block[6], block[3] = lax.optimization_barrier((total, block[6], block[3]))
    block[7] = swap(block[6], 1)
    total = down(total, [2, 3], block, False)
    total, block[4] = lax.optimization_barrier((total, block[4]))
    block[5] = swap(block[4], 1)
    total = down(total, [6, 7], block, False)
    result = down(total, [4, 5], block, True)
    back = lax.all_to_all(result, "tile", split_axis=0, concat_axis=0, tiled=True)
    return call(combine_kernel, "combine", bf16(rows, half_width), [VMEM] * 3, 4 * MIB)(back, to_core(back), table)


def local_gathered(tokens, routes, gates, w_gate, w_up, w_down):
    experts = lax.axis_size("expert")
    tile_count = lax.axis_size("tile")
    own_expert = lax.axis_index("expert")
    half_width = tokens.shape[1]
    tok_rows = tokens.shape[0]
    slot_count = max(2, tok_rows // 2)
    window_ids = lax.broadcasted_iota(jnp.int32, (1, 1, experts), 2)
    is_named = routes[:, :, None] == window_ids
    chosen = jnp.any(is_named, axis=1)
    weight = jnp.sum(jnp.where(is_named, gates[:, :, None], jnp.float32(0.0)), axis=1)
    position = jnp.cumsum(chosen.astype(jnp.int32), axis=0) - 1
    slot_ids = lax.broadcasted_iota(jnp.int32, (1, slot_count, 1), 1)
    dispatch = jnp.logical_and(chosen.T[:, None, :], position.T[:, None, :] == slot_ids)
    placing = dispatch.astype(jnp.bfloat16)
    outgoing = jnp.einsum(
        "ecr,rd->ecd", placing, tokens, preferred_element_type=jnp.float32
    ).astype(jnp.bfloat16)
    slot_weight = jnp.einsum("ecr,re->ec", dispatch.astype(jnp.float32), weight)
    everything = lax.all_gather(outgoing[None], ("expert", "tile"), axis=0, tiled=True)
    picked = lax.dynamic_slice_in_dim(everything, own_expert, 1, 1)[:, 0]
    picked = picked.reshape(experts, tile_count, slot_count, half_width)
    gathered = jnp.transpose(picked, (1, 2, 0, 3)).reshape(
        tile_count * slot_count, experts * half_width
    )
    gate_proj = jnp.dot(gathered, w_gate[0], preferred_element_type=jnp.float32)
    up_proj = jnp.dot(gathered, w_up[0], preferred_element_type=jnp.float32)
    hidden = (jax.nn.silu(gate_proj) * up_proj).astype(jnp.bfloat16)
    columns = w_down[0]
    summed = lax.dot_general(
        columns,
        lax.all_gather(hidden, "tile", axis=1, tiled=True),
        (((1,), (1,)), ((), ())),
        preferred_element_type=jnp.float32,
    )
    homeward = lax.all_to_all(summed, "tile", split_axis=1, concat_axis=0, tiled=True)
    returned = lax.all_to_all(homeward, "expert", split_axis=0, concat_axis=1, tiled=True)
    contribution = (slot_weight.reshape(1, experts * slot_count) * returned).astype(jnp.bfloat16)
    flat_places = placing.reshape(experts * slot_count, tok_rows)
    return jnp.einsum(
        "st,ds->td", flat_places, contribution, preferred_element_type=jnp.float32
    ).astype(jnp.bfloat16)


def solution(mesh):
    in_specs = (
        P(("group", "tile"), "expert"),
        P(("group", "tile"), None),
        P(("group", "tile"), None),
        P("expert", None, "tile"),
        P("expert", None, "tile"),
        P("expert", "tile", None),
    )
    out_specs = P(("group", "tile"), "expert")
    local = local_direct if mesh.shape["tile"] == 8 else local_gathered
    return jax.shard_map(local, mesh=mesh, in_specs=in_specs, out_specs=out_specs, check_vma=False)
```

```python
import functools

import jax
import jax.numpy as jnp
from jax import lax
from jax.experimental import pallas as pl
from jax.experimental.pallas import tpu as pltpu
from jax.sharding import PartitionSpec as P

MIB = 1 << 20
SLOTS = 2
VMEM = pl.BlockSpec(memory_space=pltpu.VMEM)
ANY = pl.BlockSpec(memory_space=pl.ANY)


def in_vmem(x):
    return pltpu.with_memory_space_constraint(x, pltpu.VMEM)


def in_hbm(x):
    return pltpu.with_memory_space_constraint(x, pltpu.HBM)


def call(kernel, name, out, in_specs, limit, seconds=0.0, scratch=()):
    return pl.pallas_call(
        kernel,
        out_shape=out,
        in_specs=in_specs,
        out_specs=jax.tree.map(lambda _: VMEM, out),
        scratch_shapes=scratch,
        compiler_params=pltpu.CompilerParams(vmem_limit_bytes=limit),
        cost_estimate=pl.CostEstimate(flops=int(seconds*1e15), bytes_accessed=0, transcendentals=0),
        name=name,
    )


def slot_rows(routes_ref, e, rows):
    taken = jnp.int32(0)
    found = []
    for r in range(rows):
        named = jnp.logical_or(routes_ref[0, r] == e, routes_ref[1, r] == e)
        found.append((named, taken))
        taken = taken + named.astype(jnp.int32)
    return found


def dispatch_kernel(tokens_hbm, routes_hbm, gates_hbm, sends_ref, table_ref, tokens_ref, routes_ref, gates_ref, sems):
    copies = [
        pltpu.make_async_copy(routes_hbm, routes_ref, sems.at[0]),
        pltpu.make_async_copy(gates_hbm, gates_ref, sems.at[1]),
        pltpu.make_async_copy(tokens_hbm, tokens_ref, sems.at[2]),
    ]
    for copy in copies:
        copy.start()
    for copy in copies:
        copy.wait()
    tokens = tokens_ref[...].astype(jnp.float32)
    rows = tokens.shape[0]
    tiles = sends_ref.shape[0] // 2
    for e in range(2):
        found = slot_rows(routes_ref, e, rows)
        base = e * (1 + SLOTS)
        line = (1, table_ref.shape[2])
        for r in range(rows):
            weight = jnp.where(routes_ref[0, r] == e, gates_ref[0, r], 0.0)
            weight = weight + jnp.where(routes_ref[1, r] == e, gates_ref[1, r], 0.0)
            table_ref[base, r:r + 1, :] = jnp.full(line, weight, jnp.float32)
        slots = []
        for c in range(SLOTS):
            row = jnp.zeros((1, tokens.shape[1]), jnp.float32)
            for r, (named, slot) in enumerate(found):
                here = jnp.logical_and(named, slot == c).astype(jnp.float32)
                row = row + here * tokens[r:r + 1, :]
                table_ref[base + 1 + c, r:r + 1, :] = jnp.full(line, here, jnp.float32)
            slots.append(row)
        block = jnp.concatenate(slots, axis=0).astype(jnp.bfloat16)
        for t in range(tiles):
            sends_ref[e * tiles + t] = block


def merge_kernel(blocks_ref, rows_ref):
    rows_ref[...] = blocks_ref[...].reshape(rows_ref.shape)


def project(rows_ref, w_ref, columns):
    slots, half = rows_ref.shape[0] // 2, rows_ref.shape[1]
    total = jnp.dot(rows_ref[:slots, :], w_ref[0, :half, columns], preferred_element_type=jnp.float32)
    return total + jnp.dot(rows_ref[slots:, :], w_ref[0, half:, columns], preferred_element_type=jnp.float32)


def over_columns(width, body):
    tile = 256

    def step(i, carry):
        body(pl.ds(pl.multiple_of(i * tile, tile), tile))
        return carry

    lax.fori_loop(0, width // tile, step, 0, unroll=8)


def gate_kernel(rows_ref, w_ref, out_ref):
    def body(columns):
        out_ref[:, columns] = project(rows_ref, w_ref, columns)

    over_columns(out_ref.shape[1], body)


def hidden_kernel(rows_ref, w_ref, gate_ref, hidden_ref):
    def body(columns):
        up = project(rows_ref, w_ref, columns)
        gate = gate_ref[:, columns]
        hidden_ref[:, columns] = (gate / (1.0 + jnp.exp(-gate)) * up).astype(jnp.bfloat16)

    over_columns(hidden_ref.shape[1], body)


def join_kernel(first_ref, second_ref, out_ref):
    out_ref[0] = first_ref[...]
    out_ref[1] = second_ref[...]


def down_kernel(steps, first, last, *refs):
    blocks, w_ref, rest = [refs[0].at[i] for i in range(len(steps))], refs[1], refs[2:]
    out_ref = rest[-1]
    me = lax.axis_index("tile")
    slots, width = blocks[0].shape
    total = None if first else rest[0][...]
    for step, block in zip(steps, blocks):
        columns = pl.ds(pl.multiple_of((me ^ step) * width, width), width)
        term = lax.dot_general(
            w_ref[0, :, columns], block[...], (((1,), (1,)), ((), ())), preferred_element_type=jnp.float32)
        total = term if total is None else total + term
    if not last:
        out_ref[...] = total
    else:
        total = total.T
        for t in range(out_ref.shape[0]):
            out_ref[t] = total[t * SLOTS:(t + 1) * SLOTS, :]


def combine_kernel(own_ref, other_ref, table_ref, out_ref):
    mine = lax.axis_index("expert")
    halves, features = own_ref.shape[0] // 2, own_ref.shape[2]
    weight = [table_ref[e * (1 + SLOTS)][:, :1] for e in range(2)]
    inside = [[table_ref[e * (1 + SLOTS) + 1 + c][:, :1] for c in range(SLOTS)] for e in range(2)]
    for i in range(halves):
        own, other = own_ref[mine * halves + i], other_ref[mine * halves + i]
        mixed = jnp.zeros((out_ref.shape[0], features), jnp.float32)
        for e in range(2):
            both = jnp.where(mine == e, own, other)
            for c in range(SLOTS):
                value = (weight[e] * both[c:c + 1]).astype(jnp.bfloat16).astype(jnp.float32)
                mixed = mixed + jnp.where(inside[e][c] != 0.0, value, 0.0)
        out_ref[:, i * features:(i + 1) * features] = mixed.astype(jnp.bfloat16)


def local_direct(tokens, routes, gates, w_gate, w_up, w_down):
    tiles = lax.axis_size("tile")
    rows, half_width = tokens.shape
    width, features = w_gate.shape[2], w_down.shape[1]
    slots = tiles * SLOTS
    routes, gates = routes.T, gates.T

    def swap(x, bit):
        return lax.ppermute(x, "tile", [(t, t ^ bit) for t in range(tiles)])

    def to_core(x):
        return lax.ppermute(x, "expert", [(0, 1), (1, 0)])

    f32 = lambda *shape: jax.ShapeDtypeStruct(shape, jnp.float32)
    bf16 = lambda *shape: jax.ShapeDtypeStruct(shape, jnp.bfloat16)
    sends, table = call(
        dispatch_kernel, "dispatch",
        (bf16(2 * tiles, SLOTS, half_width), f32(2 * (1 + SLOTS), rows, 128)), [ANY] * 3, 4 * MIB, 600e-6,
        [
            pltpu.VMEM((rows, half_width), jnp.bfloat16),
            pltpu.SMEM((2, rows), jnp.int32),
            pltpu.SMEM((2, rows), jnp.float32),
            pltpu.SemaphoreType.DMA((3,)),
        ],
    )(in_hbm(tokens), in_hbm(routes), in_hbm(gates))
    blocks = lax.all_to_all(sends, ("expert", "tile"), split_axis=0, concat_axis=0, tiled=True)
    x = call(merge_kernel, "merge", bf16(2 * slots, half_width), [VMEM], 4 * MIB, 0e-6)(blocks)
    gate = call(gate_kernel, "gate", f32(slots, width), [VMEM] * 2, 4 * MIB, 0e-6)(x, in_vmem(w_gate))
    hidden = call(hidden_kernel, "hidden", bf16(slots, width), [VMEM] * 3, 4 * MIB, 200e-6)(x, in_vmem(w_up), gate)

    def down(total, steps, blocks, last):
        first = total is None
        out = f32(tiles, SLOTS, features) if last else f32(features, slots)
        return call(
            functools.partial(down_kernel, steps, first, last), "down", out,
            [VMEM] * (3 - first), 10 * MIB, 2e-6,
        )(blocks, in_vmem(w_down), *(() if first else (total,)))

    def join(first, second):
        return call(join_kernel, "join", bf16(2, slots, width), [VMEM] * 2, 4 * MIB)(first, second)

    four = swap(hidden, 4)
    pair = join(hidden, swap(hidden, 1))
    near = swap(pair, 2)
    four, _ = lax.optimization_barrier((four, pair))
    five = swap(four, 1)
    total = down(None, [0, 1], pair, False)
    total, five = lax.optimization_barrier((total, five))
    middle = join(four, five)
    far = swap(middle, 2)
    total = down(total, [2, 3], near, False)
    total = down(total, [4, 5], middle, False)
    result = down(total, [6, 7], far, True)
    back = lax.all_to_all(result, "tile", split_axis=0, concat_axis=0, tiled=True)
    return call(combine_kernel, "combine", bf16(rows, half_width), [VMEM] * 3, 4 * MIB)(back, to_core(back), table)


def local_gathered(tokens, routes, gates, w_gate, w_up, w_down):
    experts = lax.axis_size("expert")
    tile_count = lax.axis_size("tile")
    own_expert = lax.axis_index("expert")
    half_width = tokens.shape[1]
    tok_rows = tokens.shape[0]
    slot_count = max(2, tok_rows // 2)
    window_ids = lax.broadcasted_iota(jnp.int32, (1, 1, experts), 2)
    is_named = routes[:, :, None] == window_ids
    chosen = jnp.any(is_named, axis=1)
    weight = jnp.sum(jnp.where(is_named, gates[:, :, None], jnp.float32(0.0)), axis=1)
    position = jnp.cumsum(chosen.astype(jnp.int32), axis=0) - 1
    slot_ids = lax.broadcasted_iota(jnp.int32, (1, slot_count, 1), 1)
    dispatch = jnp.logical_and(chosen.T[:, None, :], position.T[:, None, :] == slot_ids)
    placing = dispatch.astype(jnp.bfloat16)
    outgoing = jnp.einsum(
        "ecr,rd->ecd", placing, tokens, preferred_element_type=jnp.float32
    ).astype(jnp.bfloat16)
    slot_weight = jnp.einsum("ecr,re->ec", dispatch.astype(jnp.float32), weight)
    everything = lax.all_gather(outgoing[None], ("expert", "tile"), axis=0, tiled=True)
    picked = lax.dynamic_slice_in_dim(everything, own_expert, 1, 1)[:, 0]
    picked = picked.reshape(experts, tile_count, slot_count, half_width)
    gathered = jnp.transpose(picked, (1, 2, 0, 3)).reshape(
        tile_count * slot_count, experts * half_width
    )
    gate_proj = jnp.dot(gathered, w_gate[0], preferred_element_type=jnp.float32)
    up_proj = jnp.dot(gathered, w_up[0], preferred_element_type=jnp.float32)
    hidden = (jax.nn.silu(gate_proj) * up_proj).astype(jnp.bfloat16)
    columns = w_down[0]
    summed = lax.dot_general(
        columns,
        lax.all_gather(hidden, "tile", axis=1, tiled=True),
        (((1,), (1,)), ((), ())),
        preferred_element_type=jnp.float32,
    )
    homeward = lax.all_to_all(summed, "tile", split_axis=1, concat_axis=0, tiled=True)
    returned = lax.all_to_all(homeward, "expert", split_axis=0, concat_axis=1, tiled=True)
    contribution = (slot_weight.reshape(1, experts * slot_count) * returned).astype(jnp.bfloat16)
    flat_places = placing.reshape(experts * slot_count, tok_rows)
    return jnp.einsum(
        "st,ds->td", flat_places, contribution, preferred_element_type=jnp.float32
    ).astype(jnp.bfloat16)


def solution(mesh):
    in_specs = (
        P(("group", "tile"), "expert"),
        P(("group", "tile"), None),
        P(("group", "tile"), None),
        P("expert", None, "tile"),
        P("expert", None, "tile"),
        P("expert", "tile", None),
    )
    out_specs = P(("group", "tile"), "expert")
    local = local_direct if mesh.shape["tile"] == 8 else local_gathered
    return jax.shard_map(local, mesh=mesh, in_specs=in_specs, out_specs=out_specs, check_vma=False)
```

```python
import functools

import jax
import jax.numpy as jnp
from jax import lax
from jax.experimental import pallas as pl
from jax.experimental.pallas import tpu as pltpu
from jax.sharding import PartitionSpec as P

MIB = 1 << 20
SLOTS = 2
VMEM = pl.BlockSpec(memory_space=pltpu.VMEM)
ANY = pl.BlockSpec(memory_space=pl.ANY)


def in_vmem(x):
    return pltpu.with_memory_space_constraint(x, pltpu.VMEM)


def in_hbm(x):
    return pltpu.with_memory_space_constraint(x, pltpu.HBM)


def call(kernel, name, out, in_specs, limit, seconds=0.0, scratch=()):
    return pl.pallas_call(
        kernel,
        out_shape=out,
        in_specs=in_specs,
        out_specs=jax.tree.map(lambda _: VMEM, out),
        scratch_shapes=scratch,
        compiler_params=pltpu.CompilerParams(vmem_limit_bytes=limit),
        cost_estimate=pl.CostEstimate(flops=int(seconds*1e15), bytes_accessed=0, transcendentals=0),
        name=name,
    )


def slot_rows(routes_ref, e, rows):
    taken = jnp.int32(0)
    found = []
    for r in range(rows):
        named = jnp.logical_or(routes_ref[0, r] == e, routes_ref[1, r] == e)
        found.append((named, taken))
        taken = taken + named.astype(jnp.int32)
    return found


def dispatch_kernel(tokens_hbm, routes_hbm, gates_hbm, sends_ref, table_ref, tokens_ref, routes_ref, gates_ref, sems):
    copies = [
        pltpu.make_async_copy(routes_hbm, routes_ref, sems.at[0]),
        pltpu.make_async_copy(gates_hbm, gates_ref, sems.at[1]),
        pltpu.make_async_copy(tokens_hbm, tokens_ref, sems.at[2]),
    ]
    for copy in copies:
        copy.start()
    for copy in copies:
        copy.wait()
    tokens = tokens_ref[...].astype(jnp.float32)
    rows = tokens.shape[0]
    tiles = sends_ref.shape[0] // 2
    for e in range(2):
        found = slot_rows(routes_ref, e, rows)
        base = e * (1 + SLOTS)
        line = (1, table_ref.shape[2])
        for r in range(rows):
            weight = jnp.where(routes_ref[0, r] == e, gates_ref[0, r], 0.0)
            weight = weight + jnp.where(routes_ref[1, r] == e, gates_ref[1, r], 0.0)
            table_ref[base, r:r + 1, :] = jnp.full(line, weight, jnp.float32)
        slots = []
        for c in range(SLOTS):
            row = jnp.zeros((1, tokens.shape[1]), jnp.float32)
            for r, (named, slot) in enumerate(found):
                here = jnp.logical_and(named, slot == c).astype(jnp.float32)
                row = row + here * tokens[r:r + 1, :]
                table_ref[base + 1 + c, r:r + 1, :] = jnp.full(line, here, jnp.float32)
            slots.append(row)
        block = jnp.concatenate(slots, axis=0).astype(jnp.bfloat16)
        for t in range(tiles):
            sends_ref[e * tiles + t] = block


def merge_kernel(blocks_ref, rows_ref):
    rows_ref[...] = blocks_ref[...].reshape(rows_ref.shape)


def project(rows_ref, w_ref, columns):
    slots, half = rows_ref.shape[0] // 2, rows_ref.shape[1]
    total = jnp.dot(rows_ref[:slots, :], w_ref[0, :half, columns], preferred_element_type=jnp.float32)
    return total + jnp.dot(rows_ref[slots:, :], w_ref[0, half:, columns], preferred_element_type=jnp.float32)


def over_columns(width, body):
    tile = 512

    def step(i, carry):
        body(pl.ds(pl.multiple_of(i * tile, tile), tile))
        return carry

    lax.fori_loop(0, width // tile, step, 0, unroll=4)


def gate_kernel(rows_ref, w_ref, out_ref):
    def body(columns):
        out_ref[:, columns] = project(rows_ref, w_ref, columns)

    over_columns(out_ref.shape[1], body)


def hidden_kernel(rows_ref, w_ref, gate_ref, hidden_ref):
    def body(columns):
        up = project(rows_ref, w_ref, columns)
        gate = gate_ref[:, columns]
        hidden_ref[:, columns] = (gate / (1.0 + jnp.exp(-gate)) * up).astype(jnp.bfloat16)

    over_columns(hidden_ref.shape[1], body)


def down_kernel(steps, first, last, *refs):
    n = len(steps)
    blocks, w_ref, rest = refs[:n], refs[n], refs[n + 1:]
    out_ref = rest[-1]
    me = lax.axis_index("tile")
    slots, width = blocks[0].shape
    total = None if first else rest[0][...]
    for step, block in zip(steps, blocks):
        columns = pl.ds(pl.multiple_of((me ^ step) * width, width), width)
        term = lax.dot_general(
            w_ref[0, :, columns], block[...], (((1,), (1,)), ((), ())), preferred_element_type=jnp.float32)
        total = term if total is None else total + term
    if not last:
        out_ref[...] = total
    else:
        total = total.T
        for t in range(out_ref.shape[0]):
            out_ref[t] = total[t * SLOTS:(t + 1) * SLOTS, :]


def combine_kernel(own_ref, other_ref, table_ref, out_ref):
    mine = lax.axis_index("expert")
    halves, features = own_ref.shape[0] // 2, own_ref.shape[2]
    weight = [table_ref[e * (1 + SLOTS)][:, :1] for e in range(2)]
    inside = [[table_ref[e * (1 + SLOTS) + 1 + c][:, :1] for c in range(SLOTS)] for e in range(2)]
    for i in range(halves):
        own, other = own_ref[mine * halves + i], other_ref[mine * halves + i]
        mixed = jnp.zeros((out_ref.shape[0], features), jnp.float32)
        for e in range(2):
            both = jnp.where(mine == e, own, other)
            for c in range(SLOTS):
                value = (weight[e] * both[c:c + 1]).astype(jnp.bfloat16).astype(jnp.float32)
                mixed = mixed + jnp.where(inside[e][c] != 0.0, value, 0.0)
        out_ref[:, i * features:(i + 1) * features] = mixed.astype(jnp.bfloat16)


def local_direct(tokens, routes, gates, w_gate, w_up, w_down):
    tiles = lax.axis_size("tile")
    rows, half_width = tokens.shape
    width, features = w_gate.shape[2], w_down.shape[1]
    slots = tiles * SLOTS
    routes, gates = routes.T, gates.T

    def swap(x, bit):
        return lax.ppermute(x, "tile", [(t, t ^ bit) for t in range(tiles)])

    def to_core(x):
        return lax.ppermute(x, "expert", [(0, 1), (1, 0)])

    f32 = lambda *shape: jax.ShapeDtypeStruct(shape, jnp.float32)
    bf16 = lambda *shape: jax.ShapeDtypeStruct(shape, jnp.bfloat16)
    sends, table = call(
        dispatch_kernel, "dispatch",
        (bf16(2 * tiles, SLOTS, half_width), f32(2 * (1 + SLOTS), rows, 128)), [ANY] * 3, 4 * MIB, 600e-6,
        [
            pltpu.VMEM((rows, half_width), jnp.bfloat16),
            pltpu.SMEM((2, rows), jnp.int32),
            pltpu.SMEM((2, rows), jnp.float32),
            pltpu.SemaphoreType.DMA((3,)),
        ],
    )(in_hbm(tokens), in_hbm(routes), in_hbm(gates))
    blocks = lax.all_to_all(sends, ("expert", "tile"), split_axis=0, concat_axis=0, tiled=True)
    x = call(merge_kernel, "merge", bf16(2 * slots, half_width), [VMEM], 4 * MIB, 0e-6)(blocks)
    gate = call(gate_kernel, "gate", f32(slots, width), [VMEM] * 2, 4 * MIB, 0e-6)(x, in_vmem(w_gate))
    hidden = call(hidden_kernel, "hidden", bf16(slots, width), [VMEM] * 3, 4 * MIB, 200e-6)(x, in_vmem(w_up), gate)

    def down(total, steps, block, last):
        first = total is None
        out = f32(tiles, SLOTS, features) if last else f32(features, slots)
        return call(
            functools.partial(down_kernel, steps, first, last), "down", out,
            [VMEM] * (len(steps) + 2 - first), 10 * MIB, 0e-6,
        )(*(block[k] for k in steps), in_vmem(w_down), *(() if first else (total,)))

    block = {0: hidden}
    for k in (4, 2, 1):
        block[k] = swap(hidden, k)
    block[3] = swap(block[2], 1)
    total = down(None, [0, 1], block, False)
    total, block[4] = lax.optimization_barrier((total, block[4]))
    block[6] = swap(block[4], 2)
    block[4], block[3] = lax.optimization_barrier((block[4], block[3]))
    block[5] = swap(block[4], 1)
    total = down(total, [2, 3], block, False)
    total, block[6] = lax.optimization_barrier((total, block[6]))
    block[7] = swap(block[6], 1)
    total = down(total, [4, 6], block, False)
    total = down(total, [5], block, False)
    result = down(total, [7], block, True)
    back = lax.all_to_all(result, "tile", split_axis=0, concat_axis=0, tiled=True)
    return call(combine_kernel, "combine", bf16(rows, half_width), [VMEM] * 3, 4 * MIB)(back, to_core(back), table)


def local_gathered(tokens, routes, gates, w_gate, w_up, w_down):
    experts = lax.axis_size("expert")
    tile_count = lax.axis_size("tile")
    own_expert = lax.axis_index("expert")
    half_width = tokens.shape[1]
    tok_rows = tokens.shape[0]
    slot_count = max(2, tok_rows // 2)
    window_ids = lax.broadcasted_iota(jnp.int32, (1, 1, experts), 2)
    is_named = routes[:, :, None] == window_ids
    chosen = jnp.any(is_named, axis=1)
    weight = jnp.sum(jnp.where(is_named, gates[:, :, None], jnp.float32(0.0)), axis=1)
    position = jnp.cumsum(chosen.astype(jnp.int32), axis=0) - 1
    slot_ids = lax.broadcasted_iota(jnp.int32, (1, slot_count, 1), 1)
    dispatch = jnp.logical_and(chosen.T[:, None, :], position.T[:, None, :] == slot_ids)
    placing = dispatch.astype(jnp.bfloat16)
    outgoing = jnp.einsum(
        "ecr,rd->ecd", placing, tokens, preferred_element_type=jnp.float32
    ).astype(jnp.bfloat16)
    slot_weight = jnp.einsum("ecr,re->ec", dispatch.astype(jnp.float32), weight)
    everything = lax.all_gather(outgoing[None], ("expert", "tile"), axis=0, tiled=True)
    picked = lax.dynamic_slice_in_dim(everything, own_expert, 1, 1)[:, 0]
    picked = picked.reshape(experts, tile_count, slot_count, half_width)
    gathered = jnp.transpose(picked, (1, 2, 0, 3)).reshape(
        tile_count * slot_count, experts * half_width
    )
    gate_proj = jnp.dot(gathered, w_gate[0], preferred_element_type=jnp.float32)
    up_proj = jnp.dot(gathered, w_up[0], preferred_element_type=jnp.float32)
    hidden = (jax.nn.silu(gate_proj) * up_proj).astype(jnp.bfloat16)
    columns = w_down[0]
    summed = lax.dot_general(
        columns,
        lax.all_gather(hidden, "tile", axis=1, tiled=True),
        (((1,), (1,)), ((), ())),
        preferred_element_type=jnp.float32,
    )
    homeward = lax.all_to_all(summed, "tile", split_axis=1, concat_axis=0, tiled=True)
    returned = lax.all_to_all(homeward, "expert", split_axis=0, concat_axis=1, tiled=True)
    contribution = (slot_weight.reshape(1, experts * slot_count) * returned).astype(jnp.bfloat16)
    flat_places = placing.reshape(experts * slot_count, tok_rows)
    return jnp.einsum(
        "st,ds->td", flat_places, contribution, preferred_element_type=jnp.float32
    ).astype(jnp.bfloat16)


def solution(mesh):
    in_specs = (
        P(("group", "tile"), "expert"),
        P(("group", "tile"), None),
        P(("group", "tile"), None),
        P("expert", None, "tile"),
        P("expert", None, "tile"),
        P("expert", "tile", None),
    )
    out_specs = P(("group", "tile"), "expert")
    local = local_direct if mesh.shape["tile"] == 8 else local_gathered
    return jax.shard_map(local, mesh=mesh, in_specs=in_specs, out_specs=out_specs, check_vma=False)
```

```python
import functools

import jax
import jax.numpy as jnp
from jax import lax
from jax.experimental import pallas as pl
from jax.experimental.pallas import tpu as pltpu
from jax.sharding import PartitionSpec as P

MIB = 1 << 20
SLOTS = 2
VMEM = pl.BlockSpec(memory_space=pltpu.VMEM)
ANY = pl.BlockSpec(memory_space=pl.ANY)


def in_vmem(x):
    return pltpu.with_memory_space_constraint(x, pltpu.VMEM)


def in_hbm(x):
    return pltpu.with_memory_space_constraint(x, pltpu.HBM)


def call(kernel, name, out, in_specs, limit, seconds=0.0, scratch=()):
    return pl.pallas_call(
        kernel,
        out_shape=out,
        in_specs=in_specs,
        out_specs=jax.tree.map(lambda _: VMEM, out),
        scratch_shapes=scratch,
        compiler_params=pltpu.CompilerParams(vmem_limit_bytes=limit),
        cost_estimate=pl.CostEstimate(flops=int(seconds*1e15), bytes_accessed=0, transcendentals=0),
        name=name,
    )


def slot_rows(routes_ref, e, rows):
    taken = jnp.int32(0)
    found = []
    for r in range(rows):
        named = jnp.logical_or(routes_ref[0, r] == e, routes_ref[1, r] == e)
        found.append((named, taken))
        taken = taken + named.astype(jnp.int32)
    return found


def dispatch_kernel(tokens_hbm, routes_hbm, gates_hbm, sends_ref, table_ref, tokens_ref, routes_ref, gates_ref, sems):
    copies = [
        pltpu.make_async_copy(routes_hbm, routes_ref, sems.at[0]),
        pltpu.make_async_copy(gates_hbm, gates_ref, sems.at[1]),
        pltpu.make_async_copy(tokens_hbm, tokens_ref, sems.at[2]),
    ]
    for copy in copies:
        copy.start()
    for copy in copies:
        copy.wait()
    tokens = tokens_ref[...].astype(jnp.float32)
    rows = tokens.shape[0]
    tiles = sends_ref.shape[0] // 2
    for e in range(2):
        found = slot_rows(routes_ref, e, rows)
        base = e * (1 + SLOTS)
        line = (1, table_ref.shape[2])
        for r in range(rows):
            weight = jnp.where(routes_ref[0, r] == e, gates_ref[0, r], 0.0)
            weight = weight + jnp.where(routes_ref[1, r] == e, gates_ref[1, r], 0.0)
            table_ref[base, r:r + 1, :] = jnp.full(line, weight, jnp.float32)
        slots = []
        for c in range(SLOTS):
            row = jnp.zeros((1, tokens.shape[1]), jnp.float32)
            for r, (named, slot) in enumerate(found):
                here = jnp.logical_and(named, slot == c).astype(jnp.float32)
                row = row + here * tokens[r:r + 1, :]
                table_ref[base + 1 + c, r:r + 1, :] = jnp.full(line, here, jnp.float32)
            slots.append(row)
        block = jnp.concatenate(slots, axis=0).astype(jnp.bfloat16)
        for t in range(tiles):
            sends_ref[e * tiles + t] = block


def merge_kernel(blocks_ref, rows_ref):
    rows_ref[...] = blocks_ref[...].reshape(rows_ref.shape)


def project(rows_ref, w_ref, columns):
    slots, half = rows_ref.shape[0] // 2, rows_ref.shape[1]
    total = jnp.dot(rows_ref[:slots, :], w_ref[0, :half, columns], preferred_element_type=jnp.float32)
    return total + jnp.dot(rows_ref[slots:, :], w_ref[0, half:, columns], preferred_element_type=jnp.float32)


def over_columns(width, body):
    tile = 512

    def step(i, carry):
        body(pl.ds(pl.multiple_of(i * tile, tile), tile))
        return carry

    lax.fori_loop(0, width // tile, step, 0, unroll=4)


def gate_kernel(rows_ref, w_ref, out_ref):
    def body(columns):
        out_ref[:, columns] = project(rows_ref, w_ref, columns)

    over_columns(out_ref.shape[1], body)


def hidden_kernel(rows_ref, w_ref, gate_ref, hidden_ref):
    def body(columns):
        up = project(rows_ref, w_ref, columns)
        gate = gate_ref[:, columns]
        hidden_ref[:, columns] = (gate / (1.0 + jnp.exp(-gate)) * up).astype(jnp.bfloat16)

    over_columns(hidden_ref.shape[1], body)


def down_kernel(steps, first, last, *refs):
    n = len(steps)
    blocks, w_ref, rest = refs[:n], refs[n], refs[n + 1:]
    out_ref = rest[-1]
    me = lax.axis_index("tile")
    slots, width = blocks[0].shape
    total = None if first else rest[0][...]
    for step, block in zip(steps, blocks):
        columns = pl.ds(pl.multiple_of((me ^ step) * width, width), width)
        term = lax.dot_general(
            w_ref[0, :, columns], block[...], (((1,), (1,)), ((), ())), preferred_element_type=jnp.float32)
        total = term if total is None else total + term
    if not last:
        out_ref[...] = total
    else:
        total = total.T
        for t in range(out_ref.shape[0]):
            out_ref[t] = total[t * SLOTS:(t + 1) * SLOTS, :]


def combine_kernel(own_ref, other_ref, table_ref, out_ref):
    mine = lax.axis_index("expert")
    halves, features = own_ref.shape[0] // 2, own_ref.shape[2]
    weight = [table_ref[e * (1 + SLOTS)][:, :1] for e in range(2)]
    inside = [[table_ref[e * (1 + SLOTS) + 1 + c][:, :1] for c in range(SLOTS)] for e in range(2)]
    for i in range(halves):
        own, other = own_ref[mine * halves + i], other_ref[mine * halves + i]
        mixed = jnp.zeros((out_ref.shape[0], features), jnp.float32)
        for e in range(2):
            both = jnp.where(mine == e, own, other)
            for c in range(SLOTS):
                value = (weight[e] * both[c:c + 1]).astype(jnp.bfloat16).astype(jnp.float32)
                mixed = mixed + jnp.where(inside[e][c] != 0.0, value, 0.0)
        out_ref[:, i * features:(i + 1) * features] = mixed.astype(jnp.bfloat16)


def local_direct(tokens, routes, gates, w_gate, w_up, w_down):
    tiles = lax.axis_size("tile")
    rows, half_width = tokens.shape
    width, features = w_gate.shape[2], w_down.shape[1]
    slots = tiles * SLOTS
    routes, gates = routes.T, gates.T

    def swap(x, bit):
        return lax.ppermute(x, "tile", [(t, t ^ bit) for t in range(tiles)])

    def to_core(x):
        return lax.ppermute(x, "expert", [(0, 1), (1, 0)])

    f32 = lambda *shape: jax.ShapeDtypeStruct(shape, jnp.float32)
    bf16 = lambda *shape: jax.ShapeDtypeStruct(shape, jnp.bfloat16)
    sends, table = call(
        dispatch_kernel, "dispatch",
        (bf16(2 * tiles, SLOTS, half_width), f32(2 * (1 + SLOTS), rows, 128)), [ANY] * 3, 4 * MIB, 600e-6,
        [
            pltpu.VMEM((rows, half_width), jnp.bfloat16),
            pltpu.SMEM((2, rows), jnp.int32),
            pltpu.SMEM((2, rows), jnp.float32),
            pltpu.SemaphoreType.DMA((3,)),
        ],
    )(in_hbm(tokens), in_hbm(routes), in_hbm(gates))
    blocks = lax.all_to_all(sends, ("expert", "tile"), split_axis=0, concat_axis=0, tiled=True)
    x = call(merge_kernel, "merge", bf16(2 * slots, half_width), [VMEM], 4 * MIB, 0e-6)(blocks)
    gate = call(gate_kernel, "gate", f32(slots, width), [VMEM] * 2, 4 * MIB, 0e-6)(x, in_vmem(w_gate))
    hidden = call(hidden_kernel, "hidden", bf16(slots, width), [VMEM] * 3, 4 * MIB, 200e-6)(x, in_vmem(w_up), gate)

    def down(total, steps, block, last):
        first = total is None
        out = f32(tiles, SLOTS, features) if last else f32(features, slots)
        return call(
            functools.partial(down_kernel, steps, first, last), "down", out,
            [VMEM] * (len(steps) + 2 - first), 10 * MIB, 0e-6,
        )(*(block[k] for k in steps), in_vmem(w_down), *(() if first else (total,)))

    block = {0: hidden}
    for k in (2, 1, 4, 6):
        block[k] = swap(hidden, k)
    block[3] = swap(block[2], 1)
    total = down(None, [0, 1], block, False)
    total, block[4] = lax.optimization_barrier((total, block[4]))
    block[5] = swap(block[4], 1)
    total = down(total, [2, 4], block, False)
    total, block[6], block[3] = lax.optimization_barrier((total, block[6], block[3]))
    block[7] = swap(block[6], 1)
    total = down(total, [3, 6], block, False)
    total = down(total, [5], block, False)
    result = down(total, [7], block, True)
    back = lax.all_to_all(result, "tile", split_axis=0, concat_axis=0, tiled=True)
    return call(combine_kernel, "combine", bf16(rows, half_width), [VMEM] * 3, 4 * MIB)(back, to_core(back), table)


def local_gathered(tokens, routes, gates, w_gate, w_up, w_down):
    experts = lax.axis_size("expert")
    tile_count = lax.axis_size("tile")
    own_expert = lax.axis_index("expert")
    half_width = tokens.shape[1]
    tok_rows = tokens.shape[0]
    slot_count = max(2, tok_rows // 2)
    window_ids = lax.broadcasted_iota(jnp.int32, (1, 1, experts), 2)
    is_named = routes[:, :, None] == window_ids
    chosen = jnp.any(is_named, axis=1)
    weight = jnp.sum(jnp.where(is_named, gates[:, :, None], jnp.float32(0.0)), axis=1)
    position = jnp.cumsum(chosen.astype(jnp.int32), axis=0) - 1
    slot_ids = lax.broadcasted_iota(jnp.int32, (1, slot_count, 1), 1)
    dispatch = jnp.logical_and(chosen.T[:, None, :], position.T[:, None, :] == slot_ids)
    placing = dispatch.astype(jnp.bfloat16)
    outgoing = jnp.einsum(
        "ecr,rd->ecd", placing, tokens, preferred_element_type=jnp.float32
    ).astype(jnp.bfloat16)
    slot_weight = jnp.einsum("ecr,re->ec", dispatch.astype(jnp.float32), weight)
    everything = lax.all_gather(outgoing[None], ("expert", "tile"), axis=0, tiled=True)
    picked = lax.dynamic_slice_in_dim(everything, own_expert, 1, 1)[:, 0]
    picked = picked.reshape(experts, tile_count, slot_count, half_width)
    gathered = jnp.transpose(picked, (1, 2, 0, 3)).reshape(
        tile_count * slot_count, experts * half_width
    )
    gate_proj = jnp.dot(gathered, w_gate[0], preferred_element_type=jnp.float32)
    up_proj = jnp.dot(gathered, w_up[0], preferred_element_type=jnp.float32)
    hidden = (jax.nn.silu(gate_proj) * up_proj).astype(jnp.bfloat16)
    columns = w_down[0]
    summed = lax.dot_general(
        columns,
        lax.all_gather(hidden, "tile", axis=1, tiled=True),
        (((1,), (1,)), ((), ())),
        preferred_element_type=jnp.float32,
    )
    homeward = lax.all_to_all(summed, "tile", split_axis=1, concat_axis=0, tiled=True)
    returned = lax.all_to_all(homeward, "expert", split_axis=0, concat_axis=1, tiled=True)
    contribution = (slot_weight.reshape(1, experts * slot_count) * returned).astype(jnp.bfloat16)
    flat_places = placing.reshape(experts * slot_count, tok_rows)
    return jnp.einsum(
        "st,ds->td", flat_places, contribution, preferred_element_type=jnp.float32
    ).astype(jnp.bfloat16)


def solution(mesh):
    in_specs = (
        P(("group", "tile"), "expert"),
        P(("group", "tile"), None),
        P(("group", "tile"), None),
        P("expert", None, "tile"),
        P("expert", None, "tile"),
        P("expert", "tile", None),
    )
    out_specs = P(("group", "tile"), "expert")
    local = local_direct if mesh.shape["tile"] == 8 else local_gathered
    return jax.shard_map(local, mesh=mesh, in_specs=in_specs, out_specs=out_specs, check_vma=False)
```

```python
import functools

import jax
import jax.numpy as jnp
from jax import lax
from jax.experimental import pallas as pl
from jax.experimental.pallas import tpu as pltpu
from jax.sharding import PartitionSpec as P

MIB = 1 << 20
SLOTS = 2
VMEM = pl.BlockSpec(memory_space=pltpu.VMEM)
ANY = pl.BlockSpec(memory_space=pl.ANY)


def in_vmem(x):
    return pltpu.with_memory_space_constraint(x, pltpu.VMEM)


def in_hbm(x):
    return pltpu.with_memory_space_constraint(x, pltpu.HBM)


def call(kernel, name, out, in_specs, limit, seconds=0.0, scratch=()):
    return pl.pallas_call(
        kernel,
        out_shape=out,
        in_specs=in_specs,
        out_specs=jax.tree.map(lambda _: VMEM, out),
        scratch_shapes=scratch,
        compiler_params=pltpu.CompilerParams(vmem_limit_bytes=limit),
        cost_estimate=pl.CostEstimate(flops=int(seconds*1e15), bytes_accessed=0, transcendentals=0),
        name=name,
    )


def slot_rows(routes_ref, e, rows):
    taken = jnp.int32(0)
    found = []
    for r in range(rows):
        named = jnp.logical_or(routes_ref[0, r] == e, routes_ref[1, r] == e)
        found.append((named, taken))
        taken = taken + named.astype(jnp.int32)
    return found


def dispatch_kernel(tokens_hbm, routes_hbm, gates_hbm, sends_ref, table_ref, tokens_ref, routes_ref, gates_ref, sems):
    copies = [
        pltpu.make_async_copy(routes_hbm, routes_ref, sems.at[0]),
        pltpu.make_async_copy(gates_hbm, gates_ref, sems.at[1]),
        pltpu.make_async_copy(tokens_hbm, tokens_ref, sems.at[2]),
    ]
    for copy in copies:
        copy.start()
    for copy in copies:
        copy.wait()
    tokens = tokens_ref[...].astype(jnp.float32)
    rows = tokens.shape[0]
    tiles = sends_ref.shape[0] // 2
    for e in range(2):
        found = slot_rows(routes_ref, e, rows)
        base = e * (1 + SLOTS)
        line = (1, table_ref.shape[2])
        for r in range(rows):
            weight = jnp.where(routes_ref[0, r] == e, gates_ref[0, r], 0.0)
            weight = weight + jnp.where(routes_ref[1, r] == e, gates_ref[1, r], 0.0)
            table_ref[base, r:r + 1, :] = jnp.full(line, weight, jnp.float32)
        slots = []
        for c in range(SLOTS):
            row = jnp.zeros((1, tokens.shape[1]), jnp.float32)
            for r, (named, slot) in enumerate(found):
                here = jnp.logical_and(named, slot == c).astype(jnp.float32)
                row = row + here * tokens[r:r + 1, :]
                table_ref[base + 1 + c, r:r + 1, :] = jnp.full(line, here, jnp.float32)
            slots.append(row)
        block = jnp.concatenate(slots, axis=0).astype(jnp.bfloat16)
        for t in range(tiles):
            sends_ref[e * tiles + t] = block


def merge_kernel(blocks_ref, rows_ref):
    rows_ref[...] = blocks_ref[...].reshape(rows_ref.shape)


def project(rows_ref, w_ref, columns):
    slots, half = rows_ref.shape[0] // 2, rows_ref.shape[1]
    total = jnp.dot(rows_ref[:slots, :], w_ref[0, :half, columns], preferred_element_type=jnp.float32)
    return total + jnp.dot(rows_ref[slots:, :], w_ref[0, half:, columns], preferred_element_type=jnp.float32)


def over_columns(width, body):
    tile = 512

    def step(i, carry):
        body(pl.ds(pl.multiple_of(i * tile, tile), tile))
        return carry

    lax.fori_loop(0, width // tile, step, 0, unroll=4)


def gate_kernel(rows_ref, w_ref, out_ref):
    def body(columns):
        out_ref[:, columns] = project(rows_ref, w_ref, columns)

    over_columns(out_ref.shape[1], body)


def hidden_kernel(rows_ref, w_ref, gate_ref, hidden_ref):
    def body(columns):
        up = project(rows_ref, w_ref, columns)
        gate = gate_ref[:, columns]
        hidden_ref[:, columns] = (gate / (1.0 + jnp.exp(-gate)) * up).astype(jnp.bfloat16)

    over_columns(hidden_ref.shape[1], body)


def down_kernel(steps, first, last, *refs):
    n = len(steps)
    blocks, w_ref, rest = refs[:n], refs[n], refs[n + 1:]
    out_ref = rest[-1]
    me = lax.axis_index("tile")
    slots, width = blocks[0].shape
    total = None if first else rest[0][...]
    for step, block in zip(steps, blocks):
        columns = pl.ds(pl.multiple_of((me ^ step) * width, width), width)
        term = lax.dot_general(
            w_ref[0, :, columns], block[...], (((1,), (1,)), ((), ())), preferred_element_type=jnp.float32)
        total = term if total is None else total + term
    if not last:
        out_ref[...] = total
    else:
        total = total.T
        tiles = out_ref.shape[0] // 2
        for t in range(tiles):
            for e in range(2):
                out_ref[e * tiles + t] = total[t * SLOTS:(t + 1) * SLOTS, :]


def combine_kernel(back_ref, table_ref, out_ref):
    mine = lax.axis_index("expert")
    tiles, features = back_ref.shape[0] // 2, back_ref.shape[2]
    halves = tiles // 2
    weight = [table_ref[e * (1 + SLOTS)][:, :1] for e in range(2)]
    inside = [[table_ref[e * (1 + SLOTS) + 1 + c][:, :1] for c in range(SLOTS)] for e in range(2)]
    for i in range(halves):
        mixed = jnp.zeros((out_ref.shape[0], features), jnp.float32)
        for e in range(2):
            both = back_ref[e * tiles + mine * halves + i]
            for c in range(SLOTS):
                value = (weight[e] * both[c:c + 1]).astype(jnp.bfloat16).astype(jnp.float32)
                mixed = mixed + jnp.where(inside[e][c] != 0.0, value, 0.0)
        out_ref[:, i * features:(i + 1) * features] = mixed.astype(jnp.bfloat16)


def local_direct(tokens, routes, gates, w_gate, w_up, w_down):
    tiles = lax.axis_size("tile")
    rows, half_width = tokens.shape
    width, features = w_gate.shape[2], w_down.shape[1]
    slots = tiles * SLOTS
    routes, gates = routes.T, gates.T

    def swap(x, bit):
        return lax.ppermute(x, "tile", [(t, t ^ bit) for t in range(tiles)])

    f32 = lambda *shape: jax.ShapeDtypeStruct(shape, jnp.float32)
    bf16 = lambda *shape: jax.ShapeDtypeStruct(shape, jnp.bfloat16)
    sends, table = call(
        dispatch_kernel, "dispatch",
        (bf16(2 * tiles, SLOTS, half_width), f32(2 * (1 + SLOTS), rows, 128)), [ANY] * 3, 4 * MIB, 600e-6,
        [
            pltpu.VMEM((rows, half_width), jnp.bfloat16),
            pltpu.SMEM((2, rows), jnp.int32),
            pltpu.SMEM((2, rows), jnp.float32),
            pltpu.SemaphoreType.DMA((3,)),
        ],
    )(in_hbm(tokens), in_hbm(routes), in_hbm(gates))
    blocks = lax.all_to_all(sends, ("expert", "tile"), split_axis=0, concat_axis=0, tiled=True)
    x = call(merge_kernel, "merge", bf16(2 * slots, half_width), [VMEM], 4 * MIB, 0e-6)(blocks)
    gate = call(gate_kernel, "gate", f32(slots, width), [VMEM] * 2, 4 * MIB, 0e-6)(x, in_vmem(w_gate))
    hidden = call(hidden_kernel, "hidden", bf16(slots, width), [VMEM] * 3, 4 * MIB, 200e-6)(x, in_vmem(w_up), gate)

    def down(total, steps, block, last):
        first = total is None
        out = f32(2 * tiles, SLOTS, features) if last else f32(features, slots)
        return call(
            functools.partial(down_kernel, steps, first, last), "down", out,
            [VMEM] * (len(steps) + 2 - first), 10 * MIB, 0e-6,
        )(*(block[k] for k in steps), in_vmem(w_down), *(() if first else (total,)))

    block = {0: hidden}
    for k in (4, 2, 1):
        block[k] = swap(hidden, k)
    block[3] = swap(block[2], 1)
    total = down(None, [0, 1], block, False)
    total, block[4] = lax.optimization_barrier((total, block[4]))
    block[6] = swap(block[4], 2)
    block[4], block[3] = lax.optimization_barrier((block[4], block[3]))
    block[5] = swap(block[4], 1)
    total = down(total, [2, 3], block, False)
    total, block[6] = lax.optimization_barrier((total, block[6]))
    block[7] = swap(block[6], 1)
    total = down(total, [4, 6], block, False)
    total = down(total, [5], block, False)
    result = down(total, [7], block, True)
    back = lax.all_to_all(result, ("expert", "tile"), split_axis=0, concat_axis=0, tiled=True)
    return call(combine_kernel, "combine", bf16(rows, half_width), [VMEM] * 2, 4 * MIB)(back, table)


def local_gathered(tokens, routes, gates, w_gate, w_up, w_down):
    experts = lax.axis_size("expert")
    tile_count = lax.axis_size("tile")
    own_expert = lax.axis_index("expert")
    half_width = tokens.shape[1]
    tok_rows = tokens.shape[0]
    slot_count = max(2, tok_rows // 2)
    window_ids = lax.broadcasted_iota(jnp.int32, (1, 1, experts), 2)
    is_named = routes[:, :, None] == window_ids
    chosen = jnp.any(is_named, axis=1)
    weight = jnp.sum(jnp.where(is_named, gates[:, :, None], jnp.float32(0.0)), axis=1)
    position = jnp.cumsum(chosen.astype(jnp.int32), axis=0) - 1
    slot_ids = lax.broadcasted_iota(jnp.int32, (1, slot_count, 1), 1)
    dispatch = jnp.logical_and(chosen.T[:, None, :], position.T[:, None, :] == slot_ids)
    placing = dispatch.astype(jnp.bfloat16)
    outgoing = jnp.einsum(
        "ecr,rd->ecd", placing, tokens, preferred_element_type=jnp.float32
    ).astype(jnp.bfloat16)
    slot_weight = jnp.einsum("ecr,re->ec", dispatch.astype(jnp.float32), weight)
    everything = lax.all_gather(outgoing[None], ("expert", "tile"), axis=0, tiled=True)
    picked = lax.dynamic_slice_in_dim(everything, own_expert, 1, 1)[:, 0]
    picked = picked.reshape(experts, tile_count, slot_count, half_width)
    gathered = jnp.transpose(picked, (1, 2, 0, 3)).reshape(
        tile_count * slot_count, experts * half_width
    )
    gate_proj = jnp.dot(gathered, w_gate[0], preferred_element_type=jnp.float32)
    up_proj = jnp.dot(gathered, w_up[0], preferred_element_type=jnp.float32)
    hidden = (jax.nn.silu(gate_proj) * up_proj).astype(jnp.bfloat16)
    columns = w_down[0]
    summed = lax.dot_general(
        columns,
        lax.all_gather(hidden, "tile", axis=1, tiled=True),
        (((1,), (1,)), ((), ())),
        preferred_element_type=jnp.float32,
    )
    homeward = lax.all_to_all(summed, "tile", split_axis=1, concat_axis=0, tiled=True)
    returned = lax.all_to_all(homeward, "expert", split_axis=0, concat_axis=1, tiled=True)
    contribution = (slot_weight.reshape(1, experts * slot_count) * returned).astype(jnp.bfloat16)
    flat_places = placing.reshape(experts * slot_count, tok_rows)
    return jnp.einsum(
        "st,ds->td", flat_places, contribution, preferred_element_type=jnp.float32
    ).astype(jnp.bfloat16)


def solution(mesh):
    in_specs = (
        P(("group", "tile"), "expert"),
        P(("group", "tile"), None),
        P(("group", "tile"), None),
        P("expert", None, "tile"),
        P("expert", None, "tile"),
        P("expert", "tile", None),
    )
    out_specs = P(("group", "tile"), "expert")
    local = local_direct if mesh.shape["tile"] == 8 else local_gathered
    return jax.shard_map(local, mesh=mesh, in_specs=in_specs, out_specs=out_specs, check_vma=False)
```

```python
import functools

import jax
import jax.numpy as jnp
from jax import lax
from jax.experimental import pallas as pl
from jax.experimental.pallas import tpu as pltpu
from jax.sharding import PartitionSpec as P

MIB = 1 << 20
SLOTS = 2
VMEM = pl.BlockSpec(memory_space=pltpu.VMEM)
ANY = pl.BlockSpec(memory_space=pl.ANY)


def in_vmem(x):
    return pltpu.with_memory_space_constraint(x, pltpu.VMEM)


def in_hbm(x):
    return pltpu.with_memory_space_constraint(x, pltpu.HBM)


def call(kernel, name, out, in_specs, limit, seconds=0.0, scratch=()):
    return pl.pallas_call(
        kernel,
        out_shape=out,
        in_specs=in_specs,
        out_specs=jax.tree.map(lambda _: VMEM, out),
        scratch_shapes=scratch,
        compiler_params=pltpu.CompilerParams(vmem_limit_bytes=limit),
        cost_estimate=pl.CostEstimate(flops=int(seconds*1e15), bytes_accessed=0, transcendentals=0),
        name=name,
    )


def slot_rows(routes_ref, e, rows):
    taken = jnp.int32(0)
    found = []
    for r in range(rows):
        named = jnp.logical_or(routes_ref[0, r] == e, routes_ref[1, r] == e)
        found.append((named, taken))
        taken = taken + named.astype(jnp.int32)
    return found


def dispatch_kernel(tokens_hbm, routes_hbm, gates_hbm, sends_ref, table_ref, tokens_ref, routes_ref, gates_ref, sems):
    copies = [
        pltpu.make_async_copy(routes_hbm, routes_ref, sems.at[0]),
        pltpu.make_async_copy(gates_hbm, gates_ref, sems.at[1]),
        pltpu.make_async_copy(tokens_hbm, tokens_ref, sems.at[2]),
    ]
    for copy in copies:
        copy.start()
    for copy in copies:
        copy.wait()
    tokens = tokens_ref[...].astype(jnp.float32)
    rows = tokens.shape[0]
    tiles = sends_ref.shape[0] // 2
    for e in range(2):
        found = slot_rows(routes_ref, e, rows)
        base = e * (1 + SLOTS)
        line = (1, table_ref.shape[2])
        for r in range(rows):
            weight = jnp.where(routes_ref[0, r] == e, gates_ref[0, r], 0.0)
            weight = weight + jnp.where(routes_ref[1, r] == e, gates_ref[1, r], 0.0)
            table_ref[base, r:r + 1, :] = jnp.full(line, weight, jnp.float32)
        slots = []
        for c in range(SLOTS):
            row = jnp.zeros((1, tokens.shape[1]), jnp.float32)
            for r, (named, slot) in enumerate(found):
                here = jnp.logical_and(named, slot == c).astype(jnp.float32)
                row = row + here * tokens[r:r + 1, :]
                table_ref[base + 1 + c, r:r + 1, :] = jnp.full(line, here, jnp.float32)
            slots.append(row)
        block = jnp.concatenate(slots, axis=0).astype(jnp.bfloat16)
        for t in range(tiles):
            sends_ref[e * tiles + t] = block


def merge_kernel(blocks_ref, rows_ref):
    rows_ref[...] = blocks_ref[...].reshape(rows_ref.shape)


def project(rows_ref, w_ref, columns):
    slots, half = rows_ref.shape[0] // 2, rows_ref.shape[1]
    total = jnp.dot(rows_ref[:slots, :], w_ref[0, :half, columns], preferred_element_type=jnp.float32)
    return total + jnp.dot(rows_ref[slots:, :], w_ref[0, half:, columns], preferred_element_type=jnp.float32)


def over_columns(width, body):
    tile = 512

    def step(i, carry):
        body(pl.ds(pl.multiple_of(i * tile, tile), tile))
        return carry

    lax.fori_loop(0, width // tile, step, 0, unroll=4)


def gate_kernel(rows_ref, w_ref, out_ref):
    def body(columns):
        out_ref[:, columns] = project(rows_ref, w_ref, columns)

    over_columns(out_ref.shape[1], body)


def hidden_kernel(rows_ref, w_ref, gate_ref, hidden_ref):
    def body(columns):
        up = project(rows_ref, w_ref, columns)
        gate = gate_ref[:, columns]
        hidden_ref[:, columns] = (gate / (1.0 + jnp.exp(-gate)) * up).astype(jnp.bfloat16)

    over_columns(hidden_ref.shape[1], body)


def down_kernel(steps, first, last, *refs):
    n = len(steps)
    blocks, w_ref, rest = refs[:n], refs[n], refs[n + 1:]
    out_ref = rest[-1]
    me = lax.axis_index("tile")
    slots, width = blocks[0].shape
    total = None if first else rest[0][...]
    for step, block in zip(steps, blocks):
        columns = pl.ds(pl.multiple_of((me ^ step) * width, width), width)
        term = lax.dot_general(
            w_ref[0, :, columns], block[...], (((1,), (1,)), ((), ())), preferred_element_type=jnp.float32)
        total = term if total is None else total + term
    if not last:
        out_ref[...] = total
    else:
        total = total.T
        tiles = out_ref.shape[0] // 2
        for t in range(tiles):
            for e in range(2):
                out_ref[e * tiles + t] = total[t * SLOTS:(t + 1) * SLOTS, :]


def combine_kernel(back_ref, table_ref, out_ref):
    mine = lax.axis_index("expert")
    tiles, features = back_ref.shape[0] // 2, back_ref.shape[2]
    halves = tiles // 2
    weight = [table_ref[e * (1 + SLOTS)][:, :1] for e in range(2)]
    inside = [[table_ref[e * (1 + SLOTS) + 1 + c][:, :1] for c in range(SLOTS)] for e in range(2)]
    for i in range(halves):
        mixed = jnp.zeros((out_ref.shape[0], features), jnp.float32)
        for e in range(2):
            both = back_ref[e * tiles + mine * halves + i]
            for c in range(SLOTS):
                value = (weight[e] * both[c:c + 1]).astype(jnp.bfloat16).astype(jnp.float32)
                mixed = mixed + jnp.where(inside[e][c] != 0.0, value, 0.0)
        out_ref[:, i * features:(i + 1) * features] = mixed.astype(jnp.bfloat16)


def local_direct(tokens, routes, gates, w_gate, w_up, w_down):
    tiles = lax.axis_size("tile")
    rows, half_width = tokens.shape
    width, features = w_gate.shape[2], w_down.shape[1]
    slots = tiles * SLOTS
    routes, gates = routes.T, gates.T

    def swap(x, bit):
        return lax.ppermute(x, "tile", [(t, t ^ bit) for t in range(tiles)])

    f32 = lambda *shape: jax.ShapeDtypeStruct(shape, jnp.float32)
    bf16 = lambda *shape: jax.ShapeDtypeStruct(shape, jnp.bfloat16)
    sends, table = call(
        dispatch_kernel, "dispatch",
        (bf16(2 * tiles, SLOTS, half_width), f32(2 * (1 + SLOTS), rows, 128)), [ANY] * 3, 4 * MIB, 600e-6,
        [
            pltpu.VMEM((rows, half_width), jnp.bfloat16),
            pltpu.SMEM((2, rows), jnp.int32),
            pltpu.SMEM((2, rows), jnp.float32),
            pltpu.SemaphoreType.DMA((3,)),
        ],
    )(in_hbm(tokens), in_hbm(routes), in_hbm(gates))
    blocks = lax.all_to_all(sends, ("expert", "tile"), split_axis=0, concat_axis=0, tiled=True)
    x = call(merge_kernel, "merge", bf16(2 * slots, half_width), [VMEM], 4 * MIB, 0e-6)(blocks)
    gate = call(gate_kernel, "gate", f32(slots, width), [VMEM] * 2, 4 * MIB, 0e-6)(x, in_vmem(w_gate))
    hidden = call(hidden_kernel, "hidden", bf16(slots, width), [VMEM] * 3, 4 * MIB, 200e-6)(x, in_vmem(w_up), gate)

    def down(total, steps, block, last):
        first = total is None
        out = f32(2 * tiles, SLOTS, features) if last else f32(features, slots)
        return call(
            functools.partial(down_kernel, steps, first, last), "down", out,
            [VMEM] * (len(steps) + 2 - first), 10 * MIB, 0e-6,
        )(*(block[k] for k in steps), in_vmem(w_down), *(() if first else (total,)))

    block = {0: hidden}
    for k in (2, 1, 4, 6):
        block[k] = swap(hidden, k)
    block[3] = swap(block[2], 1)
    total = down(None, [0, 1], block, False)
    total, block[4] = lax.optimization_barrier((total, block[4]))
    block[5] = swap(block[4], 1)
    total = down(total, [2, 4], block, False)
    total, block[6], block[3] = lax.optimization_barrier((total, block[6], block[3]))
    block[7] = swap(block[6], 1)
    total = down(total, [3, 6], block, False)
    total = down(total, [5], block, False)
    result = down(total, [7], block, True)
    back = lax.all_to_all(result, ("expert", "tile"), split_axis=0, concat_axis=0, tiled=True)
    return call(combine_kernel, "combine", bf16(rows, half_width), [VMEM] * 2, 4 * MIB)(back, table)


def local_gathered(tokens, routes, gates, w_gate, w_up, w_down):
    experts = lax.axis_size("expert")
    tile_count = lax.axis_size("tile")
    own_expert = lax.axis_index("expert")
    half_width = tokens.shape[1]
    tok_rows = tokens.shape[0]
    slot_count = max(2, tok_rows // 2)
    window_ids = lax.broadcasted_iota(jnp.int32, (1, 1, experts), 2)
    is_named = routes[:, :, None] == window_ids
    chosen = jnp.any(is_named, axis=1)
    weight = jnp.sum(jnp.where(is_named, gates[:, :, None], jnp.float32(0.0)), axis=1)
    position = jnp.cumsum(chosen.astype(jnp.int32), axis=0) - 1
    slot_ids = lax.broadcasted_iota(jnp.int32, (1, slot_count, 1), 1)
    dispatch = jnp.logical_and(chosen.T[:, None, :], position.T[:, None, :] == slot_ids)
    placing = dispatch.astype(jnp.bfloat16)
    outgoing = jnp.einsum(
        "ecr,rd->ecd", placing, tokens, preferred_element_type=jnp.float32
    ).astype(jnp.bfloat16)
    slot_weight = jnp.einsum("ecr,re->ec", dispatch.astype(jnp.float32), weight)
    everything = lax.all_gather(outgoing[None], ("expert", "tile"), axis=0, tiled=True)
    picked = lax.dynamic_slice_in_dim(everything, own_expert, 1, 1)[:, 0]
    picked = picked.reshape(experts, tile_count, slot_count, half_width)
    gathered = jnp.transpose(picked, (1, 2, 0, 3)).reshape(
        tile_count * slot_count, experts * half_width
    )
    gate_proj = jnp.dot(gathered, w_gate[0], preferred_element_type=jnp.float32)
    up_proj = jnp.dot(gathered, w_up[0], preferred_element_type=jnp.float32)
    hidden = (jax.nn.silu(gate_proj) * up_proj).astype(jnp.bfloat16)
    columns = w_down[0]
    summed = lax.dot_general(
        columns,
        lax.all_gather(hidden, "tile", axis=1, tiled=True),
        (((1,), (1,)), ((), ())),
        preferred_element_type=jnp.float32,
    )
    homeward = lax.all_to_all(summed, "tile", split_axis=1, concat_axis=0, tiled=True)
    returned = lax.all_to_all(homeward, "expert", split_axis=0, concat_axis=1, tiled=True)
    contribution = (slot_weight.reshape(1, experts * slot_count) * returned).astype(jnp.bfloat16)
    flat_places = placing.reshape(experts * slot_count, tok_rows)
    return jnp.einsum(
        "st,ds->td", flat_places, contribution, preferred_element_type=jnp.float32
    ).astype(jnp.bfloat16)


def solution(mesh):
    in_specs = (
        P(("group", "tile"), "expert"),
        P(("group", "tile"), None),
        P(("group", "tile"), None),
        P("expert", None, "tile"),
        P("expert", None, "tile"),
        P("expert", "tile", None),
    )
    out_specs = P(("group", "tile"), "expert")
    local = local_direct if mesh.shape["tile"] == 8 else local_gathered
    return jax.shard_map(local, mesh=mesh, in_specs=in_specs, out_specs=out_specs, check_vma=False)
```
